32 devices in a mesh: parts: 2 (over y), slab: 4 (over z), cross: 2 (over x), sub: 2 (over core).
Axes of the slice: x: 2, y: 2, z: 4, core: 2. Of those that a mesh axis runs over, the one named last changes fastest.
Arguments:
- populations: float32 [19, 96, 24, 256], P(None, ('parts', 'slab'), 'cross', 'sub'), parts along dimension 1, may hold values from 0 to 1
- membrane: float32 [512, 3, 642], P(('parts', 'slab', 'cross', 'sub')), parts along dimension 0, may hold values from -4 to 4
- anchors: int32 [512, 3], P(('parts', 'slab', 'cross', 'sub')), parts along dimension 0, may hold values from 0 to 255, as said below
- targets: int32 [512], P(('parts', 'slab', 'cross', 'sub')), parts along dimension 0, may hold values from 0 to 255, as said below
Outputs:
- new_populations: float32 [19, 96, 24, 256], P(None, ('parts', 'slab'), 'cross', 'sub'), parts along dimension 1
- vertex_velocity: float32 [512, 3, 642], P(('parts', 'slab', 'cross', 'sub')), parts along dimension 0
The draws below stay inside these ranges and needn't reach their ends.
There are 2 independent parts, one for each index of `parts`. The reference program is written for one: setup_inputs(seed, part) draws one part's arguments, and reference() takes and returns one part's arrays. A program takes and returns all parts, laid end to end along the dimension named above; each array names one. Nothing has to cross between parts.
Inputs may be any that keep to these rules, and one draw needn't show every extreme that they name: `targets`: slot numbers are owner * 16 + slot, owners counted slab-major over slab, cross, sub. The map is a bijection of the 256 slots. A cell keeps its owner or moves to the device one step up or one step down along slab (wrapping) with the same cross and sub indices; one device hands at most 4 cells to each of these two neighbours, and in every draw some device hands exactly 4 to its upper neighbour. `anchors`: the anchor lies inside the lattice block of the device that owns the cell's slot after migration.
All inputs are finite; a program needn't handle non-finite values.
Results may differ from the reference program's by a relative error of at most 0.0003.
Values sent between devices are 32-bit elements; how exact they have to be, the bound alone decides.
No kernel may reach another device: no remote copies, remote signals or barrier semaphores. Data moves between devices by JAX's collectives and lax.ppermute only.
A program may use at most 128 MiB of HBM per device.

```python
import math
import jax
import jax.numpy as jnp
import numpy as np
from jax import lax

V = 642
GHOST = 6
MIG = 4
LX = 12
LY = 12
LZ = 128
CELLS_DEV = 16
NX = 48
NY = 24
NZ = 256
CELLS = 256


lattice_dirs = np.array([[0, 0, 0], [1, 0, 0], [-1, 0, 0], [0, 1, 0], [0, -1, 0], [0, 0, 1], [0, 0, -1], [1, 1, 0], [-1, -1, 0], [1, -1, 0], [-1, 1, 0], [1, 0, 1], [-1, 0, -1], [1, 0, -1], [-1, 0, 1], [0, 1, 1], [0, -1, -1], [0, 1, -1], [0, -1, 1]], dtype=np.int32)


lattice_weights = [1.0 / 3.0] + [1.0 / 18.0] * 6 + [1.0 / 36.0] * 12


rest_radius = 3.0


def rest_shape_drawn(length, dtype):
    position = jnp.arange(length, dtype=jnp.int32)
    height = 1.0 - (2.0 * position.astype(dtype) + 1.0) / length
    across = jnp.sqrt(1.0 - height * height)
    azimuth = (position * 1597 % 2584).astype(dtype) * (2.0 * math.pi / 2584.0)
    return rest_radius * jnp.stack([across * jnp.cos(azimuth), across * jnp.sin(azimuth), height])


def swap_map(key):
    slab_count = NX // LX
    cross_count = NY // LY
    sub_count = NZ // LZ
    plane_count = cross_count * sub_count
    devices = slab_count * plane_count
    orders = jax.vmap(lambda device_key: jax.random.permutation(device_key, CELLS_DEV))(jax.random.split(jax.random.fold_in(key, 101), devices))
    counts = jax.random.randint(jax.random.fold_in(key, 102), (devices,), 0, MIG + 1)
    forced = jax.random.randint(jax.random.fold_in(key, 103), (), 0, devices)
    device = jnp.arange(devices, dtype=jnp.int32)
    counts = jnp.where(device == forced, MIG, counts)
    upper = (device // plane_count + 1) % slab_count * plane_count + device % plane_count
    lower_slots = (device[:, None] * CELLS_DEV + orders[:, :MIG]).reshape(-1)
    upper_slots = (upper[:, None] * CELLS_DEV + orders[upper, MIG:2 * MIG]).reshape(-1)
    active = (jnp.arange(MIG, dtype=jnp.int32)[None, :] < counts[:, None]).reshape(-1)
    moved = jnp.arange(devices * CELLS_DEV, dtype=jnp.int32)
    moved = moved.at[lower_slots].set(jnp.where(active, upper_slots, lower_slots))
    moved = moved.at[upper_slots].set(jnp.where(active, lower_slots, upper_slots))
    return moved.astype(jnp.int32)


def draw_targets(key, part):
    return swap_map(key)


def draw_anchors(key, part):
    moved = swap_map(key)
    key = jax.random.fold_in(key, 7)
    cross_count = NY // LY
    sub_count = NZ // LZ
    plane_count = cross_count * sub_count
    slot_number = jnp.arange(CELLS, dtype=jnp.int32)
    device = slot_number // CELLS_DEV
    split_keys = jax.random.split(key, 3)
    final = jnp.stack([device // plane_count * LX + jax.random.randint(split_keys[0], (CELLS,), 0, LX), device // sub_count % cross_count * LY + jax.random.randint(split_keys[1], (CELLS,), 0, LY), device % sub_count * LZ + jax.random.randint(split_keys[2], (CELLS,), 0, LZ)], axis=1)
    final = final.at[CELLS - 1].set(jnp.array([NX - 1, NY - 1, NZ - 1], jnp.int32))
    final = final.at[0].set(jnp.zeros((3,), jnp.int32))
    return final[moved].astype(jnp.int32)


def draw_membrane(key, part):
    key = jax.random.fold_in(key, 11)
    first_key, second_key, third_key, fourth_key = jax.random.split(key, 4)
    resting = rest_shape_drawn(V, jnp.float32)
    heading = 2.0 * jax.random.randint(fourth_key, (CELLS, 3, 1), 0, 2).astype(jnp.float32) - 1.0
    stretch = jax.random.uniform(first_key, (CELLS, 3, 1), jnp.float32, 0.88, 1.05)
    jitter = 0.12 * jax.random.uniform(second_key, (CELLS, 3, V), jnp.float32, -1.0, 1.0)
    offset = heading * jax.random.uniform(third_key, (CELLS, 3, 1), jnp.float32, 0.5, 0.7)
    return stretch * resting[None] + jitter + offset


def draw_populations(key, part):
    key = jax.random.fold_in(key, 23)
    split_keys = jax.random.split(key, 3)
    grid = (NX, NY, NZ)
    density = 1.0 + 0.05 * jax.random.uniform(split_keys[0], grid, jnp.float32, -1.0, 1.0)
    velocity = 0.04 * jnp.clip(jax.random.normal(split_keys[1], (3,) + grid, jnp.float32), -2.5, 2.5)
    heading = jnp.asarray(lattice_dirs, jnp.float32)
    weights = jnp.asarray(lattice_weights, jnp.float32)[:, None, None, None]
    aligned = heading[:, 0, None, None, None] * velocity[0] + heading[:, 1, None, None, None] * velocity[1] + heading[:, 2, None, None, None] * velocity[2]
    kinetic = velocity[0] * velocity[0] + velocity[1] * velocity[1] + velocity[2] * velocity[2]
    equilibrium = weights * density * (1.0 + 3.0 * aligned + 4.5 * aligned * aligned - 1.5 * kinetic)
    noise = 1.0 + 0.03 * jax.random.uniform(split_keys[2], (19,) + grid, jnp.float32, -1.0, 1.0)
    return equilibrium * noise


def setup_inputs(seed: int = 0, part: int = 0) -> dict:
    key_of = jax.random.split(jax.random.key(seed), 5)
    part_keys = jax.random.split(jax.random.fold_in(key_of[4], part), 5)
    return {
        "populations": draw_populations(jax.random.fold_in(jax.random.fold_in(key_of[4], part), 71), part),
        "membrane": draw_membrane(jax.random.fold_in(jax.random.fold_in(key_of[4], part), 71), part),
        "anchors": draw_anchors(jax.random.fold_in(jax.random.fold_in(key_of[4], part), 71), part),
        "targets": draw_targets(jax.random.fold_in(jax.random.fold_in(key_of[4], part), 71), part),
    }


lattice_dirs = np.array([[0, 0, 0], [1, 0, 0], [-1, 0, 0], [0, 1, 0], [0, -1, 0], [0, 0, 1], [0, 0, -1], [1, 1, 0], [-1, -1, 0], [1, -1, 0], [-1, 1, 0], [1, 0, 1], [-1, 0, -1], [1, 0, -1], [-1, 0, 1], [0, 1, 1], [0, -1, -1], [0, 1, -1], [0, -1, 1]], dtype=np.int32)
lattice_weights = [1.0 / 3.0] + [1.0 / 18.0] * 6 + [1.0 / 36.0] * 12
relax_time = 0.8
spring_stiff = 0.05
bend_stiff = 0.002
rest_radius = 3.0
link_strides = (21, 34, 55)
highest = lax.Precision.HIGHEST

def rest_shape(length, dtype):
    position = jnp.arange(length, dtype=jnp.int32)
    height = 1.0 - (2.0 * position.astype(dtype) + 1.0) / length
    across = jnp.sqrt(1.0 - height * height)
    azimuth = (position * 1597 % 2584).astype(dtype) * (2.0 * math.pi / 2584.0)
    return rest_radius * jnp.stack([across * jnp.cos(azimuth), across * jnp.sin(azimuth), height])

def along_chain(values, stride):
    padding = jnp.zeros(values.shape[:-1] + (abs(stride),), values.dtype)
    if stride > 0:
        return jnp.concatenate([values[..., stride:], padding], axis=-1)
    return jnp.concatenate([padding, values[..., :stride]], axis=-1)

def laplace(values, unities):
    total = jnp.zeros_like(values)
    for stride in link_strides:
        for signed in (stride, -stride):
            total = total + along_chain(unities, signed) * (along_chain(values, signed) - values)
    return total

def membrane_force(membrane):
    resting = rest_shape(membrane.shape[-1], membrane.dtype)
    unities = jnp.ones((membrane.shape[-1],), membrane.dtype)
    stretch = jnp.zeros_like(membrane)
    for stride in link_strides:
        for signed in (stride, -stride):
            linked = along_chain(unities, signed)
            difference = along_chain(membrane, signed) - membrane
            rest_gap = along_chain(resting, signed) - resting
            rest_square = lax.optimization_barrier(jnp.sum(rest_gap * rest_gap, axis=0))
            now_square = lax.optimization_barrier(jnp.sum(difference * difference, axis=1, keepdims=True))
            stretch = stretch + linked * (now_square - rest_square) / rest_square * difference
    bending = laplace(laplace(membrane - resting, unities), unities)
    return spring_stiff * stretch - bend_stiff * bending

def kernel_rows(membrane, reach):
    node_offsets = jnp.arange(2 * reach, dtype=jnp.int32).astype(membrane.dtype) - reach
    offsets = node_offsets[None, None, :, None] - membrane[:, :, None, :]
    return jnp.where(jnp.abs(offsets) < 2.0, 0.25 * (1.0 + jnp.cos(0.5 * math.pi * offsets)), 0.0)

def planar(weights):
    return (weights[:, 1, :, None, :] * weights[:, 2, None, :, :]).reshape(weights.shape[0], -1, weights.shape[-1])

def spread_group(forcing, weights):
    lifted = (forcing[:, :, None, :] * weights[:, 0, None, :, :]).reshape(forcing.shape[0], -1, forcing.shape[-1])
    return jnp.einsum('bjv,bmv->bjm', lifted, planar(weights), precision=highest)

def sample_group(patches, weights):
    mixed = jnp.einsum('bjm,bmv->bjv', patches, planar(weights), precision=highest)
    mixed = mixed.reshape(weights.shape[0], 3, weights.shape[2], weights.shape[3])
    return lax.optimization_barrier(jnp.sum(mixed * weights[:, 0, None, :, :], axis=2))

def drift(pops, forcing):
    heading = jnp.asarray(lattice_dirs.T, pops.dtype)
    density = lax.optimization_barrier(jnp.sum(pops, axis=0))
    momentum = jnp.einsum('ai,ixyz->axyz', heading, pops, precision=highest)
    return (density, (momentum + 0.5 * forcing) / density)

def collide(pops, forcing):
    density, velocity = drift(pops, forcing)
    heading = jnp.asarray(lattice_dirs, pops.dtype)
    weights = jnp.asarray(lattice_weights, pops.dtype)[:, None, None, None]
    aligned = jnp.einsum('ia,axyz->ixyz', heading, velocity, precision=highest)
    pushed = jnp.einsum('ia,axyz->ixyz', heading, forcing, precision=highest)
    kinetic = lax.optimization_barrier(jnp.sum(velocity * velocity, axis=0))
    power_in = lax.optimization_barrier(jnp.sum(velocity * forcing, axis=0))
    equilibrium = weights * density * (1.0 + 3.0 * aligned + 4.5 * aligned * aligned - 1.5 * kinetic)
    source = weights * (3.0 * (pushed - power_in) + 9.0 * aligned * pushed)
    return pops - (pops - equilibrium) / relax_time + (1.0 - 0.5 / relax_time) * source

def fold_cycle(padded, axis, reach):
    length = padded.shape[axis] - 2 * reach
    interior = lax.slice_in_dim(padded, reach, reach + length, axis=axis)
    lower_rim = lax.slice_in_dim(padded, 0, reach, axis=axis)
    upper_rim = lax.slice_in_dim(padded, reach + length, length + 2 * reach, axis=axis)
    middle_shape = list(interior.shape)
    middle_shape[axis] = length - 2 * reach
    return interior + jnp.concatenate([upper_rim, jnp.zeros(middle_shape, padded.dtype), lower_rim], axis=axis)

def reference(populations, membrane, anchors, targets):
    reach = GHOST
    cells = membrane.shape[0]
    vertices = membrane.shape[2]
    moved = jnp.zeros_like(membrane).at[targets].set(membrane)
    placed = jnp.zeros_like(anchors).at[targets].set(anchors)
    group_size = math.gcd(cells, 64)
    groups = cells // group_size

    def spread_one(inputs):
        block_shape = inputs
        return spread_group(membrane_force(block_shape), kernel_rows(block_shape, reach))
    patches = lax.map(spread_one, moved.reshape(groups, group_size, 3, vertices))
    patches = patches.reshape(cells, 3, 2 * reach, 2 * reach, 2 * reach)
    extent = populations.shape[1:]
    padded = jnp.zeros((3,) + tuple((side + 2 * reach for side in extent)), populations.dtype)

    def place(position, total):
        corner = placed[position]
        root = (jnp.int32(0), corner[0], corner[1], corner[2])
        current = lax.dynamic_slice(total, root, (3, 2 * reach, 2 * reach, 2 * reach))
        return lax.dynamic_update_slice(total, current + patches[position], root)
    padded = lax.fori_loop(0, cells, place, padded)
    body_force = padded
    for axis in (1, 2, 3):
        body_force = fold_cycle(body_force, axis, reach)
    post = collide(populations, body_force)
    pieces = []
    for position in range(19):
        heading = tuple((int(value) for value in lattice_dirs[position]))
        pieces.append(jnp.roll(post[position], heading, axis=(0, 1, 2)))
    renewed = jnp.stack(pieces)
    _, velocity = drift(renewed, body_force)
    flow = jnp.pad(velocity, ((0, 0), (reach, reach), (reach, reach), (reach, reach)), mode='wrap')

    def sample_one(inputs):
        corners, block_shape = inputs
        gathered = jax.vmap(lambda corner: lax.dynamic_slice(flow, (jnp.int32(0), corner[0], corner[1], corner[2]), (3, 2 * reach, 2 * reach, 2 * reach)))(corners)
        return sample_group(gathered.reshape(corners.shape[0], 6 * reach, 4 * reach * reach), kernel_rows(block_shape, reach))
    vertex_velocity = lax.map(sample_one, (placed.reshape(groups, group_size, 3), moved.reshape(groups, group_size, 3, vertices)))
    return (renewed, vertex_velocity.reshape(cells, 3, vertices))
```

```python
import functools
import math

import jax
import jax.numpy as jnp
import numpy as np
from jax import lax
from jax.experimental import pallas as pl
from jax.experimental.pallas import tpu as pltpu
from jax.sharding import PartitionSpec as P

REACH = 6
MIG = 4
STRIDES = (21, 34, 55)
DIRS = (
    (0, 0, 0),
    (1, 0, 0), (-1, 0, 0), (0, 1, 0), (0, -1, 0), (0, 0, 1), (0, 0, -1),
    (1, 1, 0), (-1, -1, 0), (1, -1, 0), (-1, 1, 0),
    (1, 0, 1), (-1, 0, -1), (1, 0, -1), (-1, 0, 1),
    (0, 1, 1), (0, -1, -1), (0, 1, -1), (0, -1, 1),
)
RISING = (5, 11, 14, 15, 18)
FALLING = (6, 12, 13, 16, 17)
WEIGHTS = (1.0 / 3.0,) + (1.0 / 18.0,) * 6 + (1.0 / 36.0,) * 12
FAR = 100.0
F32 = jnp.float32
VMEM = pl.BlockSpec(memory_space=pltpu.VMEM)
SMEM = pl.BlockSpec(memory_space=pltpu.SMEM)


def params(limit=40):
    return pltpu.CompilerParams(vmem_limit_bytes=limit * 1024 * 1024)


def chain_table(vertices, width):
    v = np.arange(vertices)
    h = 1.0 - (2.0 * v + 1.0) / vertices
    t = 2.0 * math.pi / 2584.0 * (v * 1597 % 2584)
    across = np.sqrt(1.0 - h * h)
    rest = 3.0 * np.stack([across * np.cos(t), across * np.sin(t), h])
    table = np.zeros((16, width))
    for n, s in enumerate(STRIDES):
        gap = rest[:, s:] - rest[:, :-s]
        table[5 * n : 5 * n + 3, : vertices - s] = gap
        table[5 * n + 3, : vertices - s] = 0.05 / np.sum(gap * gap, axis=0)
        table[5 * n + 4, : vertices - s] = 1.0
    return jnp.asarray(table, F32)


def pack_kernel(capacity, slabs, plane, here, targets, anchors, membrane, up, down, up_info, down_info):
    for r in range(MIG):
        up_info[r, 0] = -1
        down_info[r, 0] = -1

    def step(c, counts):
        target = targets[c]
        owner = target // capacity
        peer = owner // plane
        slot = target - owner * capacity
        slab = here[0]
        leaving = owner != here[3]
        rises = jnp.logical_and(leaving, peer == lax.rem(slab + 1, slabs))
        falls = jnp.logical_and(leaving, peer == lax.rem(slab + slabs - 1, slabs))

        @pl.when(rises)
        def _():
            n = counts[0]
            up[n] = membrane[c]
            up_info[n, 0] = slot
            for d in range(3):
                up_info[n, 1 + d] = anchors[c, d]

        @pl.when(falls)
        def _():
            n = counts[1]
            down[n] = membrane[c]
            down_info[n, 0] = slot
            for d in range(3):
                down_info[n, 1 + d] = anchors[c, d]

        return (
            jnp.minimum(counts[0] + rises.astype(jnp.int32), MIG - 1 + 1),
            jnp.minimum(counts[1] + falls.astype(jnp.int32), MIG - 1 + 1),
        )

    lax.fori_loop(0, capacity, step, (jnp.int32(0), jnp.int32(0)))


def assemble_kernel(
    capacity, vertices, extent, here, targets, anchors, below_info, above_info, membrane, below, above, pos, corner
):
    pos[...] = jnp.full(pos.shape, FAR, F32)
    roots = [here[d] * extent[d] for d in range(3)]

    def put(slot, source, n, known):
        for a in range(3):
            pos[a, pl.ds(slot, 1), 0:vertices] = source(a)
        for d in range(3):
            corner[slot, d] = known(d) - roots[d]

    def step(c, carry):
        target = targets[c]
        owner = target // capacity
        slot = target - owner * capacity

        @pl.when(owner == here[3])
        def _():
            put(slot, lambda a: membrane[a, pl.ds(c, 1), :], c, lambda d: anchors[c, d])

        return carry

    lax.fori_loop(0, capacity, step, jnp.int32(0))
    for cells, info in ((below, below_info), (above, above_info)):
        for r in range(MIG):
            slot = info[r, 0]

            @pl.when(slot >= 0)
            def _():
                put(slot, lambda a: cells[r, a : a + 1, :], r, lambda d: info[r, 1 + d])


def wide(tile, width):
    return jnp.concatenate([tile] * (width // 128), axis=1)


def waves(x):
    h = (x - 4.0 * jnp.floor(0.25 * x + 0.5)) * (math.pi / 4.0)
    q = h * h
    sine = h * (1.0 + q * (-1 / 6 + q * (1 / 120 + q * (-1 / 5040 + q * (1 / 362880 - q * (1 / 39916800))))))
    cosine = 1.0 + q * (
        -1 / 2 + q * (1 / 24 + q * (-1 / 720 + q * (1 / 40320 + q * (-1 / 3628800 + q * (1 / 479001600)))))
    )
    return 0.25 - 0.5 * sine * sine, 0.5 * sine * cosine


def fill_waves(pos, wave):
    for a in range(3):
        wave[2 * a], wave[2 * a + 1] = waves(pos[a])


def fill_force(pos, table, force):
    cells, width = pos.shape[1:]
    for h in range(cells // 8):
        rows = slice(8 * h, 8 * h + 8)
        x = [pos[a, rows, :] for a in range(3)]
        lap = [jnp.zeros((8, width), F32) for _ in range(3)]
        pulls = []
        for n, s in enumerate(STRIDES):
            gap = [table[5 * n + a : 5 * n + a + 1, :] for a in range(3)]
            scale = table[5 * n + 3 : 5 * n + 4, :]
            mask = table[5 * n + 4 : 5 * n + 5, :]
            d = [pltpu.roll(x[a], width - s, 1) - x[a] for a in range(3)]
            square = d[0] * d[0] + d[1] * d[1] + d[2] * d[2]
            strain = square * scale - 0.05 * mask
            pulls.append([strain * d[a] for a in range(3)])
            for a in range(3):
                bend = mask * d[a] - gap[a]
                lap[a] = lap[a] + bend - pltpu.roll(bend, s, 1)
        for a in range(3):
            total = jnp.zeros((8, width), F32)
            for n, s in enumerate(STRIDES):
                mask = table[5 * n + 4 : 5 * n + 5, :]
                t = pulls[n][a] - 0.002 * (mask * (pltpu.roll(lap[a], width - s, 1) - lap[a]))
                total = total + t - pltpu.roll(t, s, 1)
            force[a, rows, :] = total


def split(x):
    high = x.astype(jnp.bfloat16)
    return high, (x - high.astype(F32)).astype(jnp.bfloat16)


def row_of(ref, i, c):
    return jnp.broadcast_to(ref[i, pl.ds(c, 1), :], (8, ref.shape[2]))


def fill_planar(pos, wave, c, high, low):
    width = pos.shape[2]
    row = lax.broadcasted_iota(jnp.int32, (8, 128), 0)
    rowf = wide((row - REACH).astype(F32), width)
    odd = wide((row & 1), width) == 1
    flip = wide((row & 2), width) == 0
    z, cz, sz = row_of(pos, 2, c), row_of(wave, 4, c), row_of(wave, 5, c)
    base = jnp.where(odd, sz, cz)
    pattern = 0.25 + jnp.where(flip, -base, base)
    wz = jnp.concatenate(
        [
            jnp.where(jnp.abs(rowf - z) < 2.0, pattern, 0.0),
            jnp.where(jnp.abs(rowf + 8.0 - z) < 2.0, pattern, 0.0),
        ],
        axis=0,
    )
    x, cx, sx = row_of(pos, 0, c), row_of(wave, 0, c), row_of(wave, 1, c)
    quarter = (0.25 - cx, 0.25 - sx, 0.25 + cx, 0.25 + sx)
    for kx in range(2 * REACH):
        wx = jnp.where(jnp.abs(x - float(kx - REACH)) < 2.0, quarter[kx % 4], 0.0)
        high[16 * kx : 16 * kx + 16, :], low[16 * kx : 16 * kx + 16, :] = split(
            jnp.concatenate([wx, wx], axis=0) * wz
        )


def rows_weight(pos, wave, c, anchor, images):
    width = pos.shape[2]
    n = lax.broadcasted_iota(jnp.int32, (8, 128), 0) - 1 - anchor
    nf = wide(n.astype(F32), width)
    odd = wide(n & 1, width) == 1
    flip = wide(n & 2, width) == 2
    y, cy, sy = row_of(pos, 1, c), row_of(wave, 2, c), row_of(wave, 3, c)
    base = jnp.where(odd, sy, cy)
    pattern = 0.25 + jnp.where(flip, -base, base)
    halves = []
    for h in range(2):
        gap = nf + 8.0 * h - y
        near = jnp.abs(gap - float(images[0])) < 2.0
        for image in images[1:]:
            near = jnp.logical_or(near, jnp.abs(gap - float(image)) < 2.0)
        halves.append(jnp.where(near, pattern, 0.0))
    return jnp.concatenate(halves, axis=0)


def nt_dot(a, b):
    return lax.dot_general(a, b, (((1,), (1,)), ((), ())), preferred_element_type=F32)


def spread_kernel(images, first, corner, pos, table, *refs):
    if first:
        acc, far, wave, force, high, low, patch = refs
        acc[...] = jnp.zeros(acc.shape, F32)
        far[...] = jnp.zeros(far.shape, F32)
    else:
        acc_in, far_in, acc, far, wave, force, high, low, patch = refs
        acc[...] = acc_in[...]
        far[...] = far_in[...]
    cells = pos.shape[1]
    fill_waves(pos, wave)
    fill_force(pos, table, force)

    def weigh(c, b):
        fill_planar(pos, wave, c, high.at[b], low.at[b])
        wy = rows_weight(pos, wave, c, corner[c, 1], images)
        lifted = []
        for a in range(3):
            f = row_of(force, a, c)
            lifted.append(jnp.concatenate([f, f], axis=0) * wy)
        lhigh, llow = split(jnp.concatenate(lifted, axis=0))
        both = nt_dot(jnp.concatenate([lhigh, llow], axis=0), high[b])
        total = both[:48] + both[48:] + nt_dot(lhigh, low[b])
        patch[c, :, 0:192] = total

    def weigh_two(i, carry):
        weigh(2 * i, 0)
        weigh(2 * i + 1, 1)
        return carry

    lax.fori_loop(0, cells // 2, weigh_two, 0)
    lane = lax.broadcasted_iota(jnp.int32, (48, 128), 1)

    def rolled(c, kx, z0):
        t = kx // 8
        return pltpu.roll(
            patch[c, :, 128 * t : 128 * t + 128], (z0 + 256 - 16 * (kx % 8)) & 127, 1
        )

    def place(c, carry):
        z0 = corner[c, 2] - REACH
        x0 = corner[c, 0]
        inside = jnp.logical_and(lane >= z0, lane < z0 + 16)
        for kx in range(2 * REACH):
            acc[x0 + kx] += jnp.where(inside, rolled(c, kx, z0), 0.0)
        return carry

    lax.fori_loop(0, cells, place, 0)

    def place_far(c, carry):
        z0 = corner[c, 2] - REACH
        x0 = corner[c, 0]

        @pl.when(jnp.logical_or(z0 < 0, z0 + 12 > 128))
        def _():
            outside = jnp.logical_or(lane >= z0 + 128, lane < z0 - 112)
            for kx in range(2 * REACH):
                far[x0 + kx] += jnp.where(outside, rolled(c, kx, z0), 0.0)

        return carry

    lax.fori_loop(0, cells, place_far, 0)


def spread(images, corner, pos, table, sums=None):
    cells, width = pos.shape[1:]
    shape = jax.ShapeDtypeStruct((24, 48, 128), F32)
    first = sums is None
    return pl.pallas_call(
        functools.partial(spread_kernel, images, first),
        out_shape=(shape, shape),
        in_specs=[SMEM, VMEM, VMEM] + ([] if first else [VMEM, VMEM]),
        out_specs=(VMEM, VMEM),
        scratch_shapes=[
            pltpu.VMEM((6, cells, width), F32),
            pltpu.VMEM((3, cells, width), F32),
            pltpu.VMEM((2, 192, width), jnp.bfloat16),
            pltpu.VMEM((2, 192, width), jnp.bfloat16),
            pltpu.VMEM((cells, 48, 256), F32),
        ],
        compiler_params=params(),
        name="spread",
        cost_estimate=pl.CostEstimate(flops=int(2e9), bytes_accessed=4_000_000, transcendentals=0),
    )(corner, pos, table, *(() if first else sums))


def sample_kernel(images, corner, pos, low_side, own, high_side, low_far, own_far, high_far, out, flow, far, wave, high, low):
    cells, width = pos.shape[1:]
    at = 0
    for part, part_far in ((low_side, low_far), (own, own_far), (high_side, high_far)):
        size = part.shape[0]
        flow[at : at + size] = part[...]
        far[at : at + size] = part_far[...]
        at += size
    fill_waves(pos, wave)
    lane = lax.broadcasted_iota(jnp.int32, (48, 128), 1)
    group = lane // 16

    def sample(c, b):
        fill_planar(pos, wave, c, high.at[b], low.at[b])
        z0 = corner[c, 2] - REACH
        x0 = corner[c, 0]
        outside = jnp.logical_or(lane >= z0 + 128, lane < z0 - 112)
        tiles = [jnp.zeros((48, 128), F32), jnp.zeros((48, 128), F32)]
        for kx in range(2 * REACH):
            g = kx % 8
            source = jnp.where(outside, far[x0 + kx], flow[x0 + kx])
            turned = pltpu.roll(source, (16 * g + 256 - z0) & 127, 1)
            tiles[kx // 8] = jnp.where(group == g, turned, tiles[kx // 8])
        whole = jnp.concatenate([tiles[0], tiles[1][:, 0:64]], axis=1)
        qhigh, qlow = split(whole)
        both = jnp.dot(jnp.concatenate([qhigh, qlow], axis=0), high[b], preferred_element_type=F32)
        mixed = both[:48] + both[48:] + jnp.dot(qhigh, low[b], preferred_element_type=F32)
        wy = rows_weight(pos, wave, c, corner[c, 1], images)
        for a in range(3):
            out[a, pl.ds(c, 1), :] = jnp.sum(mixed[16 * a : 16 * a + 16] * wy, axis=0, keepdims=True)

    def sample_two(i, carry):
        sample(2 * i, 0)
        sample(2 * i + 1, 1)
        return carry

    lax.fori_loop(0, cells // 2, sample_two, 0)


def sampled(images, corner, pos, parts):
    cells, width = pos.shape[1:]
    return pl.pallas_call(
        functools.partial(sample_kernel, images),
        out_shape=jax.ShapeDtypeStruct((3, cells, width), F32),
        in_specs=[SMEM] + [VMEM] * 7,
        out_specs=VMEM,
        scratch_shapes=[
            pltpu.VMEM((24, 48, 128), F32),
            pltpu.VMEM((24, 48, 128), F32),
            pltpu.VMEM((6, cells, width), F32),
            pltpu.VMEM((2, 192, width), jnp.bfloat16),
            pltpu.VMEM((2, 192, width), jnp.bfloat16),
        ],
        compiler_params=params(),
        name="sample",
        cost_estimate=pl.CostEstimate(flops=int(2e9), bytes_accessed=4_000_000, transcendentals=0),
    )(corner, pos, *parts)


def extend_kernel(pops, x_low, x_high, y_low, y_high, out):
    nx, ny = pops.shape[:2]
    directions = pops.shape[2]
    for x in range(nx + 2):
        middle = x_low[0] if x == 0 else (x_high[0] if x == nx + 1 else pops[x - 1])
        block = jnp.concatenate([y_low[x : x + 1], middle, y_high[x : x + 1], y_low[x : x + 1], y_low[x : x + 1]], axis=0)
        out[:, x] = jnp.transpose(block, (1, 0, 2))


def collide_kernel(pops, own, from_low, from_high, post, force, edge):
    planes = pops.shape[1]
    n_low, n_high = from_low.shape[0], from_high.shape[0]
    for e in range(planes):
        total = own[e]
        if e < n_low:
            total = total + from_low[e]
        if e >= planes - n_high:
            total = total + from_high[e - (planes - n_high)]
        force[e] = total
    lane = lax.broadcasted_iota(jnp.int32, (16, 128), 1)

    def plane(e, carry):
        p = [pops[i, e] for i in range(19)]
        f = [force[e, 16 * a : 16 * a + 16, :] for a in range(3)]
        rho = p[0]
        for i in range(1, 19):
            rho = rho + p[i]
        u = []
        for a in range(3):
            m = 0.5 * f[a]
            for i in range(1, 19):
                if DIRS[i][a] == 1:
                    m = m + p[i]
                elif DIRS[i][a] == -1:
                    m = m - p[i]
            u.append(m / rho)
        kinetic = u[0] * u[0] + u[1] * u[1] + u[2] * u[2]
        power = u[0] * f[0] + u[1] * f[1] + u[2] * f[2]
        level = 1.25 * rho * (1.0 - 1.5 * kinetic) - 1.125 * power
        bow, tilt = 5.625 * rho, 3.75 * rho
        new = [None] * 19
        new[0] = WEIGHTS[0] * level - 0.25 * p[0]
        for i in range(1, 19, 2):
            along = [a for a in range(3) if DIRS[i][a] != 0]
            cu, cf = None, None
            for a in along:
                tu, tf = u[a], f[a]
                if DIRS[i][a] < 0:
                    tu, tf = -tu, -tf
                cu = tu if cu is None else cu + tu
                cf = tf if cf is None else cf + tf
            even = WEIGHTS[i] * (level + cu * (bow * cu + 3.375 * cf))
            odd = WEIGHTS[i] * (tilt * cu + 1.125 * cf)
            new[i] = even + odd - 0.25 * p[i]
            new[i + 1] = even - odd - 0.25 * p[i + 1]
        for i in range(19):
            post[i, e] = new[i]
        for j in range(5):
            edge[j, e] = jnp.where(
                lane == 0, pltpu.roll(new[RISING[j]], 1, 1), pltpu.roll(new[FALLING[j]], 127, 1)
            )
        return carry

    lax.fori_loop(0, planes, plane, 0)


def stream_kernel(post, edge, force, pops, velocity):
    ny = pops.shape[1]
    lane = lax.broadcasted_iota(jnp.int32, (ny, 128), 1)
    velocity[...] = jnp.zeros(velocity.shape, F32)

    def plane(x, carry):
        n = []
        for i in range(19):
            cx, cy, cz = DIRS[i]
            value = post[i, x + 1 - cx, 1 - cy : 1 - cy + ny, :]
            if cz == 1:
                side = edge[RISING.index(i), x + 1 - cx, 1 - cy : 1 - cy + ny, :]
                value = jnp.where(lane == 0, side, pltpu.roll(value, 1, 1))
            elif cz == -1:
                side = edge[FALLING.index(i), x + 1 - cx, 1 - cy : 1 - cy + ny, :]
                value = jnp.where(lane == 127, side, pltpu.roll(value, 127, 1))
            n.append(value)
        rho = n[0]
        for i in range(1, 19):
            rho = rho + n[i]
        for a in range(3):
            m = 0.5 * force[x + 1, 16 * a + 1 : 16 * a + 1 + ny, :]
            for i in range(1, 19):
                if DIRS[i][a] == 1:
                    m = m + n[i]
                elif DIRS[i][a] == -1:
                    m = m - n[i]
            velocity[x, 16 * a + 1 : 16 * a + 1 + ny, :] = m / rho
        pops[x] = jnp.transpose(jnp.stack(n), (1, 0, 2))
        return carry

    lax.fori_loop(0, pops.shape[0], plane, 0)


def shifted(x, axis, distance):
    count = lax.axis_size(axis)
    return lax.ppermute(x, axis, [(i, (i + distance) % count) for i in range(count)])


def on_device(populations, membrane, anchors, targets):
    extent = populations.shape[1:]
    capacity, _, vertices = membrane.shape
    slabs, crosses, subs = (lax.axis_size(a) for a in ("slab", "cross", "sub"))
    assert subs == 2 and extent == (12, 12, 128) and capacity % 8 == 0
    width = -(-vertices // 128) * 128
    place = [lax.axis_index(a) for a in ("slab", "cross", "sub")]
    here = jnp.stack(place + [(place[0] * crosses + place[1]) * subs + place[2]]).astype(jnp.int32)
    table = chain_table(vertices, width)

    cell = jax.ShapeDtypeStruct((MIG, 3, vertices), F32)
    info = jax.ShapeDtypeStruct((MIG, 4), jnp.int32)
    up, down, up_info, down_info = pl.pallas_call(
        functools.partial(pack_kernel, capacity, slabs, crosses * subs),
        out_shape=(cell, cell, info, info),
        in_specs=[SMEM, SMEM, SMEM, VMEM],
        out_specs=(VMEM, VMEM, SMEM, SMEM),
        compiler_params=params(),
        name="pack",
    )(here, targets, anchors, membrane)
    below, above = shifted(up, "slab", 1), shifted(down, "slab", -1)
    below_info, above_info = shifted(up_info, "slab", 1), shifted(down_info, "slab", -1)
    pos, corner = pl.pallas_call(
        functools.partial(assemble_kernel, capacity, vertices, extent),
        out_shape=(
            jax.ShapeDtypeStruct((3, capacity, width), F32),
            jax.ShapeDtypeStruct((capacity, 3), jnp.int32),
        ),
        in_specs=[SMEM] * 5 + [VMEM] * 3,
        out_specs=(VMEM, SMEM),
        compiler_params=params(),
        name="assemble",
    )(here, targets, anchors, below_info, above_info, jnp.transpose(membrane, (1, 0, 2)), below, above)

    pops = jnp.transpose(populations, (1, 2, 0, 3))
    x_low = shifted(pops[extent[0] - 1 :], "slab", 1)
    x_high = shifted(pops[:1], "slab", -1)
    first = jnp.concatenate([x_low[:, 0], pops[:, 0], x_high[:, 0]])
    last = jnp.concatenate([x_low[:, -1], pops[:, -1], x_high[:, -1]])
    if crosses == 2:
        rows = shifted(jnp.stack([last, first]), "cross", 1)
        y_low, y_high = rows[0], rows[1]
    else:
        y_low, y_high = shifted(last, "cross", 1), shifted(first, "cross", -1)
    planes = extent[0] + 2
    extended = pl.pallas_call(
        extend_kernel,
        out_shape=jax.ShapeDtypeStruct((19, planes, 16, 128), F32),
        in_specs=[VMEM] * 5,
        out_specs=VMEM,
        compiler_params=params(),
        name="extend",
    )(pops, x_low, x_high, y_low, y_high)

    if crosses == 2:
        others = [(1, (extent[1], -extent[1]))]
    else:
        others = [(1, (-extent[1],)), (-1, (extent[1],))]
    visitors = [(shifted(corner, "cross", d), shifted(pos, "cross", d), images, d) for d, images in others]
    sums = spread((0,), corner, pos, table)
    for their_corner, their_pos, images, _ in visitors:
        sums = spread(images, their_corner, their_pos, table, sums)
    acc = sums[0] + shifted(sums[1], "sub", 1)
    from_high = shifted(acc[: REACH + 1], "slab", -1)
    from_low = shifted(acc[REACH + extent[0] - 1 : 2 * REACH + extent[0] - 1], "slab", 1)
    own = acc[REACH - 1 : REACH - 1 + planes]

    post, force, edge = pl.pallas_call(
        collide_kernel,
        out_shape=(
            jax.ShapeDtypeStruct((19, planes, 16, 128), F32),
            jax.ShapeDtypeStruct((planes, 48, 128), F32),
            jax.ShapeDtypeStruct((5, planes, 16, 128), F32),
        ),
        in_specs=[VMEM] * 4,
        out_specs=(VMEM,) * 3,
        compiler_params=params(),
        name="collide",
    )(extended, own, from_low, from_high)
    edge = shifted(edge, "sub", 1)
    renewed, velocity = pl.pallas_call(
        stream_kernel,
        out_shape=(
            jax.ShapeDtypeStruct((extent[0], extent[1], 19, 128), F32),
            jax.ShapeDtypeStruct((extent[0], 48, 128), F32),
        ),
        in_specs=[VMEM] * 3,
        out_specs=(VMEM,) * 2,
        compiler_params=params(),
        name="stream",
    )(post, edge, force)

    low_side = shifted(velocity[extent[0] - REACH :], "slab", 1)
    high_side = shifted(velocity[: REACH - 1], "slab", -1)
    parts = (low_side, velocity, high_side)
    parts = parts + tuple(shifted(part, "sub", 1) for part in parts)
    shares = [
        shifted(sampled(images, their_corner, their_pos, parts), "cross", -d)
        for their_corner, their_pos, images, d in visitors
    ]
    total = sampled((0,), corner, pos, parts)
    for share in shares:
        total = total + share
    return (
        jnp.transpose(renewed, (2, 0, 1, 3)),
        jnp.transpose(total[:, :, :vertices], (1, 0, 2)),
    )


def solution(mesh):
    placed = (
        P(None, ("parts", "slab"), "cross", "sub"),
        P(("parts", "slab", "cross", "sub"), None, None),
        P(("parts", "slab", "cross", "sub"), None),
        P(("parts", "slab", "cross", "sub")),
    )
    return jax.shard_map(
        on_device,
        mesh=mesh,
        in_specs=placed,
        out_specs=(
            P(None, ("parts", "slab"), "cross", "sub"),
            P(("parts", "slab", "cross", "sub"), None, None),
        ),
        check_vma=False,
    )
```

```python
import functools
import math

import jax
import jax.numpy as jnp
import numpy as np
from jax import lax
from jax.experimental import pallas as pl
from jax.experimental.pallas import tpu as pltpu
from jax.sharding import PartitionSpec as P

REACH = 6
MIG = 4
STRIDES = (21, 34, 55)
DIRS = (
    (0, 0, 0),
    (1, 0, 0), (-1, 0, 0), (0, 1, 0), (0, -1, 0), (0, 0, 1), (0, 0, -1),
    (1, 1, 0), (-1, -1, 0), (1, -1, 0), (-1, 1, 0),
    (1, 0, 1), (-1, 0, -1), (1, 0, -1), (-1, 0, 1),
    (0, 1, 1), (0, -1, -1), (0, 1, -1), (0, -1, 1),
)
RISING = (5, 11, 14, 15, 18)
FALLING = (6, 12, 13, 16, 17)
WEIGHTS = (1.0 / 3.0,) + (1.0 / 18.0,) * 6 + (1.0 / 36.0,) * 12
FAR = 100.0
F32 = jnp.float32
WIDTH = 768
VMEM = pl.BlockSpec(memory_space=pltpu.VMEM)
SMEM = pl.BlockSpec(memory_space=pltpu.SMEM)


def params(limit=14):
    return pltpu.CompilerParams(vmem_limit_bytes=limit * 1024 * 1024)


def chain_table(vertices, width):
    v = np.arange(vertices)
    h = 1.0 - (2.0 * v + 1.0) / vertices
    t = 2.0 * math.pi / 2584.0 * (v * 1597 % 2584)
    across = np.sqrt(1.0 - h * h)
    rest = 3.0 * np.stack([across * np.cos(t), across * np.sin(t), h])
    table = np.zeros((16, width))
    for n, s in enumerate(STRIDES):
        gap = rest[:, s:] - rest[:, :-s]
        table[5 * n : 5 * n + 3, : vertices - s] = gap
        table[5 * n + 3, : vertices - s] = 0.05 / np.sum(gap * gap, axis=0)
        table[5 * n + 4, : vertices - s] = 1.0
    return jnp.asarray(table, F32)


def pack_kernel(capacity, slabs, plane, groups, here, infos, *refs):
    cells, (sides, up, down) = refs[:groups], refs[groups:]
    ny, directions = sides.shape[1:3]
    tiles = WIDTH // 128
    held = 3 * tiles * MIG
    spare = up.shape[0] - 8
    up[0 : groups * held, :] = jnp.full((groups * held, 128), -1.0, F32)
    down[0 : groups * held, :] = jnp.full((groups * held, 128), -1.0, F32)
    over = lax.rem(here[0] + 1, slabs)
    under = lax.rem(here[0] + slabs - 1, slabs)
    for g in range(groups):
        n_up, n_down = jnp.int32(0), jnp.int32(0)
        for c in range(capacity):
            owner = infos[g * capacity + c, 0] // capacity
            peer = owner // plane
            leaving = owner != here[3 + g]
            rises = jnp.logical_and(leaving, peer == over)
            falls = jnp.logical_and(leaving, peer == under)
            to_up = g * held + jnp.minimum(n_up, MIG - 1)
            to_down = g * held + jnp.minimum(n_down, MIG - 1)

            def put(message, start):
                for a in range(3):
                    for t in range(tiles):
                        row = cells[g][a, c : c + 1, 128 * t : 128 * t + 128]
                        message[pl.ds(start + (a * tiles + t) * MIG, 1), :] = row

            @pl.when(rises)
            def _():
                put(up, to_up)

            @pl.when(falls)
            def _():
                put(down, to_down)

            n_up = n_up + rises.astype(jnp.int32)
            n_down = n_down + falls.astype(jnp.int32)
    for n, message in enumerate((up, down)):
        for y in range(ny):
            first = groups * held + 24 * y
            message[first : first + directions, :] = sides[n, y]


def cell_row(block, offset, r, a):
    if len(block.shape) == 3:
        return block[a, r : r + 1, :]
    tiles = WIDTH // 128
    first = offset + a * tiles * MIG + r
    return jnp.concatenate([block[first + t * MIG : first + t * MIG + 1, :] for t in range(tiles)], axis=1)


def cell_count(block):
    return block.shape[1] if len(block.shape) == 3 else MIG


def hide_rest(pos, vertices):
    width = pos.shape[2]
    lane = lax.broadcasted_iota(jnp.int32, (pos.shape[1], 128), 1) + (width - 128)
    for a in range(3):
        pos[a, :, width - 128 :] = jnp.where(lane < vertices, pos[a, :, width - 128 :], FAR)


def assemble(capacity, vertices, extent, owner, infos, sources, pos, corner):
    for first, block, offset, migrated in sources:
        for r in range(cell_count(block)):
            target = infos[first + r, 0]
            wanted = target >= 0 if migrated else target // capacity == owner
            slot = jnp.where(wanted, lax.rem(target, capacity), capacity)
            for a in range(3):
                pos[a, pl.ds(slot, 1), :] = cell_row(block, offset, r, a)
            for d in range(3):
                corner[slot, d] = lax.rem(infos[first + r, 1 + d], extent[d])
    hide_rest(pos, vertices)


def assemble_kernel(sizes, groups, offsets, *refs):
    capacity, vertices, extent = sizes
    here, infos = refs[:2]
    cells = refs[2 : 2 + 3 * groups]
    positions, corners = refs[3 + 3 * groups : 3 + 4 * groups], refs[3 + 4 * groups :]
    for g in range(groups):
        start = groups * capacity + g * 2 * MIG
        sources = [
            (g * capacity, cells[3 * g], 0, False),
            (start, cells[3 * g + 1], offsets[3 * g + 1], True),
            (start + MIG, cells[3 * g + 2], offsets[3 * g + 2], True),
        ]
        assemble(capacity, vertices, extent, here[3 + g], infos, sources, positions[g], corners[g])


def wide(tile, width):
    return jnp.concatenate([tile] * (width // 128), axis=1)


def waves(x):
    h = (x - 4.0 * jnp.floor(0.25 * x + 0.5)) * (math.pi / 4.0)
    q = h * h
    sine = h * (1.0 + q * (-1 / 6 + q * (1 / 120 + q * (-1 / 5040 + q * (1 / 362880 - q * (1 / 39916800))))))
    cosine = 1.0 + q * (
        -1 / 2 + q * (1 / 24 + q * (-1 / 720 + q * (1 / 40320 + q * (-1 / 3628800 + q * (1 / 479001600)))))
    )
    return 0.25 - 0.5 * sine * sine, 0.5 * sine * cosine


def fill_waves(pos, wave):
    cells = wave.shape[1]
    for a in range(3):
        wave[2 * a], wave[2 * a + 1] = waves(pos[a, 0:cells, :])


def fill_force(pos, table, force):
    cells, width = force.shape[1:]
    for h in range(cells // 8):
        rows = slice(8 * h, 8 * h + 8)
        x = [pos[a, rows, :] for a in range(3)]
        lap = [jnp.zeros((8, width), F32) for _ in range(3)]
        pulls = []
        for n, s in enumerate(STRIDES):
            gap = [table[5 * n + a : 5 * n + a + 1, :] for a in range(3)]
            scale = table[5 * n + 3 : 5 * n + 4, :]
            mask = table[5 * n + 4 : 5 * n + 5, :]
            d = [pltpu.roll(x[a], width - s, 1) - x[a] for a in range(3)]
            square = d[0] * d[0] + d[1] * d[1] + d[2] * d[2]
            strain = square * scale - 0.05 * mask
            pulls.append([strain * d[a] for a in range(3)])
            for a in range(3):
                bend = mask * d[a] - gap[a]
                lap[a] = lap[a] + bend - pltpu.roll(bend, s, 1)
        for a in range(3):
            total = jnp.zeros((8, width), F32)
            for n, s in enumerate(STRIDES):
                mask = table[5 * n + 4 : 5 * n + 5, :]
                t = pulls[n][a] - 0.002 * (mask * (pltpu.roll(lap[a], width - s, 1) - lap[a]))
                total = total + t - pltpu.roll(t, s, 1)
            force[a, rows, :] = total


def split(x):
    high = x.astype(jnp.bfloat16)
    return high, (x - high.astype(F32)).astype(jnp.bfloat16)


def row_of(ref, i, c):
    return jnp.broadcast_to(ref[i, pl.ds(c, 1), :], (8, ref.shape[2]))


def fill_planar(pos, wave, c, high, low):
    width = pos.shape[2]
    row = lax.broadcasted_iota(jnp.int32, (8, 128), 0)
    rowf = wide((row - REACH).astype(F32), width)
    odd = wide((row & 1), width) == 1
    flip = wide((row & 2), width) == 0
    z, cz, sz = row_of(pos, 2, c), row_of(wave, 4, c), row_of(wave, 5, c)
    base = jnp.where(odd, sz, cz)
    pattern = 0.25 + jnp.where(flip, -base, base)
    wz = jnp.concatenate(
        [
            jnp.where(jnp.abs(rowf - z) < 2.0, pattern, 0.0),
            jnp.where(jnp.abs(rowf + 8.0 - z) < 2.0, pattern, 0.0),
        ],
        axis=0,
    )
    x, cx, sx = row_of(pos, 0, c), row_of(wave, 0, c), row_of(wave, 1, c)
    quarter = (0.25 - cx, 0.25 - sx, 0.25 + cx, 0.25 + sx)
    for kx in range(2 * REACH):
        wx = jnp.where(jnp.abs(x - float(kx - REACH)) < 2.0, quarter[kx % 4], 0.0)
        high[16 * kx : 16 * kx + 16, :], low[16 * kx : 16 * kx + 16, :] = split(
            jnp.concatenate([wx, wx], axis=0) * wz
        )


def rows_weight(pos, wave, c, anchor, images):
    width = pos.shape[2]
    n = lax.broadcasted_iota(jnp.int32, (8, 128), 0) - 1 - anchor
    nf = wide(n.astype(F32), width)
    odd = wide(n & 1, width) == 1
    flip = wide(n & 2, width) == 2
    y, cy, sy = row_of(pos, 1, c), row_of(wave, 2, c), row_of(wave, 3, c)
    base = jnp.where(odd, sy, cy)
    pattern = 0.25 + jnp.where(flip, -base, base)
    halves = []
    for h in range(2):
        gap = nf + 8.0 * h - y
        near = jnp.abs(gap - images[0]) < 2.0
        if len(images) > 1:
            near = jnp.logical_or(near, jnp.abs(gap - images[1]) < 2.0)
        halves.append(jnp.where(near, pattern, 0.0))
    return jnp.concatenate(halves, axis=0)


def nt_dot(a, b):
    return lax.dot_general(a, b, (((1,), (1,)), ((), ())), preferred_element_type=F32)


def stage_kernel(sizes, plan, last, copies, counts, together, *refs):
    _, vertices, extent = sizes
    n_cells, n_sums, n_copied = counts
    here, infos, table = refs[:3]
    refs = refs[3:]
    cells, refs = refs[:n_cells], refs[n_cells:]
    sums, refs = refs[:n_sums], refs[n_sums:]
    n_from = len({c[0] for c in copies})
    givers, refs = refs[:n_from], refs[n_from:]
    if last:
        own, down, up, far = refs[:4]
        refs = refs[4:]
    else:
        acc, refs = refs[0], refs[1:]
    takers, refs = refs[:n_copied], refs[n_copied:]
    pos, wave, force, planar, corner = refs[:5]
    if last:
        acc = refs[5]
    moves = []
    for n, (giver, source, taker, target) in enumerate(copies):
        move = pltpu.make_async_copy(givers[giver].at[source], takers[taker].at[target], refs[5].at[n])
        move.start()
        moves.append(move)
    if sums:
        total = sums[0][...]
        for more in sums[1:]:
            total = total + more[...]
        acc[...] = total
    else:
        acc[...] = jnp.zeros(acc.shape, F32)
    pos[...] = jnp.full(pos.shape, FAR, F32)
    rows = pos.shape[1] - 8
    for r in range(rows + 1):
        for d in range(3):
            corner[r, d] = 0
        for d in range(2):
            corner[r, 3 + d] = 0
    count = jnp.int32(0)
    at = 0
    for array, owner, images, offset in plan:
        block = cells[array]
        for r in range(cell_count(block)):
            target = infos[at, 0]
            wanted = target >= 0 if owner is None else target // sizes[0] == here[owner]
            row = jnp.where(wanted, count, rows)
            for a in range(3):
                pos[a, pl.ds(row, 1), :] = cell_row(block, offset, r, a)
            for d in range(3):
                corner[row, d] = lax.rem(infos[at, 1 + d], extent[d])
            corner[row, 3] = images[0]
            corner[row, 4] = images[-1]
            count = count + wanted.astype(jnp.int32)
            at += 1
    hide_rest(pos, vertices)
    fill_waves(pos, wave)
    fill_force(pos, table, force)

    def weigh(c, b):
        fill_planar(pos, wave, c, planar.at[b, 0:192], planar.at[b, 192:384])
        images = (corner[c, 3].astype(F32), corner[c, 4].astype(F32))
        wy = rows_weight(pos, wave, c, corner[c, 1], images)
        lifted = []
        for a in range(3):
            f = row_of(force, a, c)
            lifted.append(jnp.concatenate([f, f], axis=0) * wy)
        high, low = split(jnp.concatenate(lifted, axis=0))
        both = nt_dot(planar[b], high)
        total = both[:192] + both[192:] + nt_dot(planar[b, 0:192], low)
        x0, z0 = corner[c, 0], corner[c, 2] + 2
        acc[pl.ds(x0, 12), pl.ds(z0, 16), :] += total.reshape(12, 16, 48)

    def weigh_some(i, carry):
        for b in range(together):
            weigh(together * i + b, b)
        return carry

    lax.fori_loop(0, (count + together - 1) // together, weigh_some, 0)
    if last:
        for x in range(23):
            turned = jnp.transpose(acc[x, 8:136, :], (1, 0))
            if REACH - 1 <= x < REACH - 1 + own.shape[0]:
                own[x - REACH + 1] = turned
            if x < down.shape[0]:
                down[x] = turned
            if x >= 23 - up.shape[0]:
                up[x - 23 + up.shape[0]] = turned
        for n in range(3):
            outside = []
            for x in range(8 * n, 8 * n + 8):
                outside += [acc[x, 0:8, :], acc[x, 136:144, :]]
            far[n] = jnp.transpose(jnp.concatenate(outside, axis=0), (1, 0))
    for move in moves:
        move.wait()


def stage(sizes, plan, here, infos, table, cells, sums=(), last=False, givers=(), takers=(), copies=(), together=2):
    width = table.shape[1]
    rows = sum(cell_count(cells[p[0]]) for p in plan)
    counts = (len(cells), len(sums), len(takers))
    whole = pl.BlockSpec(memory_space=pl.ANY)
    fixed = pl.BlockSpec(memory_space=pltpu.HBM)
    return pl.pallas_call(
        functools.partial(stage_kernel, sizes, plan, last, copies, counts, together),
        out_shape=tuple(
            jax.ShapeDtypeStruct(shape, F32)
            for shape in ([(n, 48, 128) for n in (14, REACH + 1, REACH, 3)] if last else [(24, 152, 48)])
        )
        + tuple(takers),
        in_specs=[SMEM, SMEM, VMEM] + [VMEM] * (len(cells) + len(sums)) + [fixed] * len(givers),
        out_specs=(VMEM,) * (4 if last else 1) + (whole,) * len(takers),
        scratch_shapes=[
            pltpu.VMEM((3, rows + 8, width), F32),
            pltpu.VMEM((6, rows, width), F32),
            pltpu.VMEM((3, rows, width), F32),
            pltpu.VMEM((together, 384, width), jnp.bfloat16),
            pltpu.SMEM((rows + 8, 5), jnp.int32),
        ]
        + ([pltpu.VMEM((24, 152, 48), F32)] if last else [])
        + ([pltpu.SemaphoreType.DMA((len(copies),))] if copies else []),
        compiler_params=params(),
        name="spread",
        cost_estimate=pl.CostEstimate(flops=int(4e9), bytes_accessed=4_000_000, transcendentals=0),
    )(here, infos, table, *cells, *sums, *givers)


def fold_kernel(own_in, down_in, up_in, far, own, down, up):
    lane = lax.broadcasted_iota(jnp.int32, (48, 128), 1)
    rim = jnp.logical_or(lane < 8, lane >= 120)
    for x in range(23):
        more = jnp.where(rim, pltpu.roll(far[x // 8], (120 - 16 * (x % 8)) % 128, 1), 0.0)
        if REACH - 1 <= x < REACH - 1 + own.shape[0]:
            own[x - REACH + 1] = own_in[x - REACH + 1] + more
        if x < down.shape[0]:
            down[x] = down_in[x] + more
        n = x - 23 + up.shape[0]
        if n >= 0:
            up[n] = up_in[n] + more


def sample_kernel(images, corner, pos, low_side, own, high_side, low_far, own_far, high_far, out, flow, far, wave, high, low):
    cells = out.shape[1]
    at = 0
    for part, part_far in ((low_side, low_far), (own, own_far), (high_side, high_far)):
        size = part.shape[0]
        flow[at : at + size] = part[...]
        far[at : at + size] = part_far[...]
        at += size
    fill_waves(pos, wave)
    lane = lax.broadcasted_iota(jnp.int32, (8, 128), 1)

    def sample(c, b):
        fill_planar(pos, wave, c, high.at[b], low.at[b])
        z0 = corner[c, 2] - REACH
        x0 = corner[c, 0]
        turn = (z0 + 16 * x0 + 128) & 127
        origin = (lane - turn) & 127
        group = jnp.right_shift(origin, 4)
        z = (origin & 15) + z0
        inside = jnp.logical_and(z >= 0, z < 128)
        chosen = [group == g for g in range(8)]
        blocks = []
        for r in range(6):
            rows = slice(8 * r, 8 * r + 8)
            near = flow[pl.ds(x0, 12), rows, :]
            there = far[pl.ds(x0, 12), rows, :]
            turned = []
            for t in range(2):
                a, b_ = near[8 * t], there[8 * t]
                for g in range(1, 8 - 4 * t):
                    a = jnp.where(chosen[g], near[8 * t + g], a)
                    b_ = jnp.where(chosen[g], there[8 * t + g], b_)
                turned.append(pltpu.roll(jnp.where(inside, a, b_), (128 - turn) & 127, 1))
            blocks.append(jnp.concatenate([turned[0], turned[1][:, 0:64]], axis=1))
        qhigh, qlow = split(jnp.concatenate(blocks, axis=0))
        both = jnp.dot(jnp.concatenate([qhigh, qlow], axis=0), high[b], preferred_element_type=F32)
        mixed = both[:48] + both[48:] + jnp.dot(qhigh, low[b], preferred_element_type=F32)
        wy = rows_weight(pos, wave, c, corner[c, 1], images)
        for a in range(3):
            out[a, pl.ds(c, 1), :] = jnp.sum(mixed[16 * a : 16 * a + 16] * wy, axis=0, keepdims=True)

    def sample_some(i, carry):
        for b in range(4):
            sample(4 * i + b, b)
        return carry

    lax.fori_loop(0, cells // 4, sample_some, 0)


def sampled(cells, images, corner, pos, parts):
    width = pos.shape[2]
    return pl.pallas_call(
        functools.partial(sample_kernel, images),
        out_shape=jax.ShapeDtypeStruct((3, cells, width), F32),
        in_specs=[SMEM] + [VMEM] * 7,
        out_specs=VMEM,
        scratch_shapes=[
            pltpu.VMEM((24, 48, 128), F32),
            pltpu.VMEM((24, 48, 128), F32),
            pltpu.VMEM((6, cells, width), F32),
            pltpu.VMEM((4, 192, width), jnp.bfloat16),
            pltpu.VMEM((4, 192, width), jnp.bfloat16),
        ],
        compiler_params=params(),
        name="sample",
        cost_estimate=pl.CostEstimate(flops=int(2e9), bytes_accessed=4_000_000, transcendentals=0),
    )(corner, pos, *parts)


def extend_kernel(n_low, n_high, pops, x_low, x_high, y_low, y_high, out):
    nx, ny = pops.shape[:2]
    directions = pops.shape[2]
    for x in range(nx + 2):
        middle = x_low[0, :, 0:19, :] if x == 0 else (x_high[0, :, 0:19, :] if x == nx + 1 else pops[x - 1])
        block = jnp.concatenate([y_low[n_low, x : x + 1], middle, y_high[n_high, x : x + 1], y_low[n_low, x : x + 1], y_low[n_low, x : x + 1]], axis=0)
        out[:, x] = jnp.transpose(block, (1, 0, 2))


def collide_kernel(pops, own, from_low, from_high, *refs):
    post, force, edge = refs[-3:]
    planes = pops.shape[1]
    n_low, n_high = from_low.shape[0], from_high.shape[0]
    for e in range(planes):
        total = own[e]
        if e < n_low:
            total = total + from_low[e]
        if e >= planes - n_high:
            total = total + from_high[e - (planes - n_high)]
        force[e] = total
    lane = lax.broadcasted_iota(jnp.int32, (16, 128), 1)

    def plane(e, carry):
        p = [pops[i, e] for i in range(19)]
        f = [force[e, 16 * a : 16 * a + 16, :] for a in range(3)]
        rho = p[0]
        for i in range(1, 19):
            rho = rho + p[i]
        u = []
        for a in range(3):
            m = 0.5 * f[a]
            for i in range(1, 19):
                if DIRS[i][a] == 1:
                    m = m + p[i]
                elif DIRS[i][a] == -1:
                    m = m - p[i]
            u.append(m / rho)
        kinetic = u[0] * u[0] + u[1] * u[1] + u[2] * u[2]
        power = u[0] * f[0] + u[1] * f[1] + u[2] * f[2]
        level = 1.25 * rho * (1.0 - 1.5 * kinetic) - 1.125 * power
        bow, tilt = 5.625 * rho, 3.75 * rho
        new = [None] * 19
        new[0] = WEIGHTS[0] * level - 0.25 * p[0]
        for i in range(1, 19, 2):
            along = [a for a in range(3) if DIRS[i][a] != 0]
            cu, cf = None, None
            for a in along:
                tu, tf = u[a], f[a]
                if DIRS[i][a] < 0:
                    tu, tf = -tu, -tf
                cu = tu if cu is None else cu + tu
                cf = tf if cf is None else cf + tf
            even = WEIGHTS[i] * (level + cu * (bow * cu + 3.375 * cf))
            odd = WEIGHTS[i] * (tilt * cu + 1.125 * cf)
            new[i] = even + odd - 0.25 * p[i]
            new[i + 1] = even - odd - 0.25 * p[i + 1]
        for i in range(19):
            post[i, e] = new[i]
        for j in range(5):
            edge[j, e] = jnp.where(
                lane == 0, pltpu.roll(new[RISING[j]], 1, 1), pltpu.roll(new[FALLING[j]], 127, 1)
            )
        return carry

    lax.fori_loop(0, planes, plane, 0)


def stream_kernel(post, edge, force, pops, own, up, down, velocity):
    ny = pops.shape[1]
    lane = lax.broadcasted_iota(jnp.int32, (ny, 128), 1)
    velocity[...] = jnp.zeros(velocity.shape, F32)

    def plane(x, carry):
        n = []
        for i in range(19):
            cx, cy, cz = DIRS[i]
            value = post[i, x + 1 - cx, 1 - cy : 1 - cy + ny, :]
            if cz == 1:
                side = edge[RISING.index(i), x + 1 - cx, 1 - cy : 1 - cy + ny, :]
                value = jnp.where(lane == 0, side, pltpu.roll(value, 1, 1))
            elif cz == -1:
                side = edge[FALLING.index(i), x + 1 - cx, 1 - cy : 1 - cy + ny, :]
                value = jnp.where(lane == 127, side, pltpu.roll(value, 127, 1))
            n.append(value)
        rho = n[0]
        for i in range(1, 19):
            rho = rho + n[i]
        for a in range(3):
            m = 0.5 * force[x + 1, 16 * a + 1 : 16 * a + 1 + ny, :]
            for i in range(1, 19):
                if DIRS[i][a] == 1:
                    m = m + n[i]
                elif DIRS[i][a] == -1:
                    m = m - n[i]
            velocity[x, 16 * a + 1 : 16 * a + 1 + ny, :] = m / rho
        pops[x] = jnp.transpose(jnp.stack(n), (1, 0, 2))
        return carry

    nx = pops.shape[0]
    lax.fori_loop(0, nx, plane, 0)
    for x in range(nx):
        own[x] = pltpu.roll(velocity[x], 16 * (x + REACH) % 128, 1)
        if x >= nx - REACH:
            up[x - nx + REACH] = pltpu.roll(velocity[x], 16 * (x + REACH - nx) % 128, 1)
        if x < REACH - 1:
            down[x] = pltpu.roll(velocity[x], 16 * (x + REACH + nx) % 128, 1)


def shifted(x, axis, distance):
    count = lax.axis_size(axis)
    return lax.ppermute(x, axis, [(i, (i + distance) % count) for i in range(count)])


def on_device(populations, membrane, anchors, targets):
    extent = populations.shape[1:]
    capacity, _, vertices = membrane.shape
    slabs, crosses, subs = (lax.axis_size(a) for a in ("slab", "cross", "sub"))
    assert subs == 2 and extent == (12, 12, 128) and capacity % 8 == 0
    width = WIDTH
    assert vertices + 4 <= width < vertices + 128
    place = [lax.axis_index(a) for a in ("slab", "cross", "sub")]
    table = chain_table(vertices, width)

    notes = jnp.concatenate([targets[:, None], anchors], axis=1)
    raw = jnp.concatenate(
        [
            jnp.transpose(membrane, (1, 0, 2)),
            jnp.broadcast_to(notes.astype(F32)[None], (3, capacity, 4)),
            jnp.full((3, capacity, width - vertices - 4), FAR, F32),
        ],
        axis=2,
    )
    if crosses == 2:
        beside = [(1, (extent[1], -extent[1]))]
    else:
        beside = [(1, (-extent[1],)), (-1, (extent[1],))]
    owners = [(place[0] * crosses + (place[1] + crosses - d) % crosses) * subs + place[2] for d in [0] + [d for d, _ in beside]]
    here = jnp.stack(place + owners).astype(jnp.int32)
    guests = [shifted(raw, "cross", d) for d, _ in beside]
    groups = 1 + len(beside)
    nx, ny = extent[:2]
    planes = nx + 2
    pops = jnp.transpose(populations, (1, 2, 0, 3))
    sides = jnp.concatenate([pops[nx - 1 :], pops[:1]])
    held = 3 * (width // 128) * MIG
    message = jax.ShapeDtypeStruct((groups * held + 24 * ny + 8, 128), F32)
    home = jnp.concatenate([g[0, :, vertices : vertices + 4].astype(jnp.int32) for g in [raw] + guests])
    up, down = pl.pallas_call(
        functools.partial(pack_kernel, capacity, slabs, crosses * subs, groups),
        out_shape=(message, message),
        in_specs=[SMEM, SMEM] + [VMEM] * (groups + 1),
        out_specs=(VMEM, VMEM),
        compiler_params=params(),
        name="pack",
    )(here, home, raw, *guests, sides)
    sizes = (capacity, vertices, extent)
    below, above = shifted(up, "slab", 1), shifted(down, "slab", -1)
    images = [(0,)] + [image for _, image in beside]

    row = jax.ShapeDtypeStruct((nx,) + pops.shape[2:], F32)
    sum_1, first, last = stage(
        sizes,
        [(g, 3 + g, images[g], 0) for g in range(groups)],
        here,
        home,
        table,
        [raw] + guests,
        givers=(pops,),
        takers=(row, row),
        copies=((0, (pl.ds(0, nx), 0), 0, pl.ds(0, nx)), (0, (pl.ds(0, nx), ny - 1), 1, pl.ds(0, nx))),
        together=4,
    )
    x_low = below[groups * held : groups * held + 24 * ny].reshape(1, ny, 24, 128)
    x_high = above[groups * held : groups * held + 24 * ny].reshape(1, ny, 24, 128)
    first = jnp.concatenate([x_low[:, 0, :19], first, x_high[:, 0, :19]])
    last = jnp.concatenate([x_low[:, -1, :19], last, x_high[:, -1, :19]])
    if crosses == 2:
        rows = shifted(jnp.stack([last, first]), "cross", 1)
        y_low, y_high = (rows, 0), (rows, 1)
    else:
        y_low, y_high = (shifted(last, "cross", 1)[None], 0), (shifted(first, "cross", -1)[None], 0)
    lane = vertices - (width - 128)
    starts = [g * held + (width // 128 - 1) * MIG for g in range(groups)]
    notes_in = [m[s : s + MIG, lane : lane + 4].astype(jnp.int32) for s in starts for m in (below, above)]
    own, down_force, up_force, far = stage(
        sizes,
        [(n, None, images[g], g * held) for g in range(groups) for n in (0, 1)],
        here,
        jnp.concatenate(notes_in),
        table,
        [below, above],
        sums=(sum_1,),
        last=True,
    )
    cells = []
    for block in [raw] + guests:
        cells += [block, below, above]
    offsets = tuple(g * held for g in range(groups) for _ in range(3))
    extended = pl.pallas_call(
        functools.partial(extend_kernel, y_low[1], y_high[1]),
        out_shape=jax.ShapeDtypeStruct((19, planes, 16, 128), F32),
        in_specs=[VMEM] * 5,
        out_specs=VMEM,
        compiler_params=params(),
        name="extend",
    )(pops, x_low, x_high, y_low[0], y_high[0])

    own, down_force, up_force = pl.pallas_call(
        fold_kernel,
        out_shape=tuple(jax.ShapeDtypeStruct((n, 48, 128), F32) for n in (planes, REACH + 1, REACH)),
        in_specs=[VMEM] * 4,
        out_specs=(VMEM,) * 3,
        compiler_params=params(),
        name="fold",
    )(own, down_force, up_force, shifted(far, "sub", 1))
    from_high = shifted(down_force, "slab", -1)
    from_low = shifted(up_force, "slab", 1)

    placed = pl.pallas_call(
        functools.partial(assemble_kernel, sizes, groups, offsets),
        out_shape=(jax.ShapeDtypeStruct((3, capacity + 8, width), F32),) * groups
        + (jax.ShapeDtypeStruct((capacity + 8, 3), jnp.int32),) * groups,
        in_specs=[SMEM, SMEM] + [VMEM] * len(cells) + [pl.BlockSpec(memory_space=pl.ANY)],
        out_specs=(VMEM,) * groups + (SMEM,) * groups,
        compiler_params=params(),
        name="assemble",
    )(here, jnp.concatenate([home] + notes_in), *cells, own)
    positions, corners = placed[:groups], placed[groups:]
    post, force, edge = pl.pallas_call(
        collide_kernel,
        out_shape=(
            jax.ShapeDtypeStruct((19, planes, 16, 128), F32),
            jax.ShapeDtypeStruct((planes, 48, 128), F32),
            jax.ShapeDtypeStruct((5, planes, 16, 128), F32),
        ),
        in_specs=[VMEM] * 4 + [pl.BlockSpec(memory_space=pl.ANY)] * groups,
        out_specs=(VMEM,) * 3,
        compiler_params=params(),
        name="collide",
    )(extended, own, from_low, from_high, *positions)
    edge = shifted(edge, "sub", 1)
    renewed, velocity, up_flow, down_flow = pl.pallas_call(
        stream_kernel,
        out_shape=(jax.ShapeDtypeStruct((extent[0], extent[1], 19, 128), F32),)
        + tuple(jax.ShapeDtypeStruct((n, 48, 128), F32) for n in (extent[0], REACH, REACH - 1)),
        in_specs=[VMEM] * 3,
        out_specs=(VMEM,) * 4,
        scratch_shapes=[pltpu.VMEM((extent[0], 48, 128), F32)],
        compiler_params=params(),
        name="stream",
    )(post, edge, force)

    low_side = shifted(up_flow, "slab", 1)
    high_side = shifted(down_flow, "slab", -1)
    parts = (low_side, velocity, high_side)
    parts = parts + tuple(shifted(part, "sub", 1) for part in parts)
    shares = [
        shifted(sampled(capacity, image, corner, pos, parts), "cross", -d)
        for (d, image), corner, pos in zip(beside, corners[1:], positions[1:])
    ]
    total = sampled(capacity, (0,), corners[0], positions[0], parts)
    for share in shares:
        total = total + share
    return (
        jnp.transpose(renewed, (2, 0, 1, 3)),
        jnp.transpose(total[:, :, :vertices], (1, 0, 2)),
    )


def solution(mesh):
    placed = (
        P(None, ("parts", "slab"), "cross", "sub"),
        P(("parts", "slab", "cross", "sub"), None, None),
        P(("parts", "slab", "cross", "sub"), None),
        P(("parts", "slab", "cross", "sub")),
    )
    return jax.shard_map(
        on_device,
        mesh=mesh,
        in_specs=placed,
        out_specs=(
            P(None, ("parts", "slab"), "cross", "sub"),
            P(("parts", "slab", "cross", "sub"), None, None),
        ),
        check_vma=False,
    )
```

```python
import functools
import math

import jax
import jax.numpy as jnp
import numpy as np
from jax import lax
from jax.experimental import pallas as pl
from jax.experimental.pallas import tpu as pltpu
from jax.sharding import PartitionSpec as P

REACH = 6
MIG = 4
STRIDES = (21, 34, 55)
DIRS = (
    (0, 0, 0),
    (1, 0, 0), (-1, 0, 0), (0, 1, 0), (0, -1, 0), (0, 0, 1), (0, 0, -1),
    (1, 1, 0), (-1, -1, 0), (1, -1, 0), (-1, 1, 0),
    (1, 0, 1), (-1, 0, -1), (1, 0, -1), (-1, 0, 1),
    (0, 1, 1), (0, -1, -1), (0, 1, -1), (0, -1, 1),
)
RISING = (5, 11, 14, 15, 18)
FALLING = (6, 12, 13, 16, 17)
WEIGHTS = (1.0 / 3.0,) + (1.0 / 18.0,) * 6 + (1.0 / 36.0,) * 12
FAR = 100.0
F32 = jnp.float32
WIDTH = 768
VMEM = pl.BlockSpec(memory_space=pltpu.VMEM)
SMEM = pl.BlockSpec(memory_space=pltpu.SMEM)


def params(limit=14):
    return pltpu.CompilerParams(vmem_limit_bytes=limit * 1024 * 1024)


def chain_table(vertices, width):
    v = np.arange(vertices)
    h = 1.0 - (2.0 * v + 1.0) / vertices
    t = 2.0 * math.pi / 2584.0 * (v * 1597 % 2584)
    across = np.sqrt(1.0 - h * h)
    rest = 3.0 * np.stack([across * np.cos(t), across * np.sin(t), h])
    table = np.zeros((16, width))
    for n, s in enumerate(STRIDES):
        gap = rest[:, s:] - rest[:, :-s]
        table[5 * n : 5 * n + 3, : vertices - s] = gap
        table[5 * n + 3, : vertices - s] = 0.05 / np.sum(gap * gap, axis=0)
        table[5 * n + 4, : vertices - s] = 1.0
    return jnp.asarray(table, F32)


def pack_kernel(capacity, slabs, plane, groups, here, infos, *refs):
    cells, (sides, up, down) = refs[:groups], refs[groups:]
    ny, directions = sides.shape[1:3]
    tiles = WIDTH // 128
    held = 3 * tiles * MIG
    spare = up.shape[0] - 8
    up[0 : groups * held, :] = jnp.full((groups * held, 128), -1.0, F32)
    down[0 : groups * held, :] = jnp.full((groups * held, 128), -1.0, F32)
    over = lax.rem(here[0] + 1, slabs)
    under = lax.rem(here[0] + slabs - 1, slabs)
    for g in range(groups):
        n_up, n_down = jnp.int32(0), jnp.int32(0)
        for c in range(capacity):
            owner = infos[g * capacity + c, 0] // capacity
            peer = owner // plane
            leaving = owner != here[3 + g]
            rises = jnp.logical_and(leaving, peer == over)
            falls = jnp.logical_and(leaving, peer == under)
            to_up = g * held + jnp.minimum(n_up, MIG - 1)
            to_down = g * held + jnp.minimum(n_down, MIG - 1)

            def put(message, start):
                for a in range(3):
                    for t in range(tiles):
                        row = cells[g][a, c : c + 1, 128 * t : 128 * t + 128]
                        message[pl.ds(start + (a * tiles + t) * MIG, 1), :] = row

            @pl.when(rises)
            def _():
                put(up, to_up)

            @pl.when(falls)
            def _():
                put(down, to_down)

            n_up = n_up + rises.astype(jnp.int32)
            n_down = n_down + falls.astype(jnp.int32)
    for n, message in enumerate((up, down)):
        for y in range(ny):
            first = groups * held + 24 * y
            message[first : first + directions, :] = sides[n, y]


def cell_row(block, offset, r, a):
    if len(block.shape) == 3:
        return block[a, r : r + 1, :]
    tiles = WIDTH // 128
    first = offset + a * tiles * MIG + r
    return jnp.concatenate([block[first + t * MIG : first + t * MIG + 1, :] for t in range(tiles)], axis=1)


def cell_count(block):
    return block.shape[1] if len(block.shape) == 3 else MIG


def hide_rest(pos, vertices):
    width = pos.shape[2]
    lane = lax.broadcasted_iota(jnp.int32, (pos.shape[1], 128), 1) + (width - 128)
    for a in range(3):
        pos[a, :, width - 128 :] = jnp.where(lane < vertices, pos[a, :, width - 128 :], FAR)


def assemble(capacity, vertices, extent, owner, infos, sources, pos, corner):
    for first, block, offset, migrated in sources:
        for r in range(cell_count(block)):
            target = infos[first + r, 0]
            wanted = target >= 0 if migrated else target // capacity == owner
            slot = jnp.where(wanted, lax.rem(target, capacity), capacity)
            for a in range(3):
                pos[a, pl.ds(slot, 1), :] = cell_row(block, offset, r, a)
            for d in range(3):
                corner[slot, d] = lax.rem(infos[first + r, 1 + d], extent[d])
    hide_rest(pos, vertices)


def assemble_kernel(sizes, groups, offsets, *refs):
    capacity, vertices, extent = sizes
    here, infos = refs[:2]
    cells = refs[2 : 2 + 3 * groups]
    positions, corners = refs[3 + 3 * groups : 3 + 4 * groups], refs[3 + 4 * groups :]
    for g in range(groups):
        start = groups * capacity + g * 2 * MIG
        sources = [
            (g * capacity, cells[3 * g], 0, False),
            (start, cells[3 * g + 1], offsets[3 * g + 1], True),
            (start + MIG, cells[3 * g + 2], offsets[3 * g + 2], True),
        ]
        assemble(capacity, vertices, extent, here[3 + g], infos, sources, positions[g], corners[g])


def wide(tile, width):
    return jnp.concatenate([tile] * (width // 128), axis=1)


def waves(x):
    h = (x - 4.0 * jnp.floor(0.25 * x + 0.5)) * (math.pi / 4.0)
    q = h * h
    sine = h * (1.0 + q * (-1 / 6 + q * (1 / 120 + q * (-1 / 5040 + q * (1 / 362880 - q * (1 / 39916800))))))
    cosine = 1.0 + q * (
        -1 / 2 + q * (1 / 24 + q * (-1 / 720 + q * (1 / 40320 + q * (-1 / 3628800 + q * (1 / 479001600)))))
    )
    return 0.25 - 0.5 * sine * sine, 0.5 * sine * cosine


def fill_waves(pos, wave):
    cells = wave.shape[1]
    for a in range(3):
        wave[2 * a], wave[2 * a + 1] = waves(pos[a, 0:cells, :])


def fill_force(pos, table, force):
    cells, width = force.shape[1:]
    for h in range(cells // 8):
        rows = slice(8 * h, 8 * h + 8)
        x = [pos[a, rows, :] for a in range(3)]
        lap = [jnp.zeros((8, width), F32) for _ in range(3)]
        pulls = []
        for n, s in enumerate(STRIDES):
            gap = [table[5 * n + a : 5 * n + a + 1, :] for a in range(3)]
            scale = table[5 * n + 3 : 5 * n + 4, :]
            mask = table[5 * n + 4 : 5 * n + 5, :]
            d = [pltpu.roll(x[a], width - s, 1) - x[a] for a in range(3)]
            square = d[0] * d[0] + d[1] * d[1] + d[2] * d[2]
            strain = square * scale - 0.05 * mask
            pulls.append([strain * d[a] for a in range(3)])
            for a in range(3):
                bend = mask * d[a] - gap[a]
                lap[a] = lap[a] + bend - pltpu.roll(bend, s, 1)
        for a in range(3):
            total = jnp.zeros((8, width), F32)
            for n, s in enumerate(STRIDES):
                mask = table[5 * n + 4 : 5 * n + 5, :]
                t = pulls[n][a] - 0.002 * (mask * (pltpu.roll(lap[a], width - s, 1) - lap[a]))
                total = total + t - pltpu.roll(t, s, 1)
            force[a, rows, :] = total


def split(x):
    high = x.astype(jnp.bfloat16)
    return high, (x - high.astype(F32)).astype(jnp.bfloat16)


def row_of(ref, i, c):
    return jnp.broadcast_to(ref[i, pl.ds(c, 1), :], (8, ref.shape[2]))


def fill_planar(pos, wave, c, high, low):
    width = pos.shape[2]
    row = lax.broadcasted_iota(jnp.int32, (8, 128), 0)
    rowf = (row - REACH).astype(F32)
    joint = wide(jnp.where(row < 4, rowf + 8.0, rowf - 4.0), width)
    rowf = wide(rowf, width)
    upper = wide(row, width) < 4
    odd = wide((row & 1), width) == 1
    flip = wide((row & 2), width) == 0
    z, cz, sz = row_of(pos, 2, c), row_of(wave, 4, c), row_of(wave, 5, c)
    base = jnp.where(odd, sz, cz)
    pattern = 0.25 + jnp.where(flip, -base, base)
    wz = [
        jnp.where(jnp.abs(rows - z) < 2.0, pattern, 0.0) for rows in (rowf, joint, rowf + 4.0)
    ]
    x, cx, sx = row_of(pos, 0, c), row_of(wave, 0, c), row_of(wave, 1, c)
    quarter = (0.25 - cx, 0.25 - sx, 0.25 + cx, 0.25 + sx)
    for four in range(3):
        tiles = []
        for kx in (4 * four, 4 * four + 2):
            wx = [
                jnp.where(jnp.abs(x - float(k - REACH)) < 2.0, quarter[k % 4], 0.0) for k in (kx, kx + 1)
            ]
            tiles += [wx[0] * wz[0], jnp.where(upper, wx[0], wx[1]) * wz[1], wx[1] * wz[2]]
        rows = slice(48 * four, 48 * four + 48)
        high[rows, :], low[rows, :] = split(jnp.concatenate(tiles, axis=0))


def rows_weight(pos, wave, c, anchor, images):
    width = pos.shape[2]
    n = lax.broadcasted_iota(jnp.int32, (8, 128), 0) - 1 - anchor
    nf = wide(n.astype(F32), width)
    odd = wide(n & 1, width) == 1
    flip = wide(n & 2, width) == 2
    y, cy, sy = row_of(pos, 1, c), row_of(wave, 2, c), row_of(wave, 3, c)
    base = jnp.where(odd, sy, cy)
    pattern = 0.25 + jnp.where(flip, -base, base)
    halves = []
    for h in range(2):
        gap = nf + 8.0 * h - y
        near = jnp.abs(gap - images[0]) < 2.0
        if len(images) > 1:
            near = jnp.logical_or(near, jnp.abs(gap - images[1]) < 2.0)
        halves.append(jnp.where(near, pattern, 0.0))
    return jnp.concatenate(halves, axis=0)


def nt_dot(a, b):
    return lax.dot_general(a, b, (((1,), (1,)), ((), ())), preferred_element_type=F32)


def stage_kernel(sizes, plan, last, copies, counts, together, *refs):
    _, vertices, extent = sizes
    n_cells, n_sums, n_copied = counts
    here, infos, table = refs[:3]
    refs = refs[3:]
    cells, refs = refs[:n_cells], refs[n_cells:]
    sums, refs = refs[:n_sums], refs[n_sums:]
    n_from = len({c[0] for c in copies})
    givers, refs = refs[:n_from], refs[n_from:]
    if last:
        own, down, up, far = refs[:4]
        refs = refs[4:]
    else:
        acc, refs = refs[0], refs[1:]
    takers, refs = refs[:n_copied], refs[n_copied:]
    pos, wave, force, planar, corner, patch = refs[:6]
    if last:
        acc = refs[6]
    moves = []
    for n, (giver, source, taker, target) in enumerate(copies):
        move = pltpu.make_async_copy(givers[giver].at[source], takers[taker].at[target], refs[-1].at[n])
        move.start()
        moves.append(move)
    if sums:
        total = sums[0][...]
        for more in sums[1:]:
            total = total + more[...]
        acc[...] = total
    else:
        acc[...] = jnp.zeros(acc.shape, F32)
    pos[...] = jnp.full(pos.shape, FAR, F32)
    rows = pos.shape[1] - 8
    for r in range(rows + 1):
        for d in range(3):
            corner[r, d] = 0
        for d in range(2):
            corner[r, 3 + d] = 0
    count = jnp.int32(0)
    at = 0
    for array, owner, images, offset in plan:
        block = cells[array]
        for r in range(cell_count(block)):
            target = infos[at, 0]
            wanted = target >= 0 if owner is None else target // sizes[0] == here[owner]
            row = jnp.where(wanted, count, rows)
            for a in range(3):
                pos[a, pl.ds(row, 1), :] = cell_row(block, offset, r, a)
            for d in range(3):
                corner[row, d] = lax.rem(infos[at, 1 + d], extent[d])
            corner[row, 3] = images[0]
            corner[row, 4] = images[-1]
            count = count + wanted.astype(jnp.int32)
            at += 1
    hide_rest(pos, vertices)
    fill_waves(pos, wave)
    fill_force(pos, table, force)

    def weigh(c, b):
        fill_planar(pos, wave, c, planar.at[b, 0:144], planar.at[b, 144:288])
        images = (corner[c, 3].astype(F32), corner[c, 4].astype(F32))
        wy = rows_weight(pos, wave, c, corner[c, 1], images)
        lifted = []
        for a in range(3):
            f = row_of(force, a, c)
            lifted.append(jnp.concatenate([f, f], axis=0) * wy)
        high, low = split(jnp.concatenate(lifted, axis=0))
        both = nt_dot(planar[b], high)
        patch[b] = both[:144] + both[144:] + nt_dot(planar[b, 0:144], low)
        x0, z0 = corner[c, 0], corner[c, 2] + 2
        before = [acc[x0 + kx, pl.ds(z0, 12), :] for kx in range(12)]
        for kx in range(12):
            acc[x0 + kx, pl.ds(z0, 12), :] = before[kx] + patch[b, 12 * kx : 12 * kx + 12, :]

    def weigh_some(i, carry):
        for b in range(together):
            weigh(together * i + b, b)
        return carry

    lax.fori_loop(0, (count + together - 1) // together, weigh_some, 0)
    if last:
        for x in range(23):
            turned = jnp.transpose(acc[x, 8:136, :], (1, 0))
            if REACH - 1 <= x < REACH - 1 + own.shape[0]:
                own[x - REACH + 1] = turned
            if x < down.shape[0]:
                down[x] = turned
            if x >= 23 - up.shape[0]:
                up[x - 23 + up.shape[0]] = turned
        for n in range(3):
            outside = []
            for x in range(8 * n, 8 * n + 8):
                outside += [acc[x, 0:8, :], acc[x, 136:144, :]]
            far[n] = jnp.transpose(jnp.concatenate(outside, axis=0), (1, 0))
    for move in moves:
        move.wait()


def stage(sizes, plan, here, infos, table, cells, sums=(), last=False, givers=(), takers=(), copies=(), together=2):
    width = table.shape[1]
    rows = sum(cell_count(cells[p[0]]) for p in plan)
    counts = (len(cells), len(sums), len(takers))
    whole = pl.BlockSpec(memory_space=pl.ANY)
    fixed = pl.BlockSpec(memory_space=pltpu.HBM)
    return pl.pallas_call(
        functools.partial(stage_kernel, sizes, plan, last, copies, counts, together),
        out_shape=tuple(
            jax.ShapeDtypeStruct(shape, F32)
            for shape in ([(n, 48, 128) for n in (14, REACH + 1, REACH, 3)] if last else [(24, 152, 48)])
        )
        + tuple(takers),
        in_specs=[SMEM, SMEM, VMEM] + [VMEM] * (len(cells) + len(sums)) + [fixed] * len(givers),
        out_specs=(VMEM,) * (4 if last else 1) + (whole,) * len(takers),
        scratch_shapes=[
            pltpu.VMEM((3, rows + 8, width), F32),
            pltpu.VMEM((6, rows, width), F32),
            pltpu.VMEM((3, rows, width), F32),
            pltpu.VMEM((together, 288, width), jnp.bfloat16),
            pltpu.SMEM((rows + 8, 5), jnp.int32),
            pltpu.VMEM((together, 144, 48), F32),
        ]
        + ([pltpu.VMEM((24, 152, 48), F32)] if last else [])
        + ([pltpu.SemaphoreType.DMA((len(copies),))] if copies else []),
        compiler_params=params(),
        name="spread",
        cost_estimate=pl.CostEstimate(flops=int(4e9), bytes_accessed=4_000_000, transcendentals=0),
    )(here, infos, table, *cells, *sums, *givers)


def fold_kernel(own_in, down_in, up_in, far, own, down, up):
    lane = lax.broadcasted_iota(jnp.int32, (48, 128), 1)
    rim = jnp.logical_or(lane < 8, lane >= 120)
    for x in range(23):
        more = jnp.where(rim, pltpu.roll(far[x // 8], (120 - 16 * (x % 8)) % 128, 1), 0.0)
        if REACH - 1 <= x < REACH - 1 + own.shape[0]:
            own[x - REACH + 1] = own_in[x - REACH + 1] + more
        if x < down.shape[0]:
            down[x] = down_in[x] + more
        n = x - 23 + up.shape[0]
        if n >= 0:
            up[n] = up_in[n] + more


def sample_kernel(images, corner, pos, low_side, own, high_side, low_far, own_far, high_far, out, flow, far, wave, high, low):
    cells = out.shape[1]
    at = 0
    for part, part_far in ((low_side, low_far), (own, own_far), (high_side, high_far)):
        size = part.shape[0]
        flow[at : at + size] = part[...]
        far[at : at + size] = part_far[...]
        at += size
    fill_waves(pos, wave)
    lane = lax.broadcasted_iota(jnp.int32, (8, 128), 1)

    def sample(c, b):
        fill_planar(pos, wave, c, high.at[b], low.at[b])
        z0 = corner[c, 2] - REACH
        x0 = corner[c, 0]
        turn = (z0 + 12 * x0 + 128) & 127
        inside, chosen = [], []
        for t in range(2):
            origin = (lane - turn - 72 * t) & 127
            group = jnp.right_shift(origin * 43, 9)
            z = origin - 12 * group + z0
            inside.append(jnp.logical_and(z >= 0, z < 128))
            chosen.append([group == g for g in range(6)])
        front = lane < 72
        blocks = []
        for r in range(6):
            rows = slice(8 * r, 8 * r + 8)
            near = [flow[x0 + kx, rows, :] for kx in range(12)]
            there = [far[x0 + kx, rows, :] for kx in range(12)]
            turned = []
            for t in range(2):
                a, b_ = near[6 * t], there[6 * t]
                for g in range(1, 6):
                    a = jnp.where(chosen[t][g], near[6 * t + g], a)
                    b_ = jnp.where(chosen[t][g], there[6 * t + g], b_)
                turned.append(pltpu.roll(jnp.where(inside[t], a, b_), (128 - turn) & 127, 1))
            blocks.append(
                jnp.concatenate([jnp.where(front, turned[0], turned[1]), turned[1][:, 0:16]], axis=1)
            )
        qhigh, qlow = split(jnp.concatenate(blocks, axis=0))
        both = jnp.dot(jnp.concatenate([qhigh, qlow], axis=0), high[b], preferred_element_type=F32)
        mixed = both[:48] + both[48:] + jnp.dot(qhigh, low[b], preferred_element_type=F32)
        wy = rows_weight(pos, wave, c, corner[c, 1], images)
        for a in range(3):
            out[a, pl.ds(c, 1), :] = jnp.sum(mixed[16 * a : 16 * a + 16] * wy, axis=0, keepdims=True)

    def sample_some(i, carry):
        for b in range(4):
            sample(4 * i + b, b)
        return carry

    lax.fori_loop(0, cells // 4, sample_some, 0)


def sampled(cells, images, corner, pos, parts):
    width = pos.shape[2]
    return pl.pallas_call(
        functools.partial(sample_kernel, images),
        out_shape=jax.ShapeDtypeStruct((3, cells, width), F32),
        in_specs=[SMEM] + [VMEM] * 7,
        out_specs=VMEM,
        scratch_shapes=[
            pltpu.VMEM((24, 48, 128), F32),
            pltpu.VMEM((24, 48, 128), F32),
            pltpu.VMEM((6, cells, width), F32),
            pltpu.VMEM((4, 144, width), jnp.bfloat16),
            pltpu.VMEM((4, 144, width), jnp.bfloat16),
        ],
        compiler_params=params(),
        name="sample",
        cost_estimate=pl.CostEstimate(flops=int(2e9), bytes_accessed=4_000_000, transcendentals=0),
    )(corner, pos, *parts)


def extend_kernel(n_low, n_high, pops, x_low, x_high, y_low, y_high, out):
    nx, ny = pops.shape[:2]
    directions = pops.shape[2]
    for x in range(nx + 2):
        middle = x_low[0, :, 0:19, :] if x == 0 else (x_high[0, :, 0:19, :] if x == nx + 1 else pops[x - 1])
        block = jnp.concatenate([y_low[n_low, x : x + 1], middle, y_high[n_high, x : x + 1], y_low[n_low, x : x + 1], y_low[n_low, x : x + 1]], axis=0)
        out[:, x] = jnp.transpose(block, (1, 0, 2))


def collide_kernel(pops, own, from_low, from_high, *refs):
    post, force, edge = refs[-3:]
    planes = pops.shape[1]
    n_low, n_high = from_low.shape[0], from_high.shape[0]
    for e in range(planes):
        total = own[e]
        if e < n_low:
            total = total + from_low[e]
        if e >= planes - n_high:
            total = total + from_high[e - (planes - n_high)]
        force[e] = total
    lane = lax.broadcasted_iota(jnp.int32, (16, 128), 1)

    def plane(e, carry):
        p = [pops[i, e] for i in range(19)]
        f = [force[e, 16 * a : 16 * a + 16, :] for a in range(3)]
        rho = p[0]
        for i in range(1, 19):
            rho = rho + p[i]
        u = []
        for a in range(3):
            m = 0.5 * f[a]
            for i in range(1, 19):
                if DIRS[i][a] == 1:
                    m = m + p[i]
                elif DIRS[i][a] == -1:
                    m = m - p[i]
            u.append(m / rho)
        kinetic = u[0] * u[0] + u[1] * u[1] + u[2] * u[2]
        power = u[0] * f[0] + u[1] * f[1] + u[2] * f[2]
        level = 1.25 * rho * (1.0 - 1.5 * kinetic) - 1.125 * power
        bow, tilt = 5.625 * rho, 3.75 * rho
        new = [None] * 19
        new[0] = WEIGHTS[0] * level - 0.25 * p[0]
        for i in range(1, 19, 2):
            along = [a for a in range(3) if DIRS[i][a] != 0]
            cu, cf = None, None
            for a in along:
                tu, tf = u[a], f[a]
                if DIRS[i][a] < 0:
                    tu, tf = -tu, -tf
                cu = tu if cu is None else cu + tu
                cf = tf if cf is None else cf + tf
            even = WEIGHTS[i] * (level + cu * (bow * cu + 3.375 * cf))
            odd = WEIGHTS[i] * (tilt * cu + 1.125 * cf)
            new[i] = even + odd - 0.25 * p[i]
            new[i + 1] = even - odd - 0.25 * p[i + 1]
        for i in range(19):
            post[i, e] = new[i]
        for j in range(5):
            edge[j, e] = jnp.where(
                lane == 0, pltpu.roll(new[RISING[j]], 1, 1), pltpu.roll(new[FALLING[j]], 127, 1)
            )
        return carry

    lax.fori_loop(0, planes, plane, 0)


def arriving(post, edge, x, ny):
    lane = lax.broadcasted_iota(jnp.int32, (ny, 128), 1)
    found = []
    for i in range(19):
        cx, cy, cz = DIRS[i]
        value = post[i, x + 1 - cx, 1 - cy : 1 - cy + ny, :]
        if cz == 1:
            side = edge[RISING.index(i), x + 1 - cx, 1 - cy : 1 - cy + ny, :]
            value = jnp.where(lane == 0, side, pltpu.roll(value, 1, 1))
        elif cz == -1:
            side = edge[FALLING.index(i), x + 1 - cx, 1 - cy : 1 - cy + ny, :]
            value = jnp.where(lane == 127, side, pltpu.roll(value, 127, 1))
        found.append(value)
    return found


def flow_kernel(ny, post, edge, force, own, up, down, velocity):
    nx = own.shape[0]
    velocity[...] = jnp.zeros(velocity.shape, F32)

    def plane(x, carry):
        n = arriving(post, edge, x, ny)
        rho = n[0]
        for i in range(1, 19):
            rho = rho + n[i]
        for a in range(3):
            m = 0.5 * force[x + 1, 16 * a + 1 : 16 * a + 1 + ny, :]
            for i in range(1, 19):
                if DIRS[i][a] == 1:
                    m = m + n[i]
                elif DIRS[i][a] == -1:
                    m = m - n[i]
            velocity[x, 16 * a + 1 : 16 * a + 1 + ny, :] = m / rho
        return carry

    lax.fori_loop(0, nx, plane, 0)
    for x in range(nx):
        own[x] = pltpu.roll(velocity[x], 12 * (x + REACH) % 128, 1)
        if x >= nx - REACH:
            up[x - nx + REACH] = pltpu.roll(velocity[x], 12 * (x + REACH - nx) % 128, 1)
        if x < REACH - 1:
            down[x] = pltpu.roll(velocity[x], 12 * (x + REACH + nx) % 128, 1)


def renew_kernel(post, edge, after, pops):
    def plane(x, carry):
        pops[x] = jnp.transpose(jnp.stack(arriving(post, edge, x, pops.shape[1])), (1, 0, 2))
        return carry

    lax.fori_loop(0, pops.shape[0], plane, 0)


def shifted(x, axis, distance):
    count = lax.axis_size(axis)
    return lax.ppermute(x, axis, [(i, (i + distance) % count) for i in range(count)])


def on_device(populations, membrane, anchors, targets):
    extent = populations.shape[1:]
    capacity, _, vertices = membrane.shape
    slabs, crosses, subs = (lax.axis_size(a) for a in ("slab", "cross", "sub"))
    assert subs == 2 and extent == (12, 12, 128) and capacity % 8 == 0
    width = WIDTH
    assert vertices + 4 <= width < vertices + 128
    place = [lax.axis_index(a) for a in ("slab", "cross", "sub")]
    table = chain_table(vertices, width)

    notes = jnp.concatenate([targets[:, None], anchors], axis=1)
    raw = jnp.concatenate(
        [
            jnp.transpose(membrane, (1, 0, 2)),
            jnp.broadcast_to(notes.astype(F32)[None], (3, capacity, 4)),
            jnp.full((3, capacity, width - vertices - 4), FAR, F32),
        ],
        axis=2,
    )
    if crosses == 2:
        beside = [(1, (extent[1], -extent[1]))]
    else:
        beside = [(1, (-extent[1],)), (-1, (extent[1],))]
    owners = [(place[0] * crosses + (place[1] + crosses - d) % crosses) * subs + place[2] for d in [0] + [d for d, _ in beside]]
    here = jnp.stack(place + owners).astype(jnp.int32)
    guests = [shifted(raw, "cross", d) for d, _ in beside]
    groups = 1 + len(beside)
    nx, ny = extent[:2]
    planes = nx + 2
    pops = jnp.transpose(populations, (1, 2, 0, 3))
    sides = jnp.concatenate([pops[nx - 1 :], pops[:1]])
    held = 3 * (width // 128) * MIG
    message = jax.ShapeDtypeStruct((groups * held + 24 * ny + 8, 128), F32)
    home = jnp.concatenate([g[0, :, vertices : vertices + 4].astype(jnp.int32) for g in [raw] + guests])
    up, down = pl.pallas_call(
        functools.partial(pack_kernel, capacity, slabs, crosses * subs, groups),
        out_shape=(message, message),
        in_specs=[SMEM, SMEM] + [VMEM] * (groups + 1),
        out_specs=(VMEM, VMEM),
        compiler_params=params(),
        name="pack",
    )(here, home, raw, *guests, sides)
    sizes = (capacity, vertices, extent)
    below, above = shifted(up, "slab", 1), shifted(down, "slab", -1)
    images = [(0,)] + [image for _, image in beside]

    row = jax.ShapeDtypeStruct((nx,) + pops.shape[2:], F32)
    sum_1, first, last = stage(
        sizes,
        [(g, 3 + g, images[g], 0) for g in range(groups)],
        here,
        home,
        table,
        [raw] + guests,
        givers=(pops,),
        takers=(row, row),
        copies=((0, (pl.ds(0, nx), 0), 0, pl.ds(0, nx)), (0, (pl.ds(0, nx), ny - 1), 1, pl.ds(0, nx))),
        together=4,
    )
    x_low = below[groups * held : groups * held + 24 * ny].reshape(1, ny, 24, 128)
    x_high = above[groups * held : groups * held + 24 * ny].reshape(1, ny, 24, 128)
    first = jnp.concatenate([x_low[:, 0, :19], first, x_high[:, 0, :19]])
    last = jnp.concatenate([x_low[:, -1, :19], last, x_high[:, -1, :19]])
    if crosses == 2:
        rows = shifted(jnp.stack([last, first]), "cross", 1)
        y_low, y_high = (rows, 0), (rows, 1)
    else:
        y_low, y_high = (shifted(last, "cross", 1)[None], 0), (shifted(first, "cross", -1)[None], 0)
    lane = vertices - (width - 128)
    starts = [g * held + (width // 128 - 1) * MIG for g in range(groups)]
    notes_in = [m[s : s + MIG, lane : lane + 4].astype(jnp.int32) for s in starts for m in (below, above)]
    own, down_force, up_force, far = stage(
        sizes,
        [(n, None, images[g], g * held) for g in range(groups) for n in (0, 1)],
        here,
        jnp.concatenate(notes_in),
        table,
        [below, above],
        sums=(sum_1,),
        last=True,
    )
    cells = []
    for block in [raw] + guests:
        cells += [block, below, above]
    offsets = tuple(g * held for g in range(groups) for _ in range(3))
    extended = pl.pallas_call(
        functools.partial(extend_kernel, y_low[1], y_high[1]),
        out_shape=jax.ShapeDtypeStruct((19, planes, 16, 128), F32),
        in_specs=[VMEM] * 5,
        out_specs=VMEM,
        compiler_params=params(),
        name="extend",
    )(pops, x_low, x_high, y_low[0], y_high[0])

    own, down_force, up_force = pl.pallas_call(
        fold_kernel,
        out_shape=tuple(jax.ShapeDtypeStruct((n, 48, 128), F32) for n in (planes, REACH + 1, REACH)),
        in_specs=[VMEM] * 4,
        out_specs=(VMEM,) * 3,
        compiler_params=params(),
        name="fold",
    )(own, down_force, up_force, shifted(far, "sub", 1))
    from_high = shifted(down_force, "slab", -1)
    from_low = shifted(up_force, "slab", 1)

    placed = pl.pallas_call(
        functools.partial(assemble_kernel, sizes, groups, offsets),
        out_shape=(jax.ShapeDtypeStruct((3, capacity + 8, width), F32),) * groups
        + (jax.ShapeDtypeStruct((capacity + 8, 3), jnp.int32),) * groups,
        in_specs=[SMEM, SMEM] + [VMEM] * len(cells) + [pl.BlockSpec(memory_space=pl.ANY)],
        out_specs=(VMEM,) * groups + (SMEM,) * groups,
        compiler_params=params(),
        name="assemble",
    )(here, jnp.concatenate([home] + notes_in), *cells, own)
    positions, corners = placed[:groups], placed[groups:]
    post, force, edge = pl.pallas_call(
        collide_kernel,
        out_shape=(
            jax.ShapeDtypeStruct((19, planes, 16, 128), F32),
            jax.ShapeDtypeStruct((planes, 48, 128), F32),
            jax.ShapeDtypeStruct((5, planes, 16, 128), F32),
        ),
        in_specs=[VMEM] * 4 + [pl.BlockSpec(memory_space=pl.ANY)] * groups,
        out_specs=(VMEM,) * 3,
        compiler_params=params(),
        name="collide",
    )(extended, own, from_low, from_high, *positions)
    edge = shifted(edge, "sub", 1)
    velocity, up_flow, down_flow = pl.pallas_call(
        functools.partial(flow_kernel, ny),
        out_shape=tuple(jax.ShapeDtypeStruct((n, 48, 128), F32) for n in (nx, REACH, REACH - 1)),
        in_specs=[VMEM] * 3,
        out_specs=(VMEM,) * 3,
        scratch_shapes=[pltpu.VMEM((nx, 48, 128), F32)],
        compiler_params=params(),
        name="flow",
    )(post, edge, force)
    renewed = pl.pallas_call(
        renew_kernel,
        out_shape=jax.ShapeDtypeStruct((nx, ny, 19, 128), F32),
        in_specs=[VMEM] * 2 + [pl.BlockSpec(memory_space=pl.ANY)],
        out_specs=VMEM,
        compiler_params=params(),
        name="renew",
    )(post, edge, velocity)

    low_side = shifted(up_flow, "slab", 1)
    high_side = shifted(down_flow, "slab", -1)
    low_side, high_side, renewed = lax.optimization_barrier((low_side, high_side, renewed))
    parts = (low_side, velocity, high_side)
    parts = parts + tuple(shifted(part, "sub", 1) for part in parts)
    shares = [
        shifted(sampled(capacity, image, corner, pos, parts), "cross", -d)
        for (d, image), corner, pos in zip(beside, corners[1:], positions[1:])
    ]
    total = sampled(capacity, (0,), corners[0], positions[0], parts)
    for share in shares:
        total = total + share
    return (
        jnp.transpose(renewed, (2, 0, 1, 3)),
        jnp.transpose(total[:, :, :vertices], (1, 0, 2)),
    )


def solution(mesh):
    placed = (
        P(None, ("parts", "slab"), "cross", "sub"),
        P(("parts", "slab", "cross", "sub"), None, None),
        P(("parts", "slab", "cross", "sub"), None),
        P(("parts", "slab", "cross", "sub")),
    )
    return jax.shard_map(
        on_device,
        mesh=mesh,
        in_specs=placed,
        out_specs=(
            P(None, ("parts", "slab"), "cross", "sub"),
            P(("parts", "slab", "cross", "sub"), None, None),
        ),
        check_vma=False,
    )
```

```python
import functools
import math

import jax
import jax.numpy as jnp
import numpy as np
from jax import lax
from jax.experimental import pallas as pl
from jax.experimental.pallas import tpu as pltpu
from jax.sharding import PartitionSpec as P

REACH = 6
MIG = 4
STRIDES = (21, 34, 55)
DIRS = (
    (0, 0, 0),
    (1, 0, 0), (-1, 0, 0), (0, 1, 0), (0, -1, 0), (0, 0, 1), (0, 0, -1),
    (1, 1, 0), (-1, -1, 0), (1, -1, 0), (-1, 1, 0),
    (1, 0, 1), (-1, 0, -1), (1, 0, -1), (-1, 0, 1),
    (0, 1, 1), (0, -1, -1), (0, 1, -1), (0, -1, 1),
)
RISING = (5, 11, 14, 15, 18)
FALLING = (6, 12, 13, 16, 17)
WEIGHTS = (1.0 / 3.0,) + (1.0 / 18.0,) * 6 + (1.0 / 36.0,) * 12
FAR = 100.0
F32 = jnp.float32
WIDTH = 768
VMEM = pl.BlockSpec(memory_space=pltpu.VMEM)
SMEM = pl.BlockSpec(memory_space=pltpu.SMEM)


def params(limit=14):
    return pltpu.CompilerParams(vmem_limit_bytes=limit * 1024 * 1024)


def chain_table(vertices, width):
    v = np.arange(vertices)
    h = 1.0 - (2.0 * v + 1.0) / vertices
    t = 2.0 * math.pi / 2584.0 * (v * 1597 % 2584)
    across = np.sqrt(1.0 - h * h)
    rest = 3.0 * np.stack([across * np.cos(t), across * np.sin(t), h])
    table = np.zeros((16, width))
    for n, s in enumerate(STRIDES):
        gap = rest[:, s:] - rest[:, :-s]
        table[5 * n : 5 * n + 3, : vertices - s] = gap
        table[5 * n + 3, : vertices - s] = 0.05 / np.sum(gap * gap, axis=0)
        table[5 * n + 4, : vertices - s] = 1.0
    return jnp.asarray(table, F32)


def pack_kernel(capacity, slabs, plane, groups, begun, here, infos, *refs):
    tiles = WIDTH // 128
    held = 3 * tiles * MIG
    over = lax.rem(here[0] + 1, slabs)
    under = lax.rem(here[0] + slabs - 1, slabs)
    if begun:
        cells, (up_begun, down_begun, up, down) = refs[: groups - 1], refs[groups - 1 :]
        up[...] = up_begun[...]
        down[...] = down_begun[...]
    else:
        cells, (sides, up, down) = refs[:1], refs[1:]
        up[0 : groups * held, :] = jnp.full((groups * held, 128), -1.0, F32)
        down[0 : groups * held, :] = jnp.full((groups * held, 128), -1.0, F32)
        ny, directions = sides.shape[1:3]
        for n, message in enumerate((up, down)):
            for y in range(ny):
                first = groups * held + 24 * y
                message[first : first + directions, :] = sides[n, y]
    for n, block in enumerate(cells):
        g = n + begun
        n_up, n_down = jnp.int32(0), jnp.int32(0)
        for c in range(capacity):
            owner = infos[n * capacity + c, 0] // capacity
            peer = owner // plane
            leaving = owner != here[3 + g]
            rises = jnp.logical_and(leaving, peer == over)
            falls = jnp.logical_and(leaving, peer == under)
            to_up = g * held + jnp.minimum(n_up, MIG - 1)
            to_down = g * held + jnp.minimum(n_down, MIG - 1)

            def put(message, start):
                for a in range(3):
                    for t in range(tiles):
                        row = block[a, c : c + 1, 128 * t : 128 * t + 128]
                        message[pl.ds(start + (a * tiles + t) * MIG, 1), :] = row

            @pl.when(rises)
            def _():
                put(up, to_up)

            @pl.when(falls)
            def _():
                put(down, to_down)

            n_up = n_up + rises.astype(jnp.int32)
            n_down = n_down + falls.astype(jnp.int32)


def cell_row(block, offset, r, a):
    if len(block.shape) == 3:
        return block[a, r : r + 1, :]
    tiles = WIDTH // 128
    first = offset + a * tiles * MIG + r
    return jnp.concatenate([block[first + t * MIG : first + t * MIG + 1, :] for t in range(tiles)], axis=1)


def cell_count(block):
    return block.shape[1] if len(block.shape) == 3 else MIG


def hide_rest(pos, vertices):
    width = pos.shape[2]
    lane = lax.broadcasted_iota(jnp.int32, (pos.shape[1], 128), 1) + (width - 128)
    for a in range(3):
        pos[a, :, width - 128 :] = jnp.where(lane < vertices, pos[a, :, width - 128 :], FAR)


def assemble(capacity, vertices, extent, owner, infos, sources, pos, corner):
    for first, block, offset, migrated in sources:
        for r in range(cell_count(block)):
            target = infos[first + r, 0]
            wanted = target >= 0 if migrated else target // capacity == owner
            slot = jnp.where(wanted, lax.rem(target, capacity), capacity)
            for a in range(3):
                pos[a, pl.ds(slot, 1), :] = cell_row(block, offset, r, a)
            for d in range(3):
                corner[slot, d] = lax.rem(infos[first + r, 1 + d], extent[d])
    hide_rest(pos, vertices)


def assemble_kernel(sizes, groups, offsets, *refs):
    capacity, vertices, extent = sizes
    here, infos = refs[:2]
    cells = refs[2 : 2 + 3 * groups]
    positions, corners = refs[3 + 3 * groups : 3 + 4 * groups], refs[3 + 4 * groups :]
    for g in range(groups):
        start = groups * capacity + g * 2 * MIG
        sources = [
            (g * capacity, cells[3 * g], 0, False),
            (start, cells[3 * g + 1], offsets[3 * g + 1], True),
            (start + MIG, cells[3 * g + 2], offsets[3 * g + 2], True),
        ]
        assemble(capacity, vertices, extent, here[3 + g], infos, sources, positions[g], corners[g])


def wide(tile, width):
    return jnp.concatenate([tile] * (width // 128), axis=1)


def waves(x):
    h = (x - 4.0 * jnp.floor(0.25 * x + 0.5)) * (math.pi / 4.0)
    q = h * h
    sine = h * (1.0 + q * (-1 / 6 + q * (1 / 120 + q * (-1 / 5040 + q * (1 / 362880 - q * (1 / 39916800))))))
    cosine = 1.0 + q * (
        -1 / 2 + q * (1 / 24 + q * (-1 / 720 + q * (1 / 40320 + q * (-1 / 3628800 + q * (1 / 479001600)))))
    )
    return 0.25 - 0.5 * sine * sine, 0.5 * sine * cosine


def fill_waves(pos, wave):
    cells = wave.shape[1]
    for a in range(3):
        wave[2 * a], wave[2 * a + 1] = waves(pos[a, 0:cells, :])


def fill_force(pos, table, wave, force, count):
    cells, width = force.shape[1:]

    def some(h):
        rows = slice(8 * h, 8 * h + 8)
        for a in range(3):
            wave[2 * a, rows, :], wave[2 * a + 1, rows, :] = waves(pos[a, rows, :])
        x = [pos[a, rows, :] for a in range(3)]
        lap = [jnp.zeros((8, width), F32) for _ in range(3)]
        pulls = []
        for n, s in enumerate(STRIDES):
            gap = [table[5 * n + a : 5 * n + a + 1, :] for a in range(3)]
            scale = table[5 * n + 3 : 5 * n + 4, :]
            mask = table[5 * n + 4 : 5 * n + 5, :]
            d = [pltpu.roll(x[a], width - s, 1) - x[a] for a in range(3)]
            square = d[0] * d[0] + d[1] * d[1] + d[2] * d[2]
            strain = square * scale - 0.05 * mask
            pulls.append([strain * d[a] for a in range(3)])
            for a in range(3):
                bend = mask * d[a] - gap[a]
                lap[a] = lap[a] + bend - pltpu.roll(bend, s, 1)
        for a in range(3):
            total = jnp.zeros((8, width), F32)
            for n, s in enumerate(STRIDES):
                mask = table[5 * n + 4 : 5 * n + 5, :]
                t = pulls[n][a] - 0.002 * (mask * (pltpu.roll(lap[a], width - s, 1) - lap[a]))
                total = total + t - pltpu.roll(t, s, 1)
            force[a, rows, :] = total

    for h in range(cells // 8):
        pl.when(8 * h < count)(functools.partial(some, h))


def split(x):
    high = x.astype(jnp.bfloat16)
    return high, (x - high.astype(F32)).astype(jnp.bfloat16)


def row_of(ref, i, c):
    return jnp.broadcast_to(ref[i, pl.ds(c, 1), :], (8, ref.shape[2]))


def fill_planar(pos, wave, c, high, low):
    width = pos.shape[2]
    row = lax.broadcasted_iota(jnp.int32, (8, 128), 0)
    rowf = (row - REACH).astype(F32)
    joint = wide(jnp.where(row < 4, rowf + 8.0, rowf - 4.0), width)
    rowf = wide(rowf, width)
    upper = wide(row, width) < 4
    odd = wide((row & 1), width) == 1
    flip = wide((row & 2), width) == 0
    z, cz, sz = row_of(pos, 2, c), row_of(wave, 4, c), row_of(wave, 5, c)
    base = jnp.where(odd, sz, cz)
    pattern = 0.25 + jnp.where(flip, -base, base)
    wz = [
        jnp.where(jnp.abs(rows - z) < 2.0, pattern, 0.0) for rows in (rowf, joint, rowf + 4.0)
    ]
    x, cx, sx = row_of(pos, 0, c), row_of(wave, 0, c), row_of(wave, 1, c)
    quarter = (0.25 - cx, 0.25 - sx, 0.25 + cx, 0.25 + sx)
    for four in range(3):
        tiles = []
        for kx in (4 * four, 4 * four + 2):
            wx = [
                jnp.where(jnp.abs(x - float(k - REACH)) < 2.0, quarter[k % 4], 0.0) for k in (kx, kx + 1)
            ]
            tiles += [wx[0] * wz[0], jnp.where(upper, wx[0], wx[1]) * wz[1], wx[1] * wz[2]]
        rows = slice(48 * four, 48 * four + 48)
        high[rows, :], low[rows, :] = split(jnp.concatenate(tiles, axis=0))


def rows_weight(pos, wave, c, anchor, images):
    width = pos.shape[2]
    n = lax.broadcasted_iota(jnp.int32, (8, 128), 0) - 1 - anchor
    nf = wide(n.astype(F32), width)
    odd = wide(n & 1, width) == 1
    flip = wide(n & 2, width) == 2
    y, cy, sy = row_of(pos, 1, c), row_of(wave, 2, c), row_of(wave, 3, c)
    base = jnp.where(odd, sy, cy)
    pattern = 0.25 + jnp.where(flip, -base, base)
    halves = []
    for h in range(2):
        gap = nf + 8.0 * h - y
        near = jnp.abs(gap - images[0]) < 2.0
        if len(images) > 1:
            near = jnp.logical_or(near, jnp.abs(gap - images[1]) < 2.0)
        halves.append(jnp.where(near, pattern, 0.0))
    return jnp.concatenate(halves, axis=0)


def nt_dot(a, b):
    return lax.dot_general(a, b, (((1,), (1,)), ((), ())), preferred_element_type=F32)


def stage_kernel(sizes, plan, last, copies, counts, together, *refs):
    _, vertices, extent = sizes
    n_cells, n_sums, n_copied = counts
    here, infos, table = refs[:3]
    refs = refs[3:]
    cells, refs = refs[:n_cells], refs[n_cells:]
    sums, refs = refs[:n_sums], refs[n_sums:]
    n_from = len({c[0] for c in copies})
    givers, refs = refs[:n_from], refs[n_from:]
    if last:
        own, down, up, far = refs[:4]
        refs = refs[4:]
    else:
        acc, refs = refs[0], refs[1:]
    takers, refs = refs[:n_copied], refs[n_copied:]
    pos, wave, force, planar, corner, patch = refs[:6]
    if last:
        acc = refs[6]
    moves = []
    for n, (giver, source, taker, target) in enumerate(copies):
        move = pltpu.make_async_copy(givers[giver].at[source], takers[taker].at[target], refs[-1].at[n])
        move.start()
        moves.append(move)
    if sums:
        total = sums[0][...]
        for more in sums[1:]:
            total = total + more[...]
        acc[...] = total
    else:
        acc[...] = jnp.zeros(acc.shape, F32)
    pos[...] = jnp.full(pos.shape, FAR, F32)
    rows = pos.shape[1] - 8
    for r in range(rows + 1):
        for d in range(3):
            corner[r, d] = 0
        for d in range(2):
            corner[r, 3 + d] = 0
    count = jnp.int32(0)
    at = 0
    for array, owner, images, offset in plan:
        block = cells[array]
        for r in range(cell_count(block)):
            target = infos[at, 0]
            wanted = target >= 0 if owner is None else target // sizes[0] == here[owner]
            row = jnp.where(wanted, count, rows)
            for a in range(3):
                pos[a, pl.ds(row, 1), :] = cell_row(block, offset, r, a)
            for d in range(3):
                corner[row, d] = lax.rem(infos[at, 1 + d], extent[d])
            corner[row, 3] = images[0]
            corner[row, 4] = images[-1]
            count = count + wanted.astype(jnp.int32)
            at += 1
    hide_rest(pos, vertices)
    fill_force(pos, table, wave, force, count)

    def weigh(c, b):
        fill_planar(pos, wave, c, planar.at[b, 0:144], planar.at[b, 144:288])
        images = (corner[c, 3].astype(F32), corner[c, 4].astype(F32))
        wy = rows_weight(pos, wave, c, corner[c, 1], images)
        lifted = []
        for a in range(3):
            f = row_of(force, a, c)
            lifted.append(jnp.concatenate([f, f], axis=0) * wy)
        high, low = split(jnp.concatenate(lifted, axis=0))
        both = nt_dot(planar[b], high)
        patch[b] = both[:144] + both[144:] + nt_dot(planar[b, 0:144], low)
        x0, z0 = corner[c, 0], corner[c, 2] + 2
        before = [acc[x0 + kx, pl.ds(z0, 12), :] for kx in range(12)]
        for kx in range(12):
            acc[x0 + kx, pl.ds(z0, 12), :] = before[kx] + patch[b, 12 * kx : 12 * kx + 12, :]

    def weigh_some(i, carry):
        for b in range(together):
            weigh(together * i + b, b)
        return carry

    lax.fori_loop(0, (count + together - 1) // together, weigh_some, 0)
    if last:
        for x in range(23):
            turned = jnp.transpose(acc[x, 8:136, :], (1, 0))
            if REACH - 1 <= x < REACH - 1 + own.shape[0]:
                own[x - REACH + 1] = turned
            if x < down.shape[0]:
                down[x] = turned
            if x >= 23 - up.shape[0]:
                up[x - 23 + up.shape[0]] = turned
        for n in range(3):
            outside = []
            for x in range(8 * n, 8 * n + 8):
                outside += [acc[x, 0:8, :], acc[x, 136:144, :]]
            far[n] = jnp.transpose(jnp.concatenate(outside, axis=0), (1, 0))
    for move in moves:
        move.wait()


def stage(sizes, plan, here, infos, table, cells, sums=(), last=False, givers=(), takers=(), copies=(), together=2):
    width = table.shape[1]
    rows = sum(cell_count(cells[p[0]]) for p in plan)
    counts = (len(cells), len(sums), len(takers))
    whole = pl.BlockSpec(memory_space=pl.ANY)
    fixed = pl.BlockSpec(memory_space=pltpu.HBM)
    return pl.pallas_call(
        functools.partial(stage_kernel, sizes, plan, last, copies, counts, together),
        out_shape=tuple(
            jax.ShapeDtypeStruct(shape, F32)
            for shape in ([(n, 48, 128) for n in (14, REACH + 1, REACH, 3)] if last else [(24, 152, 48)])
        )
        + tuple(takers),
        in_specs=[SMEM, SMEM, VMEM] + [VMEM] * (len(cells) + len(sums)) + [fixed] * len(givers),
        out_specs=(VMEM,) * (4 if last else 1) + (whole,) * len(takers),
        scratch_shapes=[
            pltpu.VMEM((3, rows + 8, width), F32),
            pltpu.VMEM((6, rows, width), F32),
            pltpu.VMEM((3, rows, width), F32),
            pltpu.VMEM((together, 288, width), jnp.bfloat16),
            pltpu.SMEM((rows + 8, 5), jnp.int32),
            pltpu.VMEM((together, 144, 48), F32),
        ]
        + ([pltpu.VMEM((24, 152, 48), F32)] if last else [])
        + ([pltpu.SemaphoreType.DMA((len(copies),))] if copies else []),
        compiler_params=params(),
        name="spread",
        cost_estimate=pl.CostEstimate(flops=int(4e9), bytes_accessed=4_000_000, transcendentals=0),
    )(here, infos, table, *cells, *sums, *givers)


def fold_kernel(own_in, down_in, up_in, far, own, down, up):
    lane = lax.broadcasted_iota(jnp.int32, (48, 128), 1)
    rim = jnp.logical_or(lane < 8, lane >= 120)
    for x in range(23):
        more = jnp.where(rim, pltpu.roll(far[x // 8], (120 - 16 * (x % 8)) % 128, 1), 0.0)
        if REACH - 1 <= x < REACH - 1 + own.shape[0]:
            own[x - REACH + 1] = own_in[x - REACH + 1] + more
        if x < down.shape[0]:
            down[x] = down_in[x] + more
        n = x - 23 + up.shape[0]
        if n >= 0:
            up[n] = up_in[n] + more


def sample_kernel(images, corner, pos, low_side, own, high_side, low_far, own_far, high_far, out, flow, far, wave, high, low):
    cells = out.shape[1]
    at = 0
    for part, part_far in ((low_side, low_far), (own, own_far), (high_side, high_far)):
        size = part.shape[0]
        flow[at : at + size] = part[...]
        far[at : at + size] = part_far[...]
        at += size
    fill_waves(pos, wave)
    lane = lax.broadcasted_iota(jnp.int32, (8, 128), 1)

    def sample(c, b):
        fill_planar(pos, wave, c, high.at[b], low.at[b])
        z0 = corner[c, 2] - REACH
        x0 = corner[c, 0]
        turn = (z0 + 12 * x0 + 128) & 127
        inside, chosen = [], []
        for t in range(2):
            origin = (lane - turn - 72 * t) & 127
            group = jnp.right_shift(origin * 43, 9)
            z = origin - 12 * group + z0
            inside.append(jnp.logical_and(z >= 0, z < 128))
            chosen.append([group == g for g in range(6)])
        front = lane < 72
        blocks = []
        for r in range(6):
            rows = slice(8 * r, 8 * r + 8)
            near = [flow[x0 + kx, rows, :] for kx in range(12)]
            there = [far[x0 + kx, rows, :] for kx in range(12)]
            turned = []
            for t in range(2):
                a, b_ = near[6 * t], there[6 * t]
                for g in range(1, 6):
                    a = jnp.where(chosen[t][g], near[6 * t + g], a)
                    b_ = jnp.where(chosen[t][g], there[6 * t + g], b_)
                turned.append(pltpu.roll(jnp.where(inside[t], a, b_), (128 - turn) & 127, 1))
            blocks.append(
                jnp.concatenate([jnp.where(front, turned[0], turned[1]), turned[1][:, 0:16]], axis=1)
            )
        qhigh, qlow = split(jnp.concatenate(blocks, axis=0))
        both = jnp.dot(jnp.concatenate([qhigh, qlow], axis=0), high[b], preferred_element_type=F32)
        mixed = both[:48] + both[48:] + jnp.dot(qhigh, low[b], preferred_element_type=F32)
        wy = rows_weight(pos, wave, c, corner[c, 1], images)
        for a in range(3):
            out[a, pl.ds(c, 1), :] = jnp.sum(mixed[16 * a : 16 * a + 16] * wy, axis=0, keepdims=True)

    def sample_some(i, carry):
        for b in range(4):
            sample(4 * i + b, b)
        return carry

    lax.fori_loop(0, cells // 4, sample_some, 0)


def sampled(cells, images, corner, pos, parts):
    width = pos.shape[2]
    return pl.pallas_call(
        functools.partial(sample_kernel, images),
        out_shape=jax.ShapeDtypeStruct((3, cells, width), F32),
        in_specs=[SMEM] + [VMEM] * 7,
        out_specs=VMEM,
        scratch_shapes=[
            pltpu.VMEM((24, 48, 128), F32),
            pltpu.VMEM((24, 48, 128), F32),
            pltpu.VMEM((6, cells, width), F32),
            pltpu.VMEM((4, 144, width), jnp.bfloat16),
            pltpu.VMEM((4, 144, width), jnp.bfloat16),
        ],
        compiler_params=params(),
        name="sample",
        cost_estimate=pl.CostEstimate(flops=int(2e9), bytes_accessed=4_000_000, transcendentals=0),
    )(corner, pos, *parts)


def extend_kernel(n_low, n_high, pops, x_low, x_high, y_low, y_high, out):
    nx, ny = pops.shape[:2]
    directions = pops.shape[2]
    for x in range(nx + 2):
        middle = x_low[0, :, 0:19, :] if x == 0 else (x_high[0, :, 0:19, :] if x == nx + 1 else pops[x - 1])
        block = jnp.concatenate([y_low[n_low, x : x + 1], middle, y_high[n_high, x : x + 1], y_low[n_low, x : x + 1], y_low[n_low, x : x + 1]], axis=0)
        out[:, x] = jnp.transpose(block, (1, 0, 2))


def collide_kernel(pops, own, from_low, from_high, *refs):
    post, force, edge = refs[-3:]
    planes = pops.shape[1]
    n_low, n_high = from_low.shape[0], from_high.shape[0]
    for e in range(planes):
        total = own[e]
        if e < n_low:
            total = total + from_low[e]
        if e >= planes - n_high:
            total = total + from_high[e - (planes - n_high)]
        force[e] = total
    lane = lax.broadcasted_iota(jnp.int32, (16, 128), 1)

    def plane(e, carry):
        p = [pops[i, e] for i in range(19)]
        f = [force[e, 16 * a : 16 * a + 16, :] for a in range(3)]
        rho = p[0]
        for i in range(1, 19):
            rho = rho + p[i]
        u = []
        for a in range(3):
            m = 0.5 * f[a]
            for i in range(1, 19):
                if DIRS[i][a] == 1:
                    m = m + p[i]
                elif DIRS[i][a] == -1:
                    m = m - p[i]
            u.append(m / rho)
        kinetic = u[0] * u[0] + u[1] * u[1] + u[2] * u[2]
        power = u[0] * f[0] + u[1] * f[1] + u[2] * f[2]
        level = 1.25 * rho * (1.0 - 1.5 * kinetic) - 1.125 * power
        bow, tilt = 5.625 * rho, 3.75 * rho
        new = [None] * 19
        new[0] = WEIGHTS[0] * level - 0.25 * p[0]
        for i in range(1, 19, 2):
            along = [a for a in range(3) if DIRS[i][a] != 0]
            cu, cf = None, None
            for a in along:
                tu, tf = u[a], f[a]
                if DIRS[i][a] < 0:
                    tu, tf = -tu, -tf
                cu = tu if cu is None else cu + tu
                cf = tf if cf is None else cf + tf
            even = WEIGHTS[i] * (level + cu * (bow * cu + 3.375 * cf))
            odd = WEIGHTS[i] * (tilt * cu + 1.125 * cf)
            new[i] = even + odd - 0.25 * p[i]
            new[i + 1] = even - odd - 0.25 * p[i + 1]
        for i in range(19):
            post[i, e] = new[i]
        for j in range(5):
            edge[j, e] = jnp.where(
                lane == 0, pltpu.roll(new[RISING[j]], 1, 1), pltpu.roll(new[FALLING[j]], 127, 1)
            )
        return carry

    lax.fori_loop(0, planes, plane, 0)


def arriving(post, edge, x, ny):
    lane = lax.broadcasted_iota(jnp.int32, (ny, 128), 1)
    found = []
    for i in range(19):
        cx, cy, cz = DIRS[i]
        value = post[i, x + 1 - cx, 1 - cy : 1 - cy + ny, :]
        if cz == 1:
            side = edge[RISING.index(i), x + 1 - cx, 1 - cy : 1 - cy + ny, :]
            value = jnp.where(lane == 0, side, pltpu.roll(value, 1, 1))
        elif cz == -1:
            side = edge[FALLING.index(i), x + 1 - cx, 1 - cy : 1 - cy + ny, :]
            value = jnp.where(lane == 127, side, pltpu.roll(value, 127, 1))
        found.append(value)
    return found


def flow_kernel(ny, post, edge, force, own, up, down, velocity):
    nx = own.shape[0]
    velocity[...] = jnp.zeros(velocity.shape, F32)

    def plane(x, carry):
        n = arriving(post, edge, x, ny)
        rho = n[0]
        for i in range(1, 19):
            rho = rho + n[i]
        for a in range(3):
            m = 0.5 * force[x + 1, 16 * a + 1 : 16 * a + 1 + ny, :]
            for i in range(1, 19):
                if DIRS[i][a] == 1:
                    m = m + n[i]
                elif DIRS[i][a] == -1:
                    m = m - n[i]
            velocity[x, 16 * a + 1 : 16 * a + 1 + ny, :] = m / rho
        return carry

    lax.fori_loop(0, nx, plane, 0)
    for x in range(nx):
        own[x] = pltpu.roll(velocity[x], 12 * (x + REACH) % 128, 1)
        if x >= nx - REACH:
            up[x - nx + REACH] = pltpu.roll(velocity[x], 12 * (x + REACH - nx) % 128, 1)
        if x < REACH - 1:
            down[x] = pltpu.roll(velocity[x], 12 * (x + REACH + nx) % 128, 1)


def renew_kernel(post, edge, after, pops):
    def plane(x, carry):
        pops[x] = jnp.transpose(jnp.stack(arriving(post, edge, x, pops.shape[1])), (1, 0, 2))
        return carry

    lax.fori_loop(0, pops.shape[0], plane, 0)


def shifted(x, axis, distance):
    count = lax.axis_size(axis)
    return lax.ppermute(x, axis, [(i, (i + distance) % count) for i in range(count)])


def on_device(populations, membrane, anchors, targets):
    extent = populations.shape[1:]
    capacity, _, vertices = membrane.shape
    slabs, crosses, subs = (lax.axis_size(a) for a in ("slab", "cross", "sub"))
    assert subs == 2 and extent == (12, 12, 128) and capacity % 8 == 0
    width = WIDTH
    assert vertices + 4 <= width < vertices + 128
    place = [lax.axis_index(a) for a in ("slab", "cross", "sub")]
    table = chain_table(vertices, width)

    notes = jnp.concatenate([targets[:, None], anchors], axis=1)
    raw = jnp.concatenate(
        [
            jnp.transpose(membrane, (1, 0, 2)),
            jnp.broadcast_to(notes.astype(F32)[None], (3, capacity, 4)),
            jnp.full((3, capacity, width - vertices - 4), FAR, F32),
        ],
        axis=2,
    )
    if crosses == 2:
        beside = [(1, (extent[1], -extent[1]))]
    else:
        beside = [(1, (-extent[1],)), (-1, (extent[1],))]
    owners = [(place[0] * crosses + (place[1] + crosses - d) % crosses) * subs + place[2] for d in [0] + [d for d, _ in beside]]
    here = jnp.stack(place + owners).astype(jnp.int32)
    guests = [shifted(raw, "cross", d) for d, _ in beside]
    groups = 1 + len(beside)
    nx, ny = extent[:2]
    planes = nx + 2
    pops = jnp.transpose(populations, (1, 2, 0, 3))
    sides = jnp.concatenate([pops[nx - 1 :], pops[:1]])
    held = 3 * (width // 128) * MIG
    message = jax.ShapeDtypeStruct((groups * held + 24 * ny + 8, 128), F32)
    theirs = [g[0, :, vertices : vertices + 4].astype(jnp.int32) for g in guests]
    up, down = pl.pallas_call(
        functools.partial(pack_kernel, capacity, slabs, crosses * subs, groups, 0),
        out_shape=(message, message),
        in_specs=[SMEM, SMEM, VMEM, VMEM],
        out_specs=(VMEM, VMEM),
        compiler_params=params(),
        name="pack",
    )(here, notes, raw, sides)
    up, down = pl.pallas_call(
        functools.partial(pack_kernel, capacity, slabs, crosses * subs, groups, 1),
        out_shape=(message, message),
        in_specs=[SMEM, SMEM] + [VMEM] * (groups + 1),
        out_specs=(VMEM, VMEM),
        compiler_params=params(),
        name="pack",
    )(here, jnp.concatenate(theirs), *guests, up, down)
    home = jnp.concatenate([raw[0, :, vertices : vertices + 4].astype(jnp.int32)] + theirs)
    sizes = (capacity, vertices, extent)
    below, above = shifted(up, "slab", 1), shifted(down, "slab", -1)
    images = [(0,)] + [image for _, image in beside]

    row = jax.ShapeDtypeStruct((nx,) + pops.shape[2:], F32)
    sum_1, first, last = stage(
        sizes,
        [(g, 3 + g, images[g], 0) for g in range(groups)],
        here,
        home,
        table,
        [raw] + guests,
        givers=(pops,),
        takers=(row, row),
        copies=((0, (pl.ds(0, nx), 0), 0, pl.ds(0, nx)), (0, (pl.ds(0, nx), ny - 1), 1, pl.ds(0, nx))),
        together=4,
    )
    x_low = below[groups * held : groups * held + 24 * ny].reshape(1, ny, 24, 128)
    x_high = above[groups * held : groups * held + 24 * ny].reshape(1, ny, 24, 128)
    first = jnp.concatenate([x_low[:, 0, :19], first, x_high[:, 0, :19]])
    last = jnp.concatenate([x_low[:, -1, :19], last, x_high[:, -1, :19]])
    y_low, y_high = (shifted(last, "cross", 1)[None], 0), (shifted(first, "cross", -1)[None], 0)
    lane = vertices - (width - 128)
    starts = [g * held + (width // 128 - 1) * MIG for g in range(groups)]
    notes_in = [m[s : s + MIG, lane : lane + 4].astype(jnp.int32) for s in starts for m in (below, above)]
    own, down_force, up_force, far = stage(
        sizes,
        [(n, None, images[g], g * held) for g in range(groups) for n in (0, 1)],
        here,
        jnp.concatenate(notes_in),
        table,
        [below, above],
        sums=(sum_1,),
        last=True,
    )
    cells = []
    for block in [raw] + guests:
        cells += [block, below, above]
    offsets = tuple(g * held for g in range(groups) for _ in range(3))
    extended = pl.pallas_call(
        functools.partial(extend_kernel, y_low[1], y_high[1]),
        out_shape=jax.ShapeDtypeStruct((19, planes, 16, 128), F32),
        in_specs=[VMEM] * 5,
        out_specs=VMEM,
        compiler_params=params(),
        name="extend",
    )(pops, x_low, x_high, y_low[0], y_high[0])

    own, down_force, up_force = pl.pallas_call(
        fold_kernel,
        out_shape=tuple(jax.ShapeDtypeStruct((n, 48, 128), F32) for n in (planes, REACH + 1, REACH)),
        in_specs=[VMEM] * 4,
        out_specs=(VMEM,) * 3,
        compiler_params=params(),
        name="fold",
    )(own, down_force, up_force, shifted(far, "sub", 1))
    from_high = shifted(down_force, "slab", -1)
    from_low = shifted(up_force, "slab", 1)

    placed = pl.pallas_call(
        functools.partial(assemble_kernel, sizes, groups, offsets),
        out_shape=(jax.ShapeDtypeStruct((3, capacity + 8, width), F32),) * groups
        + (jax.ShapeDtypeStruct((capacity + 8, 3), jnp.int32),) * groups,
        in_specs=[SMEM, SMEM] + [VMEM] * len(cells) + [pl.BlockSpec(memory_space=pl.ANY)],
        out_specs=(VMEM,) * groups + (SMEM,) * groups,
        compiler_params=params(),
        name="assemble",
    )(here, jnp.concatenate([home] + notes_in), *cells, own)
    positions, corners = placed[:groups], placed[groups:]
    post, force, edge = pl.pallas_call(
        collide_kernel,
        out_shape=(
            jax.ShapeDtypeStruct((19, planes, 16, 128), F32),
            jax.ShapeDtypeStruct((planes, 48, 128), F32),
            jax.ShapeDtypeStruct((5, planes, 16, 128), F32),
        ),
        in_specs=[VMEM] * 4 + [pl.BlockSpec(memory_space=pl.ANY)] * groups,
        out_specs=(VMEM,) * 3,
        compiler_params=params(),
        name="collide",
    )(extended, own, from_low, from_high, *positions)
    edge = shifted(edge, "sub", 1)
    velocity, up_flow, down_flow = pl.pallas_call(
        functools.partial(flow_kernel, ny),
        out_shape=tuple(jax.ShapeDtypeStruct((n, 48, 128), F32) for n in (nx, REACH, REACH - 1)),
        in_specs=[VMEM] * 3,
        out_specs=(VMEM,) * 3,
        scratch_shapes=[pltpu.VMEM((nx, 48, 128), F32)],
        compiler_params=params(),
        name="flow",
    )(post, edge, force)
    renewed = pl.pallas_call(
        renew_kernel,
        out_shape=jax.ShapeDtypeStruct((nx, ny, 19, 128), F32),
        in_specs=[VMEM] * 2 + [pl.BlockSpec(memory_space=pl.ANY)],
        out_specs=VMEM,
        compiler_params=params(),
        name="renew",
    )(post, edge, velocity)

    low_side = shifted(up_flow, "slab", 1)
    high_side = shifted(down_flow, "slab", -1)
    low_side, high_side, renewed = lax.optimization_barrier((low_side, high_side, renewed))
    parts = (low_side, velocity, high_side)
    parts = parts + tuple(shifted(part, "sub", 1) for part in parts)
    shares = [
        shifted(sampled(capacity, image, corner, pos, parts), "cross", -d)
        for (d, image), corner, pos in zip(beside, corners[1:], positions[1:])
    ]
    total = sampled(capacity, (0,), corners[0], positions[0], parts)
    for share in shares:
        total = total + share
    return (
        jnp.transpose(renewed, (2, 0, 1, 3)),
        jnp.transpose(total[:, :, :vertices], (1, 0, 2)),
    )


def solution(mesh):
    placed = (
        P(None, ("parts", "slab"), "cross", "sub"),
        P(("parts", "slab", "cross", "sub"), None, None),
        P(("parts", "slab", "cross", "sub"), None),
        P(("parts", "slab", "cross", "sub")),
    )
    return jax.shard_map(
        on_device,
        mesh=mesh,
        in_specs=placed,
        out_specs=(
            P(None, ("parts", "slab"), "cross", "sub"),
            P(("parts", "slab", "cross", "sub"), None, None),
        ),
        check_vma=False,
    )
```

```python
import functools
import math

import jax
import jax.numpy as jnp
import numpy as np
from jax import lax
from jax.experimental import pallas as pl
from jax.experimental.pallas import tpu as pltpu
from jax.sharding import PartitionSpec as P

REACH = 6
MIG = 4
STRIDES = (21, 34, 55)
DIRS = (
    (0, 0, 0),
    (1, 0, 0), (-1, 0, 0), (0, 1, 0), (0, -1, 0), (0, 0, 1), (0, 0, -1),
    (1, 1, 0), (-1, -1, 0), (1, -1, 0), (-1, 1, 0),
    (1, 0, 1), (-1, 0, -1), (1, 0, -1), (-1, 0, 1),
    (0, 1, 1), (0, -1, -1), (0, 1, -1), (0, -1, 1),
)
RISING = (5, 11, 14, 15, 18)
FALLING = (6, 12, 13, 16, 17)
WEIGHTS = (1.0 / 3.0,) + (1.0 / 18.0,) * 6 + (1.0 / 36.0,) * 12
FAR = 100.0
F32 = jnp.float32
WIDTH = 768
VMEM = pl.BlockSpec(memory_space=pltpu.VMEM)
SMEM = pl.BlockSpec(memory_space=pltpu.SMEM)


def params(limit=14):
    return pltpu.CompilerParams(vmem_limit_bytes=limit * 1024 * 1024)


def chain_table(vertices, width):
    v = np.arange(vertices)
    h = 1.0 - (2.0 * v + 1.0) / vertices
    t = 2.0 * math.pi / 2584.0 * (v * 1597 % 2584)
    across = np.sqrt(1.0 - h * h)
    rest = 3.0 * np.stack([across * np.cos(t), across * np.sin(t), h])
    table = np.zeros((16, width))
    for n, s in enumerate(STRIDES):
        gap = rest[:, s:] - rest[:, :-s]
        table[5 * n : 5 * n + 3, : vertices - s] = gap
        table[5 * n + 3, : vertices - s] = 0.05 / np.sum(gap * gap, axis=0)
        table[5 * n + 4, : vertices - s] = 1.0
    return jnp.asarray(table, F32)


def pack_kernel(capacity, slabs, plane, groups, begun, here, infos, *refs):
    tiles = WIDTH // 128
    held = 3 * tiles * MIG
    over = lax.rem(here[0] + 1, slabs)
    under = lax.rem(here[0] + slabs - 1, slabs)
    if begun:
        cells, (up_begun, down_begun, up, down) = refs[: groups - 1], refs[groups - 1 :]
        up[...] = up_begun[...]
        down[...] = down_begun[...]
    else:
        cells, (sides, up, down) = refs[:1], refs[1:]
        up[0 : groups * held, :] = jnp.full((groups * held, 128), -1.0, F32)
        down[0 : groups * held, :] = jnp.full((groups * held, 128), -1.0, F32)
        ny, directions = sides.shape[1:3]
        for n, message in enumerate((up, down)):
            for y in range(ny):
                first = groups * held + 24 * y
                message[first : first + directions, :] = sides[n, y]
    for n, block in enumerate(cells):
        g = n + begun
        n_up, n_down = jnp.int32(0), jnp.int32(0)
        for c in range(capacity):
            owner = infos[n * capacity + c, 0] // capacity
            peer = owner // plane
            leaving = owner != here[3 + g]
            rises = jnp.logical_and(leaving, peer == over)
            falls = jnp.logical_and(leaving, peer == under)
            to_up = g * held + jnp.minimum(n_up, MIG - 1)
            to_down = g * held + jnp.minimum(n_down, MIG - 1)

            def put(message, start):
                for a in range(3):
                    for t in range(tiles):
                        row = block[a, c : c + 1, 128 * t : 128 * t + 128]
                        message[pl.ds(start + (a * tiles + t) * MIG, 1), :] = row

            @pl.when(rises)
            def _():
                put(up, to_up)

            @pl.when(falls)
            def _():
                put(down, to_down)

            n_up = n_up + rises.astype(jnp.int32)
            n_down = n_down + falls.astype(jnp.int32)


def cell_row(block, offset, r, a):
    if len(block.shape) == 3:
        return block[a, r : r + 1, :]
    tiles = WIDTH // 128
    first = offset + a * tiles * MIG + r
    return jnp.concatenate([block[first + t * MIG : first + t * MIG + 1, :] for t in range(tiles)], axis=1)


def cell_count(block):
    return block.shape[1] if len(block.shape) == 3 else MIG


def hide_rest(pos, vertices):
    width = pos.shape[2]
    lane = lax.broadcasted_iota(jnp.int32, (pos.shape[1], 128), 1) + (width - 128)
    for a in range(3):
        pos[a, :, width - 128 :] = jnp.where(lane < vertices, pos[a, :, width - 128 :], FAR)


def assemble(capacity, vertices, extent, owner, sources, pos, corner):
    for infos, first, block, offset, migrated in sources:
        for r in range(cell_count(block)):
            target = infos[first + r, 0]
            wanted = target >= 0 if migrated else target // capacity == owner
            slot = jnp.where(wanted, lax.rem(target, capacity), capacity)
            for a in range(3):
                pos[a, pl.ds(slot, 1), :] = cell_row(block, offset, r, a)
            for d in range(3):
                corner[slot, d] = lax.rem(infos[first + r, 1 + d], extent[d])
    hide_rest(pos, vertices)


def assemble_kernel(sizes, groups, offsets, *refs):
    capacity, vertices, extent = sizes
    here, home, came = refs[:3]
    refs = refs[1:]
    cells = refs[2 : 2 + 3 * groups]
    positions, corners = refs[3 + 3 * groups : 3 + 4 * groups], refs[3 + 4 * groups :]
    for g in range(groups):
        start = g * 2 * MIG
        sources = [
            (home, g * capacity, cells[3 * g], 0, False),
            (came, start, cells[3 * g + 1], offsets[3 * g + 1], True),
            (came, start + MIG, cells[3 * g + 2], offsets[3 * g + 2], True),
        ]
        assemble(capacity, vertices, extent, here[3 + g], sources, positions[g], corners[g])


def wide(tile, width):
    return jnp.concatenate([tile] * (width // 128), axis=1)


def waves(x):
    h = (x - 4.0 * jnp.floor(0.25 * x + 0.5)) * (math.pi / 4.0)
    q = h * h
    sine = h * (1.0 + q * (-1 / 6 + q * (1 / 120 + q * (-1 / 5040 + q * (1 / 362880 - q * (1 / 39916800))))))
    cosine = 1.0 + q * (
        -1 / 2 + q * (1 / 24 + q * (-1 / 720 + q * (1 / 40320 + q * (-1 / 3628800 + q * (1 / 479001600)))))
    )
    return 0.25 - 0.5 * sine * sine, 0.5 * sine * cosine


def fill_waves(pos, wave):
    cells = wave.shape[1]
    for a in range(3):
        wave[2 * a], wave[2 * a + 1] = waves(pos[a, 0:cells, :])


def fill_force(pos, table, wave, force, count):
    cells, width = force.shape[1:]

    def some(h):
        rows = slice(8 * h, 8 * h + 8)
        for a in range(3):
            wave[2 * a, rows, :], wave[2 * a + 1, rows, :] = waves(pos[a, rows, :])
        x = [pos[a, rows, :] for a in range(3)]
        lap = [jnp.zeros((8, width), F32) for _ in range(3)]
        pulls = []
        for n, s in enumerate(STRIDES):
            gap = [table[5 * n + a : 5 * n + a + 1, :] for a in range(3)]
            scale = table[5 * n + 3 : 5 * n + 4, :]
            mask = table[5 * n + 4 : 5 * n + 5, :]
            d = [pltpu.roll(x[a], width - s, 1) - x[a] for a in range(3)]
            square = d[0] * d[0] + d[1] * d[1] + d[2] * d[2]
            strain = square * scale - 0.05 * mask
            pulls.append([strain * d[a] for a in range(3)])
            for a in range(3):
                bend = mask * d[a] - gap[a]
                lap[a] = lap[a] + bend - pltpu.roll(bend, s, 1)
        for a in range(3):
            total = jnp.zeros((8, width), F32)
            for n, s in enumerate(STRIDES):
                mask = table[5 * n + 4 : 5 * n + 5, :]
                t = pulls[n][a] - 0.002 * (mask * (pltpu.roll(lap[a], width - s, 1) - lap[a]))
                total = total + t - pltpu.roll(t, s, 1)
            force[a, rows, :] = total

    for h in range(cells // 8):
        pl.when(8 * h < count)(functools.partial(some, h))


def split(x):
    high = x.astype(jnp.bfloat16)
    return high, (x - high.astype(F32)).astype(jnp.bfloat16)


def row_of(ref, i, c):
    return jnp.broadcast_to(ref[i, pl.ds(c, 1), :], (8, ref.shape[2]))


def fill_planar(pos, wave, c, high, low):
    width = pos.shape[2]
    row = lax.broadcasted_iota(jnp.int32, (8, 128), 0)
    rowf = (row - REACH).astype(F32)
    joint = wide(jnp.where(row < 4, rowf + 8.0, rowf - 4.0), width)
    rowf = wide(rowf, width)
    upper = wide(row, width) < 4
    odd = wide((row & 1), width) == 1
    flip = wide((row & 2), width) == 0
    z, cz, sz = row_of(pos, 2, c), row_of(wave, 4, c), row_of(wave, 5, c)
    base = jnp.where(odd, sz, cz)
    pattern = 0.25 + jnp.where(flip, -base, base)
    wz = [
        jnp.where(jnp.abs(rows - z) < 2.0, pattern, 0.0) for rows in (rowf, joint, rowf + 4.0)
    ]
    x, cx, sx = row_of(pos, 0, c), row_of(wave, 0, c), row_of(wave, 1, c)
    quarter = (0.25 - cx, 0.25 - sx, 0.25 + cx, 0.25 + sx)
    for four in range(3):
        tiles = []
        for kx in (4 * four, 4 * four + 2):
            wx = [
                jnp.where(jnp.abs(x - float(k - REACH)) < 2.0, quarter[k % 4], 0.0) for k in (kx, kx + 1)
            ]
            tiles += [wx[0] * wz[0], jnp.where(upper, wx[0], wx[1]) * wz[1], wx[1] * wz[2]]
        rows = slice(48 * four, 48 * four + 48)
        high[rows, :], low[rows, :] = split(jnp.concatenate(tiles, axis=0))


def rows_weight(pos, wave, c, anchor, images):
    width = pos.shape[2]
    n = lax.broadcasted_iota(jnp.int32, (8, 128), 0) - 1 - anchor
    nf = wide(n.astype(F32), width)
    odd = wide(n & 1, width) == 1
    flip = wide(n & 2, width) == 2
    y, cy, sy = row_of(pos, 1, c), row_of(wave, 2, c), row_of(wave, 3, c)
    base = jnp.where(odd, sy, cy)
    pattern = 0.25 + jnp.where(flip, -base, base)
    halves = []
    for h in range(2):
        gap = nf + 8.0 * h - y
        near = jnp.abs(gap - images[0]) < 2.0
        if len(images) > 1:
            near = jnp.logical_or(near, jnp.abs(gap - images[1]) < 2.0)
        halves.append(jnp.where(near, pattern, 0.0))
    return jnp.concatenate(halves, axis=0)


def nt_dot(a, b):
    return lax.dot_general(a, b, (((1,), (1,)), ((), ())), preferred_element_type=F32)


def stage_kernel(sizes, plan, last, copies, counts, together, *refs):
    _, vertices, extent = sizes
    n_cells, n_sums, n_copied = counts
    here, infos, table = refs[:3]
    refs = refs[3:]
    cells, refs = refs[:n_cells], refs[n_cells:]
    sums, refs = refs[:n_sums], refs[n_sums:]
    n_from = len({c[0] for c in copies})
    givers, refs = refs[:n_from], refs[n_from:]
    if last:
        own, down, up, far = refs[:4]
        refs = refs[4:]
    else:
        acc, refs = refs[0], refs[1:]
    takers, refs = refs[:n_copied], refs[n_copied:]
    pos, wave, force, planar, corner, patch = refs[:6]
    if last:
        acc = refs[6]
    moves = []
    for n, (giver, source, taker, target) in enumerate(copies):
        move = pltpu.make_async_copy(givers[giver].at[source], takers[taker].at[target], refs[-1].at[n])
        move.start()
        moves.append(move)
    if sums:
        total = sums[0][...]
        for more in sums[1:]:
            total = total + more[...]
        acc[...] = total
    else:
        acc[...] = jnp.zeros(acc.shape, F32)
    pos[...] = jnp.full(pos.shape, FAR, F32)
    rows = pos.shape[1] - 8
    for r in range(rows + 1):
        for d in range(3):
            corner[r, d] = 0
        for d in range(2):
            corner[r, 3 + d] = 0
    count = jnp.int32(0)
    at = 0
    for array, owner, images, offset in plan:
        block = cells[array]
        for r in range(cell_count(block)):
            target = infos[at, 0]
            wanted = target >= 0 if owner is None else target // sizes[0] == here[owner]
            row = jnp.where(wanted, count, rows)
            for a in range(3):
                pos[a, pl.ds(row, 1), :] = cell_row(block, offset, r, a)
            for d in range(3):
                corner[row, d] = lax.rem(infos[at, 1 + d], extent[d])
            corner[row, 3] = images[0]
            corner[row, 4] = images[-1]
            count = count + wanted.astype(jnp.int32)
            at += 1
    hide_rest(pos, vertices)
    fill_force(pos, table, wave, force, count)

    def weigh(c, b):
        fill_planar(pos, wave, c, planar.at[b, 0:144], planar.at[b, 144:288])
        images = (corner[c, 3].astype(F32), corner[c, 4].astype(F32))
        wy = rows_weight(pos, wave, c, corner[c, 1], images)
        lifted = []
        for a in range(3):
            f = row_of(force, a, c)
            lifted.append(jnp.concatenate([f, f], axis=0) * wy)
        high, low = split(jnp.concatenate(lifted, axis=0))
        both = nt_dot(planar[b], high)
        patch[b] = both[:144] + both[144:] + nt_dot(planar[b, 0:144], low)
        x0, z0 = corner[c, 0], corner[c, 2] + 2
        before = [acc[x0 + kx, pl.ds(z0, 12), :] for kx in range(12)]
        for kx in range(12):
            acc[x0 + kx, pl.ds(z0, 12), :] = before[kx] + patch[b, 12 * kx : 12 * kx + 12, :]

    def weigh_some(i, carry):
        for b in range(together):
            weigh(together * i + b, b)
        return carry

    lax.fori_loop(0, (count + together - 1) // together, weigh_some, 0)
    if last:
        for x in range(23):
            turned = jnp.transpose(acc[x, 8:136, :], (1, 0))
            if REACH - 1 <= x < REACH - 1 + own.shape[0]:
                own[x - REACH + 1] = turned
            if x < down.shape[0]:
                down[x] = turned
            if x >= 23 - up.shape[0]:
                up[x - 23 + up.shape[0]] = turned
        for n in range(3):
            outside = []
            for x in range(8 * n, 8 * n + 8):
                outside += [acc[x, 0:8, :], acc[x, 136:144, :]]
            far[n] = jnp.transpose(jnp.concatenate(outside, axis=0), (1, 0))
    for move in moves:
        move.wait()


def stage(sizes, plan, here, infos, table, cells, sums=(), last=False, givers=(), takers=(), copies=(), together=2):
    width = table.shape[1]
    rows = sum(cell_count(cells[p[0]]) for p in plan)
    counts = (len(cells), len(sums), len(takers))
    whole = pl.BlockSpec(memory_space=pl.ANY)
    fixed = pl.BlockSpec(memory_space=pltpu.HBM)
    return pl.pallas_call(
        functools.partial(stage_kernel, sizes, plan, last, copies, counts, together),
        out_shape=tuple(
            jax.ShapeDtypeStruct(shape, F32)
            for shape in ([(n, 48, 128) for n in (14, REACH + 1, REACH, 3)] if last else [(24, 152, 48)])
        )
        + tuple(takers),
        in_specs=[SMEM, SMEM, VMEM] + [VMEM] * (len(cells) + len(sums)) + [fixed] * len(givers),
        out_specs=(VMEM,) * (4 if last else 1) + (whole,) * len(takers),
        scratch_shapes=[
            pltpu.VMEM((3, rows + 8, width), F32),
            pltpu.VMEM((6, rows, width), F32),
            pltpu.VMEM((3, rows, width), F32),
            pltpu.VMEM((together, 288, width), jnp.bfloat16),
            pltpu.SMEM((rows + 8, 5), jnp.int32),
            pltpu.VMEM((together, 144, 48), F32),
        ]
        + ([pltpu.VMEM((24, 152, 48), F32)] if last else [])
        + ([pltpu.SemaphoreType.DMA((len(copies),))] if copies else []),
        compiler_params=params(),
        name="spread",
        cost_estimate=pl.CostEstimate(flops=int(4e9), bytes_accessed=4_000_000, transcendentals=0),
    )(here, infos, table, *cells, *sums, *givers)


def fold_kernel(own_in, down_in, up_in, far, own, down, up):
    lane = lax.broadcasted_iota(jnp.int32, (48, 128), 1)
    rim = jnp.logical_or(lane < 8, lane >= 120)
    for x in range(23):
        more = jnp.where(rim, pltpu.roll(far[x // 8], (120 - 16 * (x % 8)) % 128, 1), 0.0)
        if REACH - 1 <= x < REACH - 1 + own.shape[0]:
            own[x - REACH + 1] = own_in[x - REACH + 1] + more
        if x < down.shape[0]:
            down[x] = down_in[x] + more
        n = x - 23 + up.shape[0]
        if n >= 0:
            up[n] = up_in[n] + more


def sample_kernel(images, corner, pos, low_side, own, high_side, low_far, own_far, high_far, out, flow, far, wave, high, low):
    cells = out.shape[1]
    at = 0
    for part, part_far in ((low_side, low_far), (own, own_far), (high_side, high_far)):
        size = part.shape[0]
        flow[at : at + size] = part[...]
        far[at : at + size] = part_far[...]
        at += size
    fill_waves(pos, wave)
    lane = lax.broadcasted_iota(jnp.int32, (8, 128), 1)

    def sample(c, b):
        fill_planar(pos, wave, c, high.at[b], low.at[b])
        z0 = corner[c, 2] - REACH
        x0 = corner[c, 0]
        turn = (z0 + 12 * x0 + 128) & 127
        inside, chosen = [], []
        for t in range(2):
            origin = (lane - turn - 72 * t) & 127
            group = jnp.right_shift(origin * 43, 9)
            z = origin - 12 * group + z0
            inside.append(jnp.logical_and(z >= 0, z < 128))
            chosen.append([group == g for g in range(6)])
        front = lane < 72
        blocks = []
        for r in range(6):
            rows = slice(8 * r, 8 * r + 8)
            near = [flow[x0 + kx, rows, :] for kx in range(12)]
            there = [far[x0 + kx, rows, :] for kx in range(12)]
            turned = []
            for t in range(2):
                a, b_ = near[6 * t], there[6 * t]
                for g in range(1, 6):
                    a = jnp.where(chosen[t][g], near[6 * t + g], a)
                    b_ = jnp.where(chosen[t][g], there[6 * t + g], b_)
                turned.append(pltpu.roll(jnp.where(inside[t], a, b_), (128 - turn) & 127, 1))
            blocks.append(
                jnp.concatenate([jnp.where(front, turned[0], turned[1]), turned[1][:, 0:16]], axis=1)
            )
        qhigh, qlow = split(jnp.concatenate(blocks, axis=0))
        both = jnp.dot(jnp.concatenate([qhigh, qlow], axis=0), high[b], preferred_element_type=F32)
        mixed = both[:48] + both[48:] + jnp.dot(qhigh, low[b], preferred_element_type=F32)
        wy = rows_weight(pos, wave, c, corner[c, 1], images)
        for a in range(3):
            out[a, pl.ds(c, 1), :] = jnp.sum(mixed[16 * a : 16 * a + 16] * wy, axis=0, keepdims=True)

    def sample_some(i, carry):
        for b in range(4):
            sample(4 * i + b, b)
        return carry

    lax.fori_loop(0, cells // 4, sample_some, 0)


def sampled(cells, images, corner, pos, parts):
    width = pos.shape[2]
    return pl.pallas_call(
        functools.partial(sample_kernel, images),
        out_shape=jax.ShapeDtypeStruct((3, cells, width), F32),
        in_specs=[SMEM] + [VMEM] * 7,
        out_specs=VMEM,
        scratch_shapes=[
            pltpu.VMEM((24, 48, 128), F32),
            pltpu.VMEM((24, 48, 128), F32),
            pltpu.VMEM((6, cells, width), F32),
            pltpu.VMEM((4, 144, width), jnp.bfloat16),
            pltpu.VMEM((4, 144, width), jnp.bfloat16),
        ],
        compiler_params=params(),
        name="sample",
        cost_estimate=pl.CostEstimate(flops=int(2e9), bytes_accessed=4_000_000, transcendentals=0),
    )(corner, pos, *parts)


def extend_kernel(n_low, n_high, pops, x_low, x_high, y_low, y_high, out):
    nx, ny = pops.shape[:2]
    directions = pops.shape[2]
    for x in range(nx + 2):
        middle = x_low[0, :, 0:19, :] if x == 0 else (x_high[0, :, 0:19, :] if x == nx + 1 else pops[x - 1])
        block = jnp.concatenate([y_low[n_low, x : x + 1], middle, y_high[n_high, x : x + 1], y_low[n_low, x : x + 1], y_low[n_low, x : x + 1]], axis=0)
        out[:, x] = jnp.transpose(block, (1, 0, 2))


def collide_kernel(pops, own, from_low, from_high, *refs):
    post, force, edge = refs[-3:]
    planes = pops.shape[1]
    n_low, n_high = from_low.shape[0], from_high.shape[0]
    for e in range(planes):
        total = own[e]
        if e < n_low:
            total = total + from_low[e]
        if e >= planes - n_high:
            total = total + from_high[e - (planes - n_high)]
        force[e] = total
    lane = lax.broadcasted_iota(jnp.int32, (16, 128), 1)

    def plane(e, carry):
        p = [pops[i, e] for i in range(19)]
        f = [force[e, 16 * a : 16 * a + 16, :] for a in range(3)]
        rho = p[0]
        for i in range(1, 19):
            rho = rho + p[i]
        u = []
        for a in range(3):
            m = 0.5 * f[a]
            for i in range(1, 19):
                if DIRS[i][a] == 1:
                    m = m + p[i]
                elif DIRS[i][a] == -1:
                    m = m - p[i]
            u.append(m / rho)
        kinetic = u[0] * u[0] + u[1] * u[1] + u[2] * u[2]
        power = u[0] * f[0] + u[1] * f[1] + u[2] * f[2]
        level = 1.25 * rho * (1.0 - 1.5 * kinetic) - 1.125 * power
        bow, tilt = 5.625 * rho, 3.75 * rho
        new = [None] * 19
        new[0] = WEIGHTS[0] * level - 0.25 * p[0]
        for i in range(1, 19, 2):
            along = [a for a in range(3) if DIRS[i][a] != 0]
            cu, cf = None, None
            for a in along:
                tu, tf = u[a], f[a]
                if DIRS[i][a] < 0:
                    tu, tf = -tu, -tf
                cu = tu if cu is None else cu + tu
                cf = tf if cf is None else cf + tf
            even = WEIGHTS[i] * (level + cu * (bow * cu + 3.375 * cf))
            odd = WEIGHTS[i] * (tilt * cu + 1.125 * cf)
            new[i] = even + odd - 0.25 * p[i]
            new[i + 1] = even - odd - 0.25 * p[i + 1]
        for i in range(19):
            post[i, e] = new[i]
        for j in range(5):
            edge[j, e] = jnp.where(
                lane == 0, pltpu.roll(new[RISING[j]], 1, 1), pltpu.roll(new[FALLING[j]], 127, 1)
            )
        return carry

    lax.fori_loop(0, planes, plane, 0)


def arriving(post, edge, x, ny):
    lane = lax.broadcasted_iota(jnp.int32, (ny, 128), 1)
    found = []
    for i in range(19):
        cx, cy, cz = DIRS[i]
        value = post[i, x + 1 - cx, 1 - cy : 1 - cy + ny, :]
        if cz == 1:
            side = edge[RISING.index(i), x + 1 - cx, 1 - cy : 1 - cy + ny, :]
            value = jnp.where(lane == 0, side, pltpu.roll(value, 1, 1))
        elif cz == -1:
            side = edge[FALLING.index(i), x + 1 - cx, 1 - cy : 1 - cy + ny, :]
            value = jnp.where(lane == 127, side, pltpu.roll(value, 127, 1))
        found.append(value)
    return found


def flow_kernel(ny, post, edge, force, own, up, down, velocity):
    nx = own.shape[0]
    velocity[...] = jnp.zeros(velocity.shape, F32)

    def plane(x, carry):
        n = arriving(post, edge, x, ny)
        rho = n[0]
        for i in range(1, 19):
            rho = rho + n[i]
        for a in range(3):
            m = 0.5 * force[x + 1, 16 * a + 1 : 16 * a + 1 + ny, :]
            for i in range(1, 19):
                if DIRS[i][a] == 1:
                    m = m + n[i]
                elif DIRS[i][a] == -1:
                    m = m - n[i]
            velocity[x, 16 * a + 1 : 16 * a + 1 + ny, :] = m / rho
        return carry

    lax.fori_loop(0, nx, plane, 0)
    for x in range(nx):
        own[x] = pltpu.roll(velocity[x], 12 * (x + REACH) % 128, 1)
        if x >= nx - REACH:
            up[x - nx + REACH] = pltpu.roll(velocity[x], 12 * (x + REACH - nx) % 128, 1)
        if x < REACH - 1:
            down[x] = pltpu.roll(velocity[x], 12 * (x + REACH + nx) % 128, 1)


def renew_kernel(post, edge, after, pops):
    def plane(x, carry):
        pops[x] = jnp.transpose(jnp.stack(arriving(post, edge, x, pops.shape[1])), (1, 0, 2))
        return carry

    lax.fori_loop(0, pops.shape[0], plane, 0)


def shifted(x, axis, distance):
    count = lax.axis_size(axis)
    return lax.ppermute(x, axis, [(i, (i + distance) % count) for i in range(count)])


def on_device(populations, membrane, anchors, targets):
    extent = populations.shape[1:]
    capacity, _, vertices = membrane.shape
    slabs, crosses, subs = (lax.axis_size(a) for a in ("slab", "cross", "sub"))
    assert subs == 2 and extent == (12, 12, 128) and capacity % 8 == 0
    width = WIDTH
    assert vertices + 4 <= width < vertices + 128
    place = [lax.axis_index(a) for a in ("slab", "cross", "sub")]
    table = chain_table(vertices, width)

    notes = jnp.concatenate([targets[:, None], anchors], axis=1)
    raw = jnp.concatenate(
        [
            jnp.transpose(membrane, (1, 0, 2)),
            jnp.broadcast_to(notes.astype(F32)[None], (3, capacity, 4)),
            jnp.full((3, capacity, width - vertices - 4), FAR, F32),
        ],
        axis=2,
    )
    if crosses == 2:
        beside = [(1, (extent[1], -extent[1]))]
    else:
        beside = [(1, (-extent[1],)), (-1, (extent[1],))]
    owners = [(place[0] * crosses + (place[1] + crosses - d) % crosses) * subs + place[2] for d in [0] + [d for d, _ in beside]]
    here = jnp.stack(place + owners).astype(jnp.int32)
    guests = [shifted(raw, "cross", d) for d, _ in beside]
    groups = 1 + len(beside)
    nx, ny = extent[:2]
    planes = nx + 2
    pops = jnp.transpose(populations, (1, 2, 0, 3))
    sides = jnp.concatenate([pops[nx - 1 :], pops[:1]])
    held = 3 * (width // 128) * MIG
    message = jax.ShapeDtypeStruct((groups * held + 24 * ny + 8, 128), F32)
    theirs = [g[0, :, vertices : vertices + 4].astype(jnp.int32) for g in guests]
    up, down = pl.pallas_call(
        functools.partial(pack_kernel, capacity, slabs, crosses * subs, groups, 0),
        out_shape=(message, message),
        in_specs=[SMEM, SMEM, VMEM, VMEM],
        out_specs=(VMEM, VMEM),
        compiler_params=params(),
        name="pack",
    )(here, notes, raw, sides)
    up, down = pl.pallas_call(
        functools.partial(pack_kernel, capacity, slabs, crosses * subs, groups, 1),
        out_shape=(message, message),
        in_specs=[SMEM, SMEM] + [VMEM] * (groups + 1),
        out_specs=(VMEM, VMEM),
        compiler_params=params(),
        name="pack",
    )(here, jnp.concatenate(theirs), *guests, up, down)
    home = jnp.concatenate([raw[0, :, vertices : vertices + 4].astype(jnp.int32)] + theirs)
    sizes = (capacity, vertices, extent)
    below, above = shifted(up, "slab", 1), shifted(down, "slab", -1)
    images = [(0,)] + [image for _, image in beside]

    row = jax.ShapeDtypeStruct((nx,) + pops.shape[2:], F32)
    sum_1, first, last = stage(
        sizes,
        [(g, 3 + g, images[g], 0) for g in range(groups)],
        here,
        home,
        table,
        [raw] + guests,
        givers=(pops,),
        takers=(row, row),
        copies=((0, (pl.ds(0, nx), 0), 0, pl.ds(0, nx)), (0, (pl.ds(0, nx), ny - 1), 1, pl.ds(0, nx))),
        together=4,
    )
    x_low = below[groups * held : groups * held + 24 * ny].reshape(1, ny, 24, 128)
    x_high = above[groups * held : groups * held + 24 * ny].reshape(1, ny, 24, 128)
    first = jnp.concatenate([x_low[:, 0, :19], first, x_high[:, 0, :19]])
    last = jnp.concatenate([x_low[:, -1, :19], last, x_high[:, -1, :19]])
    y_low, y_high = (shifted(last, "cross", 1)[None], 0), (shifted(first, "cross", -1)[None], 0)
    lane = vertices - (width - 128)
    starts = [g * held + (width // 128 - 1) * MIG for g in range(groups)]
    notes_in = [m[s : s + MIG, lane : lane + 4].astype(jnp.int32) for s in starts for m in (below, above)]
    came = jnp.concatenate(notes_in)
    own, down_force, up_force, far = stage(
        sizes,
        [(n, None, images[g], g * held) for g in range(groups) for n in (0, 1)],
        here,
        came,
        table,
        [below, above],
        sums=(sum_1,),
        last=True,
    )
    cells = []
    for block in [raw] + guests:
        cells += [block, below, above]
    offsets = tuple(g * held for g in range(groups) for _ in range(3))
    extended = pl.pallas_call(
        functools.partial(extend_kernel, y_low[1], y_high[1]),
        out_shape=jax.ShapeDtypeStruct((19, planes, 16, 128), F32),
        in_specs=[VMEM] * 5,
        out_specs=VMEM,
        compiler_params=params(),
        name="extend",
    )(pops, x_low, x_high, y_low[0], y_high[0])

    own, down_force, up_force = pl.pallas_call(
        fold_kernel,
        out_shape=tuple(jax.ShapeDtypeStruct((n, 48, 128), F32) for n in (planes, REACH + 1, REACH)),
        in_specs=[VMEM] * 4,
        out_specs=(VMEM,) * 3,
        compiler_params=params(),
        name="fold",
    )(own, down_force, up_force, shifted(far, "sub", 1))
    from_high = shifted(down_force, "slab", -1)
    from_low = shifted(up_force, "slab", 1)

    placed = pl.pallas_call(
        functools.partial(assemble_kernel, sizes, groups, offsets),
        out_shape=(jax.ShapeDtypeStruct((3, capacity + 8, width), F32),) * groups
        + (jax.ShapeDtypeStruct((capacity + 8, 3), jnp.int32),) * groups,
        in_specs=[SMEM] * 3 + [VMEM] * len(cells) + [pl.BlockSpec(memory_space=pl.ANY)],
        out_specs=(VMEM,) * groups + (SMEM,) * groups,
        compiler_params=params(),
        name="assemble",
    )(here, home, came, *cells, own)
    positions, corners = placed[:groups], placed[groups:]
    post, force, edge = pl.pallas_call(
        collide_kernel,
        out_shape=(
            jax.ShapeDtypeStruct((19, planes, 16, 128), F32),
            jax.ShapeDtypeStruct((planes, 48, 128), F32),
            jax.ShapeDtypeStruct((5, planes, 16, 128), F32),
        ),
        in_specs=[VMEM] * 4 + [pl.BlockSpec(memory_space=pl.ANY)] * groups,
        out_specs=(VMEM,) * 3,
        compiler_params=params(),
        name="collide",
    )(extended, own, from_low, from_high, *positions)
    edge = shifted(edge, "sub", 1)
    velocity, up_flow, down_flow = pl.pallas_call(
        functools.partial(flow_kernel, ny),
        out_shape=tuple(jax.ShapeDtypeStruct((n, 48, 128), F32) for n in (nx, REACH, REACH - 1)),
        in_specs=[VMEM] * 3,
        out_specs=(VMEM,) * 3,
        scratch_shapes=[pltpu.VMEM((nx, 48, 128), F32)],
        compiler_params=params(),
        name="flow",
    )(post, edge, force)
    renewed = pl.pallas_call(
        renew_kernel,
        out_shape=jax.ShapeDtypeStruct((nx, ny, 19, 128), F32),
        in_specs=[VMEM] * 2 + [pl.BlockSpec(memory_space=pl.ANY)],
        out_specs=VMEM,
        compiler_params=params(),
        name="renew",
    )(post, edge, velocity)

    low_side = shifted(up_flow, "slab", 1)
    high_side = shifted(down_flow, "slab", -1)
    low_side, high_side, renewed = lax.optimization_barrier((low_side, high_side, renewed))
    parts = (low_side, velocity, high_side)
    parts = parts + tuple(shifted(part, "sub", 1) for part in parts)
    shares = [
        shifted(sampled(capacity, image, corner, pos, parts), "cross", -d)
        for (d, image), corner, pos in zip(beside, corners[1:], positions[1:])
    ]
    total = sampled(capacity, (0,), corners[0], positions[0], parts)
    for share in shares:
        total = total + share
    return (
        jnp.transpose(renewed, (2, 0, 1, 3)),
        jnp.transpose(total[:, :, :vertices], (1, 0, 2)),
    )


def solution(mesh):
    placed = (
        P(None, ("parts", "slab"), "cross", "sub"),
        P(("parts", "slab", "cross", "sub"), None, None),
        P(("parts", "slab", "cross", "sub"), None),
        P(("parts", "slab", "cross", "sub")),
    )
    return jax.shard_map(
        on_device,
        mesh=mesh,
        in_specs=placed,
        out_specs=(
            P(None, ("parts", "slab"), "cross", "sub"),
            P(("parts", "slab", "cross", "sub"), None, None),
        ),
        check_vma=False,
    )
```

```python
import functools
import math

import jax
import jax.numpy as jnp
import numpy as np
from jax import lax
from jax.experimental import pallas as pl
from jax.experimental.pallas import tpu as pltpu
from jax.sharding import PartitionSpec as P

REACH = 6
MIG = 4
STRIDES = (21, 34, 55)
DIRS = (
    (0, 0, 0),
    (1, 0, 0), (-1, 0, 0), (0, 1, 0), (0, -1, 0), (0, 0, 1), (0, 0, -1),
    (1, 1, 0), (-1, -1, 0), (1, -1, 0), (-1, 1, 0),
    (1, 0, 1), (-1, 0, -1), (1, 0, -1), (-1, 0, 1),
    (0, 1, 1), (0, -1, -1), (0, 1, -1), (0, -1, 1),
)
RISING = (5, 11, 14, 15, 18)
FALLING = (6, 12, 13, 16, 17)
WEIGHTS = (1.0 / 3.0,) + (1.0 / 18.0,) * 6 + (1.0 / 36.0,) * 12
FAR = 100.0
F32 = jnp.float32
WIDTH = 768
VMEM = pl.BlockSpec(memory_space=pltpu.VMEM)
SMEM = pl.BlockSpec(memory_space=pltpu.SMEM)


def params(limit=14):
    return pltpu.CompilerParams(vmem_limit_bytes=limit * 1024 * 1024)


def chain_table(vertices, width):
    v = np.arange(vertices)
    h = 1.0 - (2.0 * v + 1.0) / vertices
    t = 2.0 * math.pi / 2584.0 * (v * 1597 % 2584)
    across = np.sqrt(1.0 - h * h)
    rest = 3.0 * np.stack([across * np.cos(t), across * np.sin(t), h])
    table = np.zeros((16, width))
    for n, s in enumerate(STRIDES):
        gap = rest[:, s:] - rest[:, :-s]
        table[5 * n : 5 * n + 3, : vertices - s] = gap
        table[5 * n + 3, : vertices - s] = 0.05 / np.sum(gap * gap, axis=0)
        table[5 * n + 4, : vertices - s] = 1.0
    return jnp.asarray(table, F32)


def pack_kernel(capacity, slabs, plane, groups, begun, here, infos, *refs):
    tiles = WIDTH // 128
    held = 3 * tiles * MIG
    over = lax.rem(here[0] + 1, slabs)
    under = lax.rem(here[0] + slabs - 1, slabs)
    if begun:
        cells, (up_begun, down_begun, up, down) = refs[: groups - 1], refs[groups - 1 :]
        up[...] = up_begun[...]
        down[...] = down_begun[...]
    else:
        cells, (sides, up, down) = refs[:1], refs[1:]
        up[0 : groups * held, :] = jnp.full((groups * held, 128), -1.0, F32)
        down[0 : groups * held, :] = jnp.full((groups * held, 128), -1.0, F32)
        ny, directions = sides.shape[1:3]
        for n, message in enumerate((up, down)):
            for y in range(ny):
                first = groups * held + 24 * y
                message[first : first + directions, :] = sides[n, y]
    for n, block in enumerate(cells):
        g = n + begun
        n_up, n_down = jnp.int32(0), jnp.int32(0)
        for c in range(capacity):
            owner = infos[n * capacity + c, 0] // capacity
            peer = owner // plane
            leaving = owner != here[3 + g]
            rises = jnp.logical_and(leaving, peer == over)
            falls = jnp.logical_and(leaving, peer == under)
            to_up = g * held + jnp.minimum(n_up, MIG - 1)
            to_down = g * held + jnp.minimum(n_down, MIG - 1)

            def put(message, start):
                for a in range(3):
                    for t in range(tiles):
                        row = block[a, c : c + 1, 128 * t : 128 * t + 128]
                        message[pl.ds(start + (a * tiles + t) * MIG, 1), :] = row

            @pl.when(rises)
            def _():
                put(up, to_up)

            @pl.when(falls)
            def _():
                put(down, to_down)

            n_up = n_up + rises.astype(jnp.int32)
            n_down = n_down + falls.astype(jnp.int32)


def cell_row(block, offset, r, a):
    if len(block.shape) == 3:
        return block[a, r : r + 1, :]
    tiles = WIDTH // 128
    first = offset + a * tiles * MIG + r
    return jnp.concatenate([block[first + t * MIG : first + t * MIG + 1, :] for t in range(tiles)], axis=1)


def cell_count(block):
    return block.shape[1] if len(block.shape) == 3 else MIG


def hide_rest(pos, vertices):
    width = pos.shape[2]
    lane = lax.broadcasted_iota(jnp.int32, (pos.shape[1], 128), 1) + (width - 128)
    for a in range(3):
        pos[a, :, width - 128 :] = jnp.where(lane < vertices, pos[a, :, width - 128 :], FAR)


def assemble(capacity, vertices, extent, owner, sources, pos, corner):
    for infos, first, block, offset, migrated in sources:
        for r in range(cell_count(block)):
            target = infos[first + r, 0]
            wanted = target >= 0 if migrated else target // capacity == owner
            slot = jnp.where(wanted, lax.rem(target, capacity), capacity)
            for a in range(3):
                pos[a, pl.ds(slot, 1), :] = cell_row(block, offset, r, a)
            for d in range(3):
                corner[slot, d] = lax.rem(infos[first + r, 1 + d], extent[d])
    hide_rest(pos, vertices)


def assemble_kernel(sizes, groups, offsets, *refs):
    capacity, vertices, extent = sizes
    here, home, came = refs[:3]
    refs = refs[1:]
    cells = refs[2 : 2 + 3 * groups]
    positions, corners = refs[3 + 3 * groups : 3 + 4 * groups], refs[3 + 4 * groups :]
    for g in range(groups):
        start = g * 2 * MIG
        sources = [
            (home, g * capacity, cells[3 * g], 0, False),
            (came, start, cells[3 * g + 1], offsets[3 * g + 1], True),
            (came, start + MIG, cells[3 * g + 2], offsets[3 * g + 2], True),
        ]
        assemble(capacity, vertices, extent, here[3 + g], sources, positions[g], corners[g])


def wide(tile, width):
    return jnp.concatenate([tile] * (width // 128), axis=1)


def waves(x):
    h = (x - 4.0 * jnp.floor(0.25 * x + 0.5)) * (math.pi / 4.0)
    q = h * h
    sine = h * (1.0 + q * (-1 / 6 + q * (1 / 120 + q * (-1 / 5040 + q * (1 / 362880 - q * (1 / 39916800))))))
    cosine = 1.0 + q * (
        -1 / 2 + q * (1 / 24 + q * (-1 / 720 + q * (1 / 40320 + q * (-1 / 3628800 + q * (1 / 479001600)))))
    )
    return 0.25 - 0.5 * sine * sine, 0.5 * sine * cosine


def fill_waves(pos, wave):
    cells = wave.shape[1]
    for a in range(3):
        wave[2 * a], wave[2 * a + 1] = waves(pos[a, 0:cells, :])


def fill_force(pos, table, wave, force, count):
    cells, width = force.shape[1:]

    def some(h):
        rows = slice(8 * h, 8 * h + 8)
        for a in range(3):
            wave[2 * a, rows, :], wave[2 * a + 1, rows, :] = waves(pos[a, rows, :])
        x = [pos[a, rows, :] for a in range(3)]
        lap = [jnp.zeros((8, width), F32) for _ in range(3)]
        pulls = []
        for n, s in enumerate(STRIDES):
            gap = [table[5 * n + a : 5 * n + a + 1, :] for a in range(3)]
            scale = table[5 * n + 3 : 5 * n + 4, :]
            mask = table[5 * n + 4 : 5 * n + 5, :]
            d = [pltpu.roll(x[a], width - s, 1) - x[a] for a in range(3)]
            square = d[0] * d[0] + d[1] * d[1] + d[2] * d[2]
            strain = square * scale - 0.05 * mask
            pulls.append([strain * d[a] for a in range(3)])
            for a in range(3):
                bend = mask * d[a] - gap[a]
                lap[a] = lap[a] + bend - pltpu.roll(bend, s, 1)
        for a in range(3):
            total = jnp.zeros((8, width), F32)
            for n, s in enumerate(STRIDES):
                mask = table[5 * n + 4 : 5 * n + 5, :]
                t = pulls[n][a] - 0.002 * (mask * (pltpu.roll(lap[a], width - s, 1) - lap[a]))
                total = total + t - pltpu.roll(t, s, 1)
            force[a, rows, :] = total

    for h in range(cells // 8):
        pl.when(8 * h < count)(functools.partial(some, h))


def split(x):
    high = x.astype(jnp.bfloat16)
    return high, (x - high.astype(F32)).astype(jnp.bfloat16)


def row_of(ref, i, c):
    return jnp.broadcast_to(ref[i, pl.ds(c, 1), :], (8, ref.shape[2]))


def fill_planar(pos, wave, c, high, low):
    width = pos.shape[2]
    row = lax.broadcasted_iota(jnp.int32, (8, 128), 0)
    rowf = (row - REACH).astype(F32)
    joint = wide(jnp.where(row < 4, rowf + 8.0, rowf - 4.0), width)
    rowf = wide(rowf, width)
    upper = wide(row, width) < 4
    odd = wide((row & 1), width) == 1
    flip = wide((row & 2), width) == 0
    z, cz, sz = row_of(pos, 2, c), row_of(wave, 4, c), row_of(wave, 5, c)
    base = jnp.where(odd, sz, cz)
    pattern = 0.25 + jnp.where(flip, -base, base)
    wz = [
        jnp.where(jnp.abs(rows - z) < 2.0, pattern, 0.0) for rows in (rowf, joint, rowf + 4.0)
    ]
    x, cx, sx = row_of(pos, 0, c), row_of(wave, 0, c), row_of(wave, 1, c)
    quarter = (0.25 - cx, 0.25 - sx, 0.25 + cx, 0.25 + sx)
    for four in range(3):
        tiles = []
        for kx in (4 * four, 4 * four + 2):
            wx = [
                jnp.where(jnp.abs(x - float(k - REACH)) < 2.0, quarter[k % 4], 0.0) for k in (kx, kx + 1)
            ]
            tiles += [wx[0] * wz[0], jnp.where(upper, wx[0], wx[1]) * wz[1], wx[1] * wz[2]]
        rows = slice(48 * four, 48 * four + 48)
        high[rows, :], low[rows, :] = split(jnp.concatenate(tiles, axis=0))


def rows_weight(pos, wave, c, anchor, images):
    width = pos.shape[2]
    n = lax.broadcasted_iota(jnp.int32, (8, 128), 0) - 1 - anchor
    nf = wide(n.astype(F32), width)
    odd = wide(n & 1, width) == 1
    flip = wide(n & 2, width) == 2
    y, cy, sy = row_of(pos, 1, c), row_of(wave, 2, c), row_of(wave, 3, c)
    base = jnp.where(odd, sy, cy)
    pattern = 0.25 + jnp.where(flip, -base, base)
    halves = []
    for h in range(2):
        gap = nf + 8.0 * h - y
        near = jnp.abs(gap - images[0]) < 2.0
        if len(images) > 1:
            near = jnp.logical_or(near, jnp.abs(gap - images[1]) < 2.0)
        halves.append(jnp.where(near, pattern, 0.0))
    return jnp.concatenate(halves, axis=0)


def nt_dot(a, b):
    return lax.dot_general(a, b, (((1,), (1,)), ((), ())), preferred_element_type=F32)


def stage_kernel(sizes, plan, last, copies, counts, together, *refs):
    _, vertices, extent = sizes
    n_cells, n_sums, n_copied = counts
    here, infos, table = refs[:3]
    refs = refs[3:]
    cells, refs = refs[:n_cells], refs[n_cells:]
    sums, refs = refs[:n_sums], refs[n_sums:]
    n_from = len({c[0] for c in copies})
    givers, refs = refs[:n_from], refs[n_from:]
    if last:
        own, down, up, far = refs[:4]
        refs = refs[4:]
    else:
        acc, refs = refs[0], refs[1:]
    takers, refs = refs[:n_copied], refs[n_copied:]
    pos, wave, force, planar, corner, patch = refs[:6]
    if last:
        acc = refs[6]
    moves = []
    for n, (giver, source, taker, target) in enumerate(copies):
        move = pltpu.make_async_copy(givers[giver].at[source], takers[taker].at[target], refs[-1].at[n])
        move.start()
        moves.append(move)
    if sums:
        total = sums[0][...]
        for more in sums[1:]:
            total = total + more[...]
        acc[...] = total
    else:
        acc[...] = jnp.zeros(acc.shape, F32)
    pos[...] = jnp.full(pos.shape, FAR, F32)
    rows = pos.shape[1] - 8
    for r in range(rows + 1):
        for d in range(3):
            corner[r, d] = 0
        for d in range(2):
            corner[r, 3 + d] = 0
    count = jnp.int32(0)
    at = 0
    for array, owner, images, offset in plan:
        block = cells[array]
        for r in range(cell_count(block)):
            target = infos[at, 0]
            wanted = target >= 0 if owner is None else target // sizes[0] == here[owner]
            row = jnp.where(wanted, count, rows)
            for a in range(3):
                pos[a, pl.ds(row, 1), :] = cell_row(block, offset, r, a)
            for d in range(3):
                corner[row, d] = lax.rem(infos[at, 1 + d], extent[d])
            corner[row, 3] = images[0]
            corner[row, 4] = images[-1]
            count = count + wanted.astype(jnp.int32)
            at += 1
    hide_rest(pos, vertices)
    fill_force(pos, table, wave, force, count)

    def weigh(c, b):
        fill_planar(pos, wave, c, planar.at[b, 0:144], planar.at[b, 144:288])
        images = (corner[c, 3].astype(F32), corner[c, 4].astype(F32))
        wy = rows_weight(pos, wave, c, corner[c, 1], images)
        lifted = []
        for a in range(3):
            f = row_of(force, a, c)
            lifted.append(jnp.concatenate([f, f], axis=0) * wy)
        high, low = split(jnp.concatenate(lifted, axis=0))
        both = nt_dot(planar[b], high)
        patch[b] = both[:144] + both[144:] + nt_dot(planar[b, 0:144], low)
        x0, z0 = corner[c, 0], corner[c, 2] + 2
        before = [acc[x0 + kx, pl.ds(z0, 12), :] for kx in range(12)]
        for kx in range(12):
            acc[x0 + kx, pl.ds(z0, 12), :] = before[kx] + patch[b, 12 * kx : 12 * kx + 12, :]

    def weigh_some(i, carry):
        for b in range(together):
            weigh(together * i + b, b)
        return carry

    lax.fori_loop(0, (count + together - 1) // together, weigh_some, 0)
    if last:
        for x in range(23):
            turned = jnp.transpose(acc[x, 8:136, :], (1, 0))
            if REACH - 1 <= x < REACH - 1 + own.shape[0]:
                own[x - REACH + 1] = turned
            if x < down.shape[0]:
                down[x] = turned
            if x >= 23 - up.shape[0]:
                up[x - 23 + up.shape[0]] = turned
        for n in range(3):
            outside = []
            for x in range(8 * n, 8 * n + 8):
                outside += [acc[x, 0:8, :], acc[x, 136:144, :]]
            far[n] = jnp.transpose(jnp.concatenate(outside, axis=0), (1, 0))
    for move in moves:
        move.wait()


def stage(sizes, plan, here, infos, table, cells, sums=(), last=False, givers=(), takers=(), copies=(), together=2):
    width = table.shape[1]
    rows = sum(cell_count(cells[p[0]]) for p in plan)
    counts = (len(cells), len(sums), len(takers))
    whole = pl.BlockSpec(memory_space=pl.ANY)
    fixed = pl.BlockSpec(memory_space=pltpu.HBM)
    return pl.pallas_call(
        functools.partial(stage_kernel, sizes, plan, last, copies, counts, together),
        out_shape=tuple(
            jax.ShapeDtypeStruct(shape, F32)
            for shape in ([(n, 48, 128) for n in (14, REACH + 1, REACH, 3)] if last else [(24, 152, 48)])
        )
        + tuple(takers),
        in_specs=[SMEM, SMEM, VMEM] + [VMEM] * (len(cells) + len(sums)) + [fixed] * len(givers),
        out_specs=(VMEM,) * (4 if last else 1) + (whole,) * len(takers),
        scratch_shapes=[
            pltpu.VMEM((3, rows + 8, width), F32),
            pltpu.VMEM((6, rows, width), F32),
            pltpu.VMEM((3, rows, width), F32),
            pltpu.VMEM((together, 288, width), jnp.bfloat16),
            pltpu.SMEM((rows + 8, 5), jnp.int32),
            pltpu.VMEM((together, 144, 48), F32),
        ]
        + ([pltpu.VMEM((24, 152, 48), F32)] if last else [])
        + ([pltpu.SemaphoreType.DMA((len(copies),))] if copies else []),
        compiler_params=params(),
        name="spread",
        cost_estimate=pl.CostEstimate(flops=int(4e9), bytes_accessed=4_000_000, transcendentals=0),
    )(here, infos, table, *cells, *sums, *givers)


def fold_kernel(own_in, down_in, up_in, far, own, down, up):
    lane = lax.broadcasted_iota(jnp.int32, (48, 128), 1)
    rim = jnp.logical_or(lane < 8, lane >= 120)
    for x in range(23):
        more = jnp.where(rim, pltpu.roll(far[x // 8], (120 - 16 * (x % 8)) % 128, 1), 0.0)
        if REACH - 1 <= x < REACH - 1 + own.shape[0]:
            own[x - REACH + 1] = own_in[x - REACH + 1] + more
        if x < down.shape[0]:
            down[x] = down_in[x] + more
        n = x - 23 + up.shape[0]
        if n >= 0:
            up[n] = up_in[n] + more


def sample_kernel(images, corner, pos, low_side, own, high_side, low_far, own_far, high_far, out, flow, far, wave, high, low):
    cells = out.shape[1]
    at = 0
    for part, part_far in ((low_side, low_far), (own, own_far), (high_side, high_far)):
        size = part.shape[0]
        flow[at : at + size] = part[...]
        far[at : at + size] = part_far[...]
        at += size
    fill_waves(pos, wave)
    lane = lax.broadcasted_iota(jnp.int32, (8, 128), 1)

    def sample(c, b):
        fill_planar(pos, wave, c, high.at[b], low.at[b])
        z0 = corner[c, 2] - REACH
        x0 = corner[c, 0]
        turn = (z0 + 12 * x0 + 128) & 127
        inside, chosen = [], []
        for t in range(2):
            origin = (lane - turn - 72 * t) & 127
            group = jnp.right_shift(origin * 43, 9)
            z = origin - 12 * group + z0
            inside.append(jnp.logical_and(z >= 0, z < 128))
            chosen.append([group == g for g in range(6)])
        front = lane < 72
        blocks = []
        for r in range(6):
            rows = slice(8 * r, 8 * r + 8)
            near = [flow[x0 + kx, rows, :] for kx in range(12)]
            there = [far[x0 + kx, rows, :] for kx in range(12)]
            turned = []
            for t in range(2):
                a, b_ = near[6 * t], there[6 * t]
                for g in range(1, 6):
                    a = jnp.where(chosen[t][g], near[6 * t + g], a)
                    b_ = jnp.where(chosen[t][g], there[6 * t + g], b_)
                turned.append(pltpu.roll(jnp.where(inside[t], a, b_), (128 - turn) & 127, 1))
            blocks.append(
                jnp.concatenate([jnp.where(front, turned[0], turned[1]), turned[1][:, 0:16]], axis=1)
            )
        qhigh, qlow = split(jnp.concatenate(blocks, axis=0))
        both = jnp.dot(jnp.concatenate([qhigh, qlow], axis=0), high[b], preferred_element_type=F32)
        mixed = both[:48] + both[48:] + jnp.dot(qhigh, low[b], preferred_element_type=F32)
        wy = rows_weight(pos, wave, c, corner[c, 1], images)
        for a in range(3):
            out[a, pl.ds(c, 1), :] = jnp.sum(mixed[16 * a : 16 * a + 16] * wy, axis=0, keepdims=True)

    def sample_some(i, carry):
        for b in range(8):
            sample(8 * i + b, b)
        return carry

    lax.fori_loop(0, cells // 8, sample_some, 0)


def sampled(cells, images, corner, pos, parts):
    width = pos.shape[2]
    return pl.pallas_call(
        functools.partial(sample_kernel, images),
        out_shape=jax.ShapeDtypeStruct((3, cells, width), F32),
        in_specs=[SMEM] + [VMEM] * 7,
        out_specs=VMEM,
        scratch_shapes=[
            pltpu.VMEM((24, 48, 128), F32),
            pltpu.VMEM((24, 48, 128), F32),
            pltpu.VMEM((6, cells, width), F32),
            pltpu.VMEM((8, 144, width), jnp.bfloat16),
            pltpu.VMEM((8, 144, width), jnp.bfloat16),
        ],
        compiler_params=params(),
        name="sample",
        cost_estimate=pl.CostEstimate(flops=int(2e9), bytes_accessed=4_000_000, transcendentals=0),
    )(corner, pos, *parts)


def extend_kernel(n_low, n_high, pops, x_low, x_high, y_low, y_high, out):
    nx, ny = pops.shape[:2]
    directions = pops.shape[2]
    for x in range(nx + 2):
        middle = x_low[0, :, 0:19, :] if x == 0 else (x_high[0, :, 0:19, :] if x == nx + 1 else pops[x - 1])
        block = jnp.concatenate([y_low[n_low, x : x + 1], middle, y_high[n_high, x : x + 1], y_low[n_low, x : x + 1], y_low[n_low, x : x + 1]], axis=0)
        out[:, x] = jnp.transpose(block, (1, 0, 2))


def collide_kernel(pops, own, from_low, from_high, *refs):
    post, force, edge = refs[-3:]
    planes = pops.shape[1]
    n_low, n_high = from_low.shape[0], from_high.shape[0]
    for e in range(planes):
        total = own[e]
        if e < n_low:
            total = total + from_low[e]
        if e >= planes - n_high:
            total = total + from_high[e - (planes - n_high)]
        force[e] = total
    lane = lax.broadcasted_iota(jnp.int32, (16, 128), 1)

    def plane(e, carry):
        p = [pops[i, e] for i in range(19)]
        f = [force[e, 16 * a : 16 * a + 16, :] for a in range(3)]
        rho = p[0]
        for i in range(1, 19):
            rho = rho + p[i]
        u = []
        for a in range(3):
            m = 0.5 * f[a]
            for i in range(1, 19):
                if DIRS[i][a] == 1:
                    m = m + p[i]
                elif DIRS[i][a] == -1:
                    m = m - p[i]
            u.append(m / rho)
        kinetic = u[0] * u[0] + u[1] * u[1] + u[2] * u[2]
        power = u[0] * f[0] + u[1] * f[1] + u[2] * f[2]
        level = 1.25 * rho * (1.0 - 1.5 * kinetic) - 1.125 * power
        bow, tilt = 5.625 * rho, 3.75 * rho
        new = [None] * 19
        new[0] = WEIGHTS[0] * level - 0.25 * p[0]
        for i in range(1, 19, 2):
            along = [a for a in range(3) if DIRS[i][a] != 0]
            cu, cf = None, None
            for a in along:
                tu, tf = u[a], f[a]
                if DIRS[i][a] < 0:
                    tu, tf = -tu, -tf
                cu = tu if cu is None else cu + tu
                cf = tf if cf is None else cf + tf
            even = WEIGHTS[i] * (level + cu * (bow * cu + 3.375 * cf))
            odd = WEIGHTS[i] * (tilt * cu + 1.125 * cf)
            new[i] = even + odd - 0.25 * p[i]
            new[i + 1] = even - odd - 0.25 * p[i + 1]
        for i in range(19):
            post[i, e] = new[i]
        for j in range(5):
            edge[j, e] = jnp.where(
                lane == 0, pltpu.roll(new[RISING[j]], 1, 1), pltpu.roll(new[FALLING[j]], 127, 1)
            )
        return carry

    lax.fori_loop(0, planes, plane, 0)


def arriving(post, edge, x, ny):
    lane = lax.broadcasted_iota(jnp.int32, (ny, 128), 1)
    found = []
    for i in range(19):
        cx, cy, cz = DIRS[i]
        value = post[i, x + 1 - cx, 1 - cy : 1 - cy + ny, :]
        if cz == 1:
            side = edge[RISING.index(i), x + 1 - cx, 1 - cy : 1 - cy + ny, :]
            value = jnp.where(lane == 0, side, pltpu.roll(value, 1, 1))
        elif cz == -1:
            side = edge[FALLING.index(i), x + 1 - cx, 1 - cy : 1 - cy + ny, :]
            value = jnp.where(lane == 127, side, pltpu.roll(value, 127, 1))
        found.append(value)
    return found


def flow_kernel(ny, post, edge, force, own, up, down, velocity):
    nx = own.shape[0]
    velocity[...] = jnp.zeros(velocity.shape, F32)

    def plane(x, carry):
        n = arriving(post, edge, x, ny)
        rho = n[0]
        for i in range(1, 19):
            rho = rho + n[i]
        for a in range(3):
            m = 0.5 * force[x + 1, 16 * a + 1 : 16 * a + 1 + ny, :]
            for i in range(1, 19):
                if DIRS[i][a] == 1:
                    m = m + n[i]
                elif DIRS[i][a] == -1:
                    m = m - n[i]
            velocity[x, 16 * a + 1 : 16 * a + 1 + ny, :] = m / rho
        return carry

    lax.fori_loop(0, nx, plane, 0)
    for x in range(nx):
        own[x] = pltpu.roll(velocity[x], 12 * (x + REACH) % 128, 1)
        if x >= nx - REACH:
            up[x - nx + REACH] = pltpu.roll(velocity[x], 12 * (x + REACH - nx) % 128, 1)
        if x < REACH - 1:
            down[x] = pltpu.roll(velocity[x], 12 * (x + REACH + nx) % 128, 1)


def renew_kernel(post, edge, after, pops):
    def plane(x, carry):
        pops[x] = jnp.transpose(jnp.stack(arriving(post, edge, x, pops.shape[1])), (1, 0, 2))
        return carry

    lax.fori_loop(0, pops.shape[0], plane, 0)


def shifted(x, axis, distance):
    count = lax.axis_size(axis)
    return lax.ppermute(x, axis, [(i, (i + distance) % count) for i in range(count)])


def on_device(populations, membrane, anchors, targets):
    extent = populations.shape[1:]
    capacity, _, vertices = membrane.shape
    slabs, crosses, subs = (lax.axis_size(a) for a in ("slab", "cross", "sub"))
    assert subs == 2 and extent == (12, 12, 128) and capacity % 8 == 0
    width = WIDTH
    assert vertices + 4 <= width < vertices + 128
    place = [lax.axis_index(a) for a in ("slab", "cross", "sub")]
    table = chain_table(vertices, width)

    notes = jnp.concatenate([targets[:, None], anchors], axis=1)
    raw = jnp.concatenate(
        [
            jnp.transpose(membrane, (1, 0, 2)),
            jnp.broadcast_to(notes.astype(F32)[None], (3, capacity, 4)),
            jnp.full((3, capacity, width - vertices - 4), FAR, F32),
        ],
        axis=2,
    )
    if crosses == 2:
        beside = [(1, (extent[1], -extent[1]))]
    else:
        beside = [(1, (-extent[1],)), (-1, (extent[1],))]
    owners = [(place[0] * crosses + (place[1] + crosses - d) % crosses) * subs + place[2] for d in [0] + [d for d, _ in beside]]
    here = jnp.stack(place + owners).astype(jnp.int32)
    guests = [shifted(raw, "cross", d) for d, _ in beside]
    groups = 1 + len(beside)
    nx, ny = extent[:2]
    planes = nx + 2
    pops = jnp.transpose(populations, (1, 2, 0, 3))
    sides = jnp.concatenate([pops[nx - 1 :], pops[:1]])
    held = 3 * (width // 128) * MIG
    message = jax.ShapeDtypeStruct((groups * held + 24 * ny + 8, 128), F32)
    theirs = [g[0, :, vertices : vertices + 4].astype(jnp.int32) for g in guests]
    up, down = pl.pallas_call(
        functools.partial(pack_kernel, capacity, slabs, crosses * subs, groups, 0),
        out_shape=(message, message),
        in_specs=[SMEM, SMEM, VMEM, VMEM],
        out_specs=(VMEM, VMEM),
        compiler_params=params(),
        name="pack",
    )(here, notes, raw, sides)
    up, down = pl.pallas_call(
        functools.partial(pack_kernel, capacity, slabs, crosses * subs, groups, 1),
        out_shape=(message, message),
        in_specs=[SMEM, SMEM] + [VMEM] * (groups + 1),
        out_specs=(VMEM, VMEM),
        compiler_params=params(),
        name="pack",
    )(here, jnp.concatenate(theirs), *guests, up, down)
    home = jnp.concatenate([raw[0, :, vertices : vertices + 4].astype(jnp.int32)] + theirs)
    sizes = (capacity, vertices, extent)
    below, above = shifted(up, "slab", 1), shifted(down, "slab", -1)
    images = [(0,)] + [image for _, image in beside]

    row = jax.ShapeDtypeStruct((nx,) + pops.shape[2:], F32)
    sum_1, first, last = stage(
        sizes,
        [(g, 3 + g, images[g], 0) for g in range(groups)],
        here,
        home,
        table,
        [raw] + guests,
        givers=(pops,),
        takers=(row, row),
        copies=((0, (pl.ds(0, nx), 0), 0, pl.ds(0, nx)), (0, (pl.ds(0, nx), ny - 1), 1, pl.ds(0, nx))),
        together=4,
    )
    x_low = below[groups * held : groups * held + 24 * ny].reshape(1, ny, 24, 128)
    x_high = above[groups * held : groups * held + 24 * ny].reshape(1, ny, 24, 128)
    first = jnp.concatenate([x_low[:, 0, :19], first, x_high[:, 0, :19]])
    last = jnp.concatenate([x_low[:, -1, :19], last, x_high[:, -1, :19]])
    y_low, y_high = (shifted(last, "cross", 1)[None], 0), (shifted(first, "cross", -1)[None], 0)
    lane = vertices - (width - 128)
    starts = [g * held + (width // 128 - 1) * MIG for g in range(groups)]
    notes_in = [m[s : s + MIG, lane : lane + 4].astype(jnp.int32) for s in starts for m in (below, above)]
    came = jnp.concatenate(notes_in)
    own, down_force, up_force, far = stage(
        sizes,
        [(n, None, images[g], g * held) for g in range(groups) for n in (0, 1)],
        here,
        came,
        table,
        [below, above],
        sums=(sum_1,),
        last=True,
        together=4,
    )
    cells = []
    for block in [raw] + guests:
        cells += [block, below, above]
    offsets = tuple(g * held for g in range(groups) for _ in range(3))
    extended = pl.pallas_call(
        functools.partial(extend_kernel, y_low[1], y_high[1]),
        out_shape=jax.ShapeDtypeStruct((19, planes, 16, 128), F32),
        in_specs=[VMEM] * 5,
        out_specs=VMEM,
        compiler_params=params(),
        name="extend",
    )(pops, x_low, x_high, y_low[0], y_high[0])

    own, down_force, up_force = pl.pallas_call(
        fold_kernel,
        out_shape=tuple(jax.ShapeDtypeStruct((n, 48, 128), F32) for n in (planes, REACH + 1, REACH)),
        in_specs=[VMEM] * 4,
        out_specs=(VMEM,) * 3,
        compiler_params=params(),
        name="fold",
    )(own, down_force, up_force, shifted(far, "sub", 1))
    from_high = shifted(down_force, "slab", -1)
    from_low = shifted(up_force, "slab", 1)

    placed = pl.pallas_call(
        functools.partial(assemble_kernel, sizes, groups, offsets),
        out_shape=(jax.ShapeDtypeStruct((3, capacity + 8, width), F32),) * groups
        + (jax.ShapeDtypeStruct((capacity + 8, 3), jnp.int32),) * groups,
        in_specs=[SMEM] * 3 + [VMEM] * len(cells) + [pl.BlockSpec(memory_space=pl.ANY)],
        out_specs=(VMEM,) * groups + (SMEM,) * groups,
        compiler_params=params(),
        name="assemble",
    )(here, home, came, *cells, own)
    positions, corners = placed[:groups], placed[groups:]
    post, force, edge = pl.pallas_call(
        collide_kernel,
        out_shape=(
            jax.ShapeDtypeStruct((19, planes, 16, 128), F32),
            jax.ShapeDtypeStruct((planes, 48, 128), F32),
            jax.ShapeDtypeStruct((5, planes, 16, 128), F32),
        ),
        in_specs=[VMEM] * 4 + [pl.BlockSpec(memory_space=pl.ANY)] * groups,
        out_specs=(VMEM,) * 3,
        compiler_params=params(),
        name="collide",
    )(extended, own, from_low, from_high, *positions)
    edge = shifted(edge, "sub", 1)
    velocity, up_flow, down_flow = pl.pallas_call(
        functools.partial(flow_kernel, ny),
        out_shape=tuple(jax.ShapeDtypeStruct((n, 48, 128), F32) for n in (nx, REACH, REACH - 1)),
        in_specs=[VMEM] * 3,
        out_specs=(VMEM,) * 3,
        scratch_shapes=[pltpu.VMEM((nx, 48, 128), F32)],
        compiler_params=params(),
        name="flow",
    )(post, edge, force)
    renewed = pl.pallas_call(
        renew_kernel,
        out_shape=jax.ShapeDtypeStruct((nx, ny, 19, 128), F32),
        in_specs=[VMEM] * 2 + [pl.BlockSpec(memory_space=pl.ANY)],
        out_specs=VMEM,
        compiler_params=params(),
        name="renew",
    )(post, edge, velocity)

    low_side = shifted(up_flow, "slab", 1)
    high_side = shifted(down_flow, "slab", -1)
    low_side, high_side, renewed = lax.optimization_barrier((low_side, high_side, renewed))
    parts = (low_side, velocity, high_side)
    parts = parts + tuple(shifted(part, "sub", 1) for part in parts)
    shares = [
        shifted(sampled(capacity, image, corner, pos, parts), "cross", -d)
        for (d, image), corner, pos in zip(beside, corners[1:], positions[1:])
    ]
    total = sampled(capacity, (0,), corners[0], positions[0], parts)
    for share in shares:
        total = total + share
    return (
        jnp.transpose(renewed, (2, 0, 1, 3)),
        jnp.transpose(total[:, :, :vertices], (1, 0, 2)),
    )


def solution(mesh):
    placed = (
        P(None, ("parts", "slab"), "cross", "sub"),
        P(("parts", "slab", "cross", "sub"), None, None),
        P(("parts", "slab", "cross", "sub"), None),
        P(("parts", "slab", "cross", "sub")),
    )
    return jax.shard_map(
        on_device,
        mesh=mesh,
        in_specs=placed,
        out_specs=(
            P(None, ("parts", "slab"), "cross", "sub"),
            P(("parts", "slab", "cross", "sub"), None, None),
        ),
        check_vma=False,
    )
```
